32 devices in a mesh: groups: 2 (over y), geo: 16 (over z, x, core).
Axes of the slice: x: 2, y: 2, z: 4, core: 2. Of those that a mesh axis runs over, the one named last changes fastest.
Arguments:
- initial_spectrum: float32 [1296, 16384], P(None, ('groups', 'geo')), parts along dimension 1, may hold values from 0.05 to 1
- wind_forcing: float32 [2, 16384], P(None, ('groups', 'geo')), parts along dimension 1, may hold values from 0.2 to 1.5
- sea_mask: int32 [16384], P(('groups', 'geo')), parts along dimension 0, may hold values 0 or 1
- courant: float32 [36], replicated, may hold values from 0.2 to 0.7
- input_rate: float32 [1296], replicated, may hold values from 0.02 to 0.2
- damping: float32 [1296], replicated, may hold values from 0.2 to 1
- steep_weight: float32 [1296], replicated, may hold values from 0.0002 to 0.002
- obs_owner: int32 [4096, 1], P(('groups', 'geo')), parts along dimension 0, may hold values from 0 to 15; in each aligned block of 128 rows (0 to 127, 128 to 255, ...) at most 16 rows name the same one
- obs_point: int32 [4096], P(('groups', 'geo')), parts along dimension 0, may hold values from 0 to 511
- obs_value: float32 [4096, 36], P(('groups', 'geo')), parts along dimension 0, may hold values from -4 to 4
- obs_weight: float32 [4096], P(('groups', 'geo')), parts along dimension 0, may hold values from 4 to 40
Outputs:
- grad_wind: float32 [2, 16384], P(None, ('groups', 'geo')), parts along dimension 1
- grad_initial: float32 [1296, 16384], P(None, ('groups', 'geo')), parts along dimension 1
The draws below stay inside these ranges and needn't reach their ends.
There are 2 independent parts, one for each index of `groups`. The reference program is written for one: setup_inputs(seed, part) draws one part's arguments, and reference() takes and returns one part's arrays. A program takes and returns all parts, laid end to end along the dimension named above; an argument that names none is the same for every part. Nothing has to cross between parts.
Inputs may be any that keep to these rules, and one draw needn't show every extreme that they name: `obs_owner`: among the 128 rows of one device, at most 16 name the same owner, a bound that some block reaches of them.
All inputs are finite; a program needn't handle non-finite values. No bound on the sum of `sea_mask` on one device may be relied on, other than what follows from the above.
Results may differ from the reference program's by a relative error of at most 0.0001.
Values sent between devices are 32-bit elements; how exact they have to be, the bound alone decides.
No kernel may reach another device: no remote copies, remote signals or barrier semaphores. Data moves between devices by JAX's collectives and lax.ppermute only.
A program may use at most 64 MiB of HBM per device.

```python
import math
import jax
import jax.numpy as jnp
import numpy as np

ND = 36
NF = 36
NB = 1296
W = 128
P_DEV = 512
O_DEV = 128
CYCLES = 2
CAP = 16
POINTS = 8192
OBS = 2048
N_GEO = 16


def set_ends(array, rng, low, high):
    longest = array.shape.index(max(array.shape))
    spots = []
    for shift in (0, 1):
        where = [jax.random.randint(jax.random.fold_in(rng, axis), (), 0, length) for axis, length in enumerate(array.shape)]
        where[longest] = (where[longest] + shift) % array.shape[longest]
        spots.append(tuple(where))
    return array.at[spots[0]].set(low).at[spots[1]].set(high)


def block_scale(stream_key, dims, cuts, low, largest):
    factor_of = 1.0
    for position, parts in cuts:
        steps = jax.random.uniform(jax.random.fold_in(jax.random.fold_in(stream_key, 6), position), (parts,), jnp.float32, low / len(cuts), largest / len(cuts))
        factor_of = factor_of * jnp.repeat(jnp.exp(steps), dims[position] // parts).reshape((-1,) + (1,) * (len(dims) - 1 - position))
    return factor_of


def shared_out(key, own, number, rows, amount, top, limit, skew):
    sequence = jax.random.permutation(key, amount)
    packed, common = portions_of(amount, rows * top, limit, skew, True), portions_of(amount, rows * top, limit, skew, False)
    places = jnp.arange(amount)

    def named(lengths, offset_by):
        used = int((lengths > 0).sum())
        fixed = max(1, used // 4)
        moved = fixed + (places - fixed + offset_by * (used - fixed)) % max(1, amount - fixed)
        return jnp.zeros((amount,), jnp.int32).at[sequence[jnp.where(places < fixed, places, moved)]].set(jnp.asarray(lengths, jnp.int32))

    lengths = jnp.where(number % 4 == 0, named(packed, number // 4), named(common, number - number // 4 - 1))
    mixed = jax.random.permutation(jax.random.fold_in(own, 3), amount)
    donor, taker = mixed[0:amount // 2 * 2:2], mixed[1:amount // 2 * 2:2]
    slack = jnp.minimum(lengths[donor] - 1, limit - lengths[taker]) // 2
    slack = jnp.where((donor == sequence[0]) | (taker == sequence[0]) | (lengths[taker] == 0), 0, jnp.maximum(slack, 0))
    moved = jax.random.randint(jax.random.fold_in(own, 4), (amount // 2,), 0, 1 << 20) % (slack + 1)
    lengths = lengths.at[donor].add(-moved).at[taker].add(moved)
    members = jnp.searchsorted(jnp.cumsum(lengths), jnp.arange(rows * top), side="right").astype(jnp.int32)
    table = members.reshape(top, rows).T
    table = table[jax.random.permutation(jax.random.fold_in(own, 1), rows)]
    offset_by = jax.random.randint(jax.random.fold_in(own, 2), (rows, 1), 0, top)
    return jnp.take_along_axis(table, (jnp.arange(top)[None, :] + offset_by) % top, axis=1)


def portions_of(amount, total, bound, slope, full):
    loads = [(1 << 20) // math.isqrt(standing ** slope) + 1 for standing in range(1, amount + 1)]
    largest = bound if full else min(bound, max(-(-total // amount), total * loads[0] // sum(loads)))
    least = 1 if total - largest >= amount - 1 else 0
    counts, surplus = [largest] + [least] * (amount - 1), total - largest - least * (amount - 1)
    while surplus > 0:
        candidates = [i for i in range(1, amount) if counts[i] < largest] or [i for i in range(1, amount) if counts[i] < bound]
        pool, left = sum([loads[i] for i in candidates]), surplus
        for i in candidates:
            more = min(bound - counts[i], max(1, left * loads[i] // pool), surplus)
            counts[i] = counts[i] + more
            surplus = surplus - more
    return np.array(counts)


def centred(stream_key, extent, deviation, limit, cuts=(), held_as=jnp.bfloat16):
    result = jax.random.normal(stream_key, extent, jnp.float32) * deviation
    if len(cuts) > 0:
        result = block_scale(stream_key, extent, cuts, -0.22, 0.18) * result
    return jnp.clip(result, min=-limit, max=limit).astype(held_as)


def setup_inputs(seed: int = 0, part: int = 0) -> dict:
    keys = jax.random.split(jax.random.key(seed), 12)
    own_keys = jax.random.split(jax.random.fold_in(keys[11], part), 12)
    initial_spectrum = jnp.clip(jnp.exp(math.log(1.0) - 2.9957323 * jax.random.uniform(own_keys[0], (NB, POINTS), jnp.float32) ** block_scale(own_keys[0], (NB, POINTS), ((1, 16),), -0.2, 0.2)), 0.05, 1.0)
    wind_forcing = jnp.clip(0.2 + 1.3 * jax.random.uniform(own_keys[1], (CYCLES, POINTS), jnp.float32) ** block_scale(own_keys[1], (CYCLES, POINTS), ((1, 16),), -0.2, 0.2), 0.2, 1.5)
    sea_mask = set_ends((jax.random.randint(own_keys[2], (POINTS,), 0, 5) < 4).astype(jnp.int32), jax.random.fold_in(own_keys[2], 1), 0, 1)
    courant = jnp.clip(jnp.exp(jax.random.uniform(keys[3], (NF,), jnp.float32, math.log(0.2), math.log(0.7))), 0.2, 0.7)
    input_rate = jnp.clip(jnp.exp(jax.random.uniform(keys[4], (NB,), jnp.float32, math.log(0.02), math.log(0.2))), 0.02, 0.2)
    damping = jnp.clip(jnp.exp(jax.random.uniform(keys[5], (NB,), jnp.float32, math.log(0.2), math.log(1.0))), 0.2, 1.0)
    steep_weight = jnp.clip(jnp.exp(jax.random.uniform(keys[6], (NB,), jnp.float32, math.log(0.0002), math.log(0.002))), 0.0002, 0.002)
    obs_owner_keys = jax.random.split(jax.random.fold_in(own_keys[7], 1), OBS // O_DEV)
    obs_owner_turns = jax.random.permutation(jax.random.fold_in(own_keys[7], 3), OBS // O_DEV)
    obs_owner = jax.vmap(lambda own, number: shared_out(jax.random.fold_in(own_keys[7], 2), own, number, O_DEV, N_GEO, 1, CAP, 2))(obs_owner_keys, obs_owner_turns).reshape((OBS, 1))
    obs_point = set_ends(jax.random.randint(own_keys[8], (OBS,), 0, P_DEV), jax.random.fold_in(own_keys[8], 1), 0, P_DEV - 1).astype(jnp.int32)
    obs_value = centred(own_keys[9], (OBS, NF), 0.5, 4.0, ((0, 16),), jnp.float32)
    obs_weight = jnp.clip(jnp.exp(math.log(40.0) - 2.3025851 * jax.random.uniform(own_keys[10], (OBS,), jnp.float32) ** block_scale(own_keys[10], (OBS,), ((0, 16),), -0.2, 0.2)), 4.0, 40.0)
    return dict(initial_spectrum=initial_spectrum, wind_forcing=wind_forcing, sea_mask=sea_mask, courant=courant, input_rate=input_rate, damping=damping, steep_weight=steep_weight, obs_owner=obs_owner, obs_point=obs_point, obs_value=obs_value, obs_weight=obs_weight)


def stencil(courant, reverse):
    angle = 2.0 * math.pi * jnp.arange(ND, dtype=jnp.float32) / ND
    cosine = jnp.cos(angle)[None, :]
    sine = jnp.sin(angle)[None, :]
    if reverse:
        cosine = -cosine
        sine = -sine
    speed = courant[:, None]
    centre = (1.0 - speed * (jnp.abs(cosine) + jnp.abs(sine))).reshape(NB, 1)
    west = (speed * jnp.maximum(cosine, 0.0)).reshape(NB, 1)
    east = (speed * jnp.maximum(-cosine, 0.0)).reshape(NB, 1)
    south = (speed * jnp.maximum(sine, 0.0)).reshape(NB, 1)
    north = (speed * jnp.maximum(-sine, 0.0)).reshape(NB, 1)
    return centre, west, east, south, north


def propagate(field, sea, coeffs):
    centre, west, east, south, north = coeffs
    count = field.shape[1]
    column = jnp.arange(count, dtype=jnp.int32) % W
    masked = field * sea[None, :]
    padded = jnp.pad(masked, ((0, 0), (W, W)))
    from_west = padded[:, W - 1:W - 1 + count] * (column > 0).astype(jnp.float32)[None, :]
    from_east = padded[:, W + 1:W + 1 + count] * (column < W - 1).astype(jnp.float32)[None, :]
    from_south = padded[:, 0:count]
    from_north = padded[:, 2 * W:2 * W + count]
    total = centre * masked + west * from_west + east * from_east + south * from_south + north * from_north
    return total * sea[None, :]


def growth(state, wind_row, input_rate, damping, steep_weight):
    steep = jnp.sum(steep_weight[:, None] * state, axis=0)
    return jnp.exp(input_rate[:, None] * wind_row[None, :] - damping[:, None] * steep[None, :])


def reference(initial_spectrum, wind_forcing, sea_mask, courant, input_rate, damping, steep_weight, obs_owner, obs_point, obs_value, obs_weight):
    sea = sea_mask.astype(jnp.float32)
    forward = stencil(courant, False)
    backward = stencil(courant, True)
    spectrum = initial_spectrum
    states = []
    for cycle in range(CYCLES):
        state = propagate(spectrum, sea, forward)
        states.append(state)
        spectrum = state * growth(state, wind_forcing[cycle], input_rate, damping, steep_weight)
    count = spectrum.shape[1]
    mean_dir = jnp.mean(spectrum.reshape(NF, ND, count), axis=1)
    located = (obs_owner[:, 0] * P_DEV + obs_point).astype(jnp.int32)
    model = mean_dir[:, located].T
    misfit = obs_weight[:, None] * (model - obs_value)
    adjoint_f = jnp.zeros((NF, count), jnp.float32).at[:, located].add(misfit.T)
    adjoint = jnp.broadcast_to((adjoint_f / ND)[:, None, :], (NF, ND, count)).reshape(NB, count)
    grads = []
    for cycle in range(CYCLES - 1, -1, -1):
        state = states[cycle]
        factor = growth(state, wind_forcing[cycle], input_rate, damping, steep_weight)
        product = adjoint * state * factor
        grads.append(jnp.sum(input_rate[:, None] * product, axis=0))
        tendency = -jnp.sum(damping[:, None] * product, axis=0)
        adjoint = propagate(adjoint * factor + steep_weight[:, None] * tendency[None, :], sea, backward)
    grad_wind = jnp.stack(grads[::-1], axis=0)
    return grad_wind, adjoint
```

```python
import math

import jax
import jax.numpy as jnp
import numpy as np
from jax import lax
from jax.experimental import pallas as pl
from jax.experimental.pallas import tpu as pltpu
from jax.sharding import PartitionSpec as P

ND = 36
NF = 36
NB = 1296
W = 128
ROWS = 4
SUB = 8
GROUP = 72
TILES = GROUP // SUB
GROUPS = NB // GROUP
F32 = jnp.float32
LIMIT = 48 * 1024 * 1024

NORTH = (0, 1, 2, 4, 5, 6)
SOUTH = (2, 3, 4, 6, 7, 8)
FROM_WEST = (0, 4, 8)
FROM_EAST = (2, 6)


def direction_tables():
    angle = np.float32(2.0 * math.pi) * np.arange(ND, dtype=np.float32) / np.float32(ND)
    cosine = np.tile(np.cos(angle), 2)[:, None]
    sine = np.tile(np.sin(angle), 2)[:, None]
    lane = np.arange(W)[None, :]
    east = cosine >= 0
    west_ok = (lane > 0).astype(np.float32)
    east_ok = (lane < W - 1).astype(np.float32)
    one = np.ones((1, W), np.float32)
    forward = np.abs(cosine) * np.where(east, west_ok, east_ok)
    backward = np.abs(cosine) * np.where(east, east_ok, west_ok)
    return np.stack(
        [
            (np.abs(cosine) + np.abs(sine)) * one,
            np.abs(sine) * one,
            forward,
            backward,
            np.abs(cosine) * one,
        ]
    ).astype(np.float32)


def sublane():
    return lax.broadcasted_iota(jnp.int32, (SUB, W), 0)


def north_mask(tile, sub):
    return {2: sub < 2, 4: sub >= 4, 6: sub < 6}.get(tile)


def west_mask(tile, sub):
    return {1: sub < 1, 3: sub >= 3, 5: sub < 5, 7: sub >= 7}.get(tile)


def side(tile, sub, value, reverse):
    from_west = pltpu.roll(value, 1, 1) if tile not in (FROM_WEST if reverse else FROM_EAST) else None
    from_east = pltpu.roll(value, W - 1, 1) if tile not in (FROM_EAST if reverse else FROM_WEST) else None
    if from_east is None:
        return from_west
    if from_west is None:
        return from_east
    mask = west_mask(tile, sub)
    return jnp.where(mask, from_east, from_west) if reverse else jnp.where(mask, from_west, from_east)


def pick(tile, sub, north, south):
    mask = north_mask(tile, sub)
    if mask is None:
        return north if tile in NORTH else south
    if north is None:
        return jnp.where(mask, 0.0, south)
    if south is None:
        return jnp.where(mask, north, 0.0)
    return jnp.where(mask, north, south)


def speed(tile, sub, courant, group):
    first, second = courant[2 * group], courant[2 * group + 1]
    if tile == 4:
        return jnp.where(sub < 4, first, second)
    return jnp.full((SUB, W), first if tile < 4 else second, F32)


def weights(tile, sub, table, courant, group, reverse):
    rate = speed(tile, sub, courant, group)
    rows = pl.ds(tile * SUB, SUB)
    centre = 1.0 - rate * table[0, rows, :]
    along = rate * table[3 if reverse else 2, rows, :]
    across = rate * table[1, rows, :]
    return centre, along, across


def lanes(row):
    return pl.ds(row * W, W)


def total(value):
    return jnp.sum(value, axis=0, keepdims=True)


def whole(memory=pltpu.VMEM):
    return pl.BlockSpec(memory_space=memory)


def params():
    return pltpu.CompilerParams(vmem_limit_bytes=LIMIT)


def pack_kernel(field, north, south):
    sub = sublane()
    both = (sub < 2) | ((sub >= 4) & (sub < 6))
    for pair in range(field.shape[0] // 2):
        for row in range(2):
            def cell(half, tile, base):
                return field[2 * pair + half, pl.ds(tile * SUB, SUB), lanes(base + row)]

            def put(ref, tile, value):
                ref[pair, pl.ds(tile * SUB, SUB), lanes(row)] = value

            rest = []
            for half in range(2):
                sixth = cell(half, 6, 2)
                for place, tile in enumerate((0, 1, 5)):
                    put(north, half * 4 + place, cell(half, tile, 2))
                mixed = jnp.where(sub < 2, cell(half, 2, 2), jnp.where(sub < 4, sixth, cell(half, 4, 2)))
                put(north, half * 4 + 3, mixed)
                rest.append(sixth)
            put(north, 8, jnp.where(both, rest[0], pltpu.roll(rest[1], 2, 0)))
            rest = []
            for half in range(2):
                second = cell(half, 2, 0)
                for place, tile in enumerate((3, 7, 8)):
                    put(south, half * 4 + place, cell(half, tile, 0))
                put(south, half * 4 + 3, jnp.where(sub < 4, cell(half, 4, 0), second))
                rest.append(jnp.where(sub < 4, second, cell(half, 6, 0)))
            put(south, 8, jnp.where(both, pltpu.roll(rest[1], 2, 0), rest[0]))


def pack(field):
    steps = 3
    each = GROUPS // steps
    half = jax.ShapeDtypeStruct((GROUPS // 2, GROUP, 2 * W), F32)
    return pl.pallas_call(
        pack_kernel,
        grid=(steps,),
        in_specs=[pl.BlockSpec((each, GROUP, ROWS * W), lambda i: (i, 0, 0))],
        out_specs=[pl.BlockSpec((each // 2, GROUP, 2 * W), lambda i: (i, 0, 0))] * 2,
        out_shape=[half, half],
        compiler_params=params(),
        name="pack",
    )(field)


def unpack_north(halo, pair, half, row, sub):
    def get(tile):
        return halo[pair, pl.ds(tile * SUB, SUB), lanes(row)]

    mixed, last = get(half * 4 + 3), get(8)
    if half:
        last = pltpu.roll(last, 6, 0)
    return {
        0: get(half * 4),
        1: get(half * 4 + 1),
        2: mixed,
        4: mixed,
        5: get(half * 4 + 2),
        6: jnp.where((sub >= 2) & (sub < 4), mixed, last),
    }


def unpack_south(halo, pair, half, row, sub):
    def get(tile):
        return halo[pair, pl.ds(tile * SUB, SUB), lanes(row)]

    mixed, last = get(half * 4 + 3), get(8)
    if half:
        last = pltpu.roll(last, 6, 0)
    return {
        2: jnp.where(sub < 4, last, mixed),
        3: get(half * 4),
        4: mixed,
        6: last,
        7: get(half * 4 + 1),
        8: get(half * 4 + 2),
    }


def spread(row_ref, out):
    for start in range(0, NB, W):
        size = min(W, NB - start)
        chunk = row_ref[:, pl.ds(start, size)]
        square = jnp.broadcast_to(chunk, (W, size)) if size == W else jnp.broadcast_to(chunk, (W, size))
        out[pl.ds(start, size), :] = jnp.transpose(square)


def local_kernel(field, sea_in, wind, courant, rate_in, damp_in, steep_in, table, masked, rate, damp, steep, own, send_a, send_b):
    sub = sublane()
    spread(rate_in, rate)
    spread(damp_in, damp)
    spread(steep_in, steep)
    sea = [jnp.broadcast_to(sea_in[:, lanes(r)].astype(F32), (SUB, W)) for r in range(ROWS)]
    zero = jnp.zeros((SUB, W), F32)

    def step(group, sums):
        sums = list(sums)
        for tile in range(TILES):
            rows = pl.ds(tile * SUB, SUB)
            speeds = speed(tile, sub, courant, group)
            heavy = steep[pl.ds(pl.multiple_of(group * GROUP + tile * SUB, SUB), SUB), :]
            centre = heavy * (1.0 - speeds * table[0, rows, :])
            along = heavy * speeds * table[4, rows, :]
            across = heavy * speeds * table[1, rows, :]
            east = west_mask(tile, sub)
            if east is None:
                west_part, east_part = (along, None) if tile in FROM_WEST else (None, along)
            else:
                west_part, east_part = jnp.where(east, along, 0.0), jnp.where(east, 0.0, along)
            mask = north_mask(tile, sub)
            if mask is None:
                north_part, south_part = (across, None) if tile in NORTH else (None, across)
            else:
                north_part, south_part = jnp.where(mask, across, 0.0), jnp.where(mask, 0.0, across)
            for r in range(ROWS):
                cell = field[group, rows, lanes(r)] * sea[r]
                masked[group, rows, lanes(r)] = cell
                for place, part in enumerate((centre, west_part, east_part, north_part, south_part)):
                    if part is not None:
                        sums[place * ROWS + r] = sums[place * ROWS + r] + part * cell
        return tuple(sums)

    sums = lax.fori_loop(0, GROUPS, step, (zero,) * (5 * ROWS))
    sums = [total(value) for value in sums]
    lane = lax.broadcasted_iota(jnp.int32, (1, W), 1)
    local = []
    for r in range(ROWS):
        value = sums[r]
        value = value + jnp.where(lane > 0, pltpu.roll(sums[ROWS + r], 1, 1), 0.0)
        value = value + jnp.where(lane < W - 1, pltpu.roll(sums[2 * ROWS + r], W - 1, 1), 0.0)
        if r > 0:
            value = value + sums[3 * ROWS + r - 1]
        if r < ROWS - 1:
            value = value + sums[4 * ROWS + r + 1]
        local.append(value * sea[r][0:1, :])
    own[...] = jnp.zeros_like(own)
    for r in range(ROWS):
        own[0:1, lanes(r)] = local[r]
        own[1:2, lanes(r)] = sums[3 * ROWS + r]
        own[2:3, lanes(r)] = sums[4 * ROWS + r]

    def fill(ref, base, passing):
        ref[...] = jnp.zeros_like(ref)
        ref[0:2, :] = wind[:, pl.ds(base * W, 2 * W)]
        ref[2:3, :] = sea_in[:, pl.ds(base * W, 2 * W)].astype(F32)
        ref[3:4, :] = own[0:1, pl.ds(base * W, 2 * W)]
        ref[4:5, :] = own[passing : passing + 1, pl.ds(base * W, 2 * W)]

    even = lax.rem(lax.axis_index("geo"), 2) == 0

    @pl.when(even)
    def _():
        fill(send_a, 2, 1)
        fill(send_b, 0, 2)

    @pl.when(jnp.logical_not(even))
    def _():
        fill(send_a, 0, 2)
        fill(send_b, 2, 1)


def local(field, sea, wind, courant, rate, damp, steep, table):
    cells = (GROUPS, GROUP, ROWS * W)
    small = jax.ShapeDtypeStruct((SUB, 2 * W), F32)
    return pl.pallas_call(
        local_kernel,
        in_specs=[whole(), whole(), whole(), whole(pltpu.SMEM), whole(), whole(), whole(), whole()],
        out_specs=[whole()] * 7,
        out_shape=[
            pltpu.VMEM(cells, F32),
            pltpu.VMEM((NB, W), F32),
            pltpu.VMEM((NB, W), F32),
            pltpu.VMEM((NB, W), F32),
            pltpu.VMEM((SUB, ROWS * W), F32),
            small,
            small,
        ],
        compiler_params=params(),
        name="local",
    )(field, sea, wind, courant, rate, damp, steep, table)


def sort_kernel(owner, point, value, weight, out, flat, load, *, ranks, capacity):
    rows = owner.shape[0]
    flat[...] = jnp.zeros_like(flat)
    flat[0:1, :] = point[...].astype(F32)
    flat[1:2, :] = weight[...]
    columns = jnp.transpose(flat[...])
    load[...] = jnp.zeros_like(load)
    load[:, 0:NF] = value[...] * columns[:, 1:2]
    load[:, NF : NF + 1] = columns[:, 1:2]
    load[:, NF + 1 : NF + 2] = columns[:, 0:1]
    hits = (owner[...] == lax.broadcasted_iota(jnp.int32, (rows, ranks), 1)).astype(F32)
    before = lax.broadcasted_iota(jnp.int32, (rows, rows), 1) < lax.broadcasted_iota(jnp.int32, (rows, rows), 0)
    counts = jnp.dot(before.astype(F32), hits, preferred_element_type=F32)
    order = jnp.sum(counts * hits, axis=1, keepdims=True).astype(jnp.int32)
    target = owner[...] * capacity + order
    places = (target == lax.broadcasted_iota(jnp.int32, (rows, ranks * capacity), 1)).astype(F32)
    out[...] = lax.dot_general(
        places,
        load[...],
        (((0,), (0,)), ((), ())),
        precision=lax.Precision.HIGHEST,
        preferred_element_type=F32,
    )


def sort(owner, point, value, weight, ranks):
    rows = owner.shape[0]
    capacity = max(2, 2 * rows // ranks)

    def kernel(*refs):
        sort_kernel(*refs, ranks=ranks, capacity=capacity)

    return pl.pallas_call(
        kernel,
        in_specs=[whole()] * 4,
        out_specs=whole(),
        out_shape=jax.ShapeDtypeStruct((ranks * capacity, W), F32),
        scratch_shapes=[pltpu.VMEM((SUB, rows), F32), pltpu.VMEM((rows, W), F32)],
        compiler_params=params(),
        name="sort",
    )(owner, point.reshape(1, rows), value, weight.reshape(1, rows))


def place_kernel(arrived, out, weight):
    slots = arrived.shape[0]
    point = arrived[:, NF + 1 : NF + 2].astype(jnp.int32)
    hits = (point == lax.broadcasted_iota(jnp.int32, (slots, ROWS * W), 1)).astype(F32)
    sums = lax.dot_general(
        arrived[...],
        hits,
        (((0,), (0,)), ((), ())),
        precision=lax.Precision.HIGHEST,
        preferred_element_type=F32,
    )
    for f in range(NF):
        out[f // 2, f % 2 : f % 2 + 1, :] = sums[f : f + 1, :]
    weight[...] = jnp.broadcast_to(sums[NF : NF + 1, :], weight.shape)


def place(arrived):
    return pl.pallas_call(
        place_kernel,
        in_specs=[whole()],
        out_specs=[whole()] * 2,
        out_shape=[
            pltpu.VMEM((GROUPS, SUB, ROWS * W), F32),
            pltpu.VMEM((SUB, ROWS * W), F32),
        ],
        compiler_params=params(),
        name="place",
    )(arrived)


def sides(first, second):
    even = lax.rem(lax.axis_index("geo"), 2) == 0
    one, two = first[...], second[...]
    return jnp.where(even, two, one), jnp.where(even, one, two)


def forward_kernel(
    masked, from_south, from_north, aux_a, aux_b, own, wind, sea_in, courant, rate, damp, steep, table, wanted, gain,
    ahead, ahead_south, ahead_north, factor, lam, adjoint, state, send_a, send_b, moved,
):
    sub = sublane()
    south, north = sides(aux_a, aux_b)
    zero = jnp.zeros((SUB, W), F32)

    def full(value):
        return jnp.broadcast_to(value, (SUB, W))

    sea, wind0, steep0 = {}, {}, {}
    for r in range(ROWS):
        sea[r] = full(sea_in[:, lanes(r)].astype(F32))
        wind0[r] = full(wind[0:1, lanes(r)])
        steep0[r] = own[0:1, lanes(r)]
    for r in (0, 1):
        sea[r - 2] = full(south[2:3, r * W : (r + 1) * W])
        sea[r + 4] = full(north[2:3, r * W : (r + 1) * W])
    wind0[-1] = full(south[0:1, W : 2 * W])
    wind0[4] = full(north[0:1, 0:W])
    steep0[0] = steep0[0] + sea[0][0:1, :] * south[4:5, W : 2 * W]
    steep0[3] = steep0[3] + sea[3][0:1, :] * north[4:5, 0:W]
    steep0[-1] = south[3:4, W : 2 * W] + sea[-1][0:1, :] * own[2:3, lanes(0)]
    steep0[4] = north[3:4, 0:W] + sea[4][0:1, :] * own[1:2, lanes(3)]
    state[...] = jnp.zeros_like(state)
    for r in range(-1, 5):
        state[0:1, pl.ds((r + 1) * W, W)] = steep0[r]
        steep0[r] = full(steep0[r])

    def coefficients(group, tile):
        rows = pl.ds(pl.multiple_of(group * GROUP + tile * SUB, SUB), SUB)
        return rate[rows, :], damp[rows, :], steep[rows, :]

    def first(pair, sums):
        sums = list(sums)
        for half in range(2):
            group = 2 * pair + half
            ghosts = {
                -2: unpack_north(from_south, pair, half, 0, sub),
                -1: unpack_north(from_south, pair, half, 1, sub),
                4: unpack_south(from_north, pair, half, 0, sub),
                5: unpack_south(from_north, pair, half, 1, sub),
            }
            for tile in range(TILES):
                rows = pl.ds(tile * SUB, SUB)
                centre, along, across = weights(tile, sub, table, courant, group, False)
                grow, fade, heavy = coefficients(group, tile)
                cell = {r: masked[group, rows, lanes(r)] for r in range(ROWS)}
                for r, parts in ghosts.items():
                    cell[r] = parts[tile] * sea[r] if tile in parts else None

                def move(field, r):
                    value = centre * field[r] + along * side(tile, sub, field[r], False)
                    return sea[r] * (value + across * pick(tile, sub, field.get(r - 1), field.get(r + 1)))

                nxt = {}
                for r in range(-1, 5):
                    if cell[r] is None:
                        nxt[r] = None
                        continue
                    if r == -1:
                        value = centre * cell[r] + along * side(tile, sub, cell[r], False)
                        value = sea[r] * (value + across * cell[-2])
                    elif r == 4:
                        value = centre * cell[r] + along * side(tile, sub, cell[r], False)
                        value = sea[r] * (value + across * cell[5])
                    else:
                        value = move(cell, r)
                    nxt[r] = value * jnp.exp(grow * wind0[r] - fade * steep0[r])
                for r in range(ROWS):
                    ahead[group, rows, lanes(r)] = nxt[r]
                    value = move(nxt, r)
                    moved[group, rows, lanes(r)] = value
                    sums[r] = sums[r] + heavy * value
                if nxt[-1] is not None:
                    ahead_south[group, rows, :] = nxt[-1]
                if nxt[4] is not None:
                    ahead_north[group, rows, :] = nxt[4]
        return tuple(sums)

    sums = lax.fori_loop(0, GROUPS // 2, first, (zero,) * ROWS)
    steep1 = [total(value) for value in sums]
    for r in range(ROWS):
        state[1:2, pl.ds((r + 1) * W, W)] = steep1[r]
    steep1 = [full(value) for value in steep1]
    wind1 = [full(wind[1:2, lanes(r)]) for r in range(ROWS)]
    gains = [gain[0:1, lanes(r)] for r in range(ROWS)]

    def second(group, sums):
        sums = list(sums)
        parts = [[[None] * 3 for _ in range(ROWS)] for _ in range(2)]
        for tile in range(TILES):
            rows = pl.ds(tile * SUB, SUB)
            grow, fade, _ = coefficients(group, tile)
            for r in range(ROWS):
                value = jnp.exp(grow * wind1[r] - fade * steep1[r])
                factor[group, rows, lanes(r)] = value
                value = value * moved[group, rows, lanes(r)]
                for place, term in enumerate((value, grow * value, fade * value)):
                    for f in range(2):
                        if (f == 0 and tile > 4) or (f == 1 and tile < 4):
                            continue
                        mine = term
                        if tile == 4:
                            mine = jnp.where(sub < 4, term, 0.0) if f == 0 else jnp.where(sub < 4, 0.0, term)
                        old = parts[f][r][place]
                        parts[f][r][place] = mine if old is None else old + mine
        for r in range(ROWS):
            for f in range(2):
                mean, up, down = [total(value) for value in parts[f][r]]
                value = (gains[r] * (mean * (1.0 / ND)) - wanted[group, f : f + 1, lanes(r)]) * (1.0 / ND)
                lam[group, f : f + 1, lanes(r)] = value
                sums[r] = sums[r] + value * up
                sums[ROWS + r] = sums[ROWS + r] - value * down
        return tuple(sums)

    sums = lax.fori_loop(0, GROUPS, second, (jnp.zeros((1, W), F32),) * (2 * ROWS))
    for r in range(ROWS):
        state[2:3, pl.ds((r + 1) * W, W)] = sums[ROWS + r]
        state[3:4, pl.ds((r + 1) * W, W)] = sums[r]
    tend = [full(sums[ROWS + r]) for r in range(ROWS)]

    def third(group, sums):
        sums = list(sums)
        for tile in range(TILES):
            rows = pl.ds(tile * SUB, SUB)
            centre, along, across = weights(tile, sub, table, courant, group, True)
            grow, fade, heavy = coefficients(group, tile)
            cell = {}
            for r in range(ROWS):
                cell[r] = sea[r] * (
                    spread_lam(lam, group, tile, lanes(r), sub) * factor[group, rows, lanes(r)] + heavy * tend[r]
                )
            for r in range(ROWS):
                value = centre * cell[r] + along * side(tile, sub, cell[r], True)
                other = pick(tile, sub, cell.get(r + 1), cell.get(r - 1))
                if other is not None:
                    value = value + across * other
                value = sea[r] * value
                adjoint[group, rows, lanes(r)] = value
                value = value * ahead[group, rows, lanes(r)]
                sums[r] = sums[r] + grow * value
                sums[ROWS + r] = sums[ROWS + r] - fade * value
        return tuple(sums)

    sums = lax.fori_loop(0, GROUPS, third, (zero,) * (2 * ROWS))
    for r in range(ROWS):
        state[4:5, pl.ds((r + 1) * W, W)] = total(sums[ROWS + r])
        state[5:6, pl.ds((r + 1) * W, W)] = total(sums[r])

    def fill(ref, base):
        for f in range(NF):
            ref[f : f + 1, :] = lam[f // 2, f % 2 : f % 2 + 1, pl.ds(base * W, 2 * W)]
        here = pl.ds((base + 1) * W, 2 * W)
        ref[NF : NF + 1, :] = state[1:2, here]
        ref[NF + 1 : NF + 2, :] = state[2:3, here]
        ref[NF + 2 : NF + 3, :] = state[4:5, here]
        ref[NF + 3 : NF + 4, :] = state[4:5, here]

    even = lax.rem(lax.axis_index("geo"), 2) == 0

    @pl.when(even)
    def _():
        fill(send_a, 2)
        fill(send_b, 0)

    @pl.when(jnp.logical_not(even))
    def _():
        fill(send_a, 0)
        fill(send_b, 2)


def spread_lam(lam, group, tile, where, sub):
    if tile < 4:
        return lam[group, 0:1, where]
    if tile > 4:
        return lam[group, 1:2, where]
    return jnp.where(sub < 4, lam[group, 0:1, where], lam[group, 1:2, where])


def forward(*args):
    cells = (GROUPS, GROUP, ROWS * W)
    edge = (GROUPS, GROUP, W)
    small = jax.ShapeDtypeStruct((NF + 4, 2 * W), F32)
    specs = [whole()] * len(args)
    specs[8] = whole(pltpu.SMEM)
    return pl.pallas_call(
        forward_kernel,
        in_specs=specs,
        out_specs=[whole()] * 9,
        out_shape=[
            pltpu.VMEM(cells, F32),
            pltpu.VMEM(edge, F32),
            pltpu.VMEM(edge, F32),
            pltpu.VMEM(cells, F32),
            pltpu.VMEM((GROUPS, SUB, ROWS * W), F32),
            pltpu.VMEM(cells, F32),
            pltpu.VMEM((SUB, 6 * W), F32),
            small,
            small,
        ],
        scratch_shapes=[pltpu.VMEM(cells, F32)],
        compiler_params=params(),
        name="forward",
    )(*args)


def backward_kernel(
    ahead, ahead_south, ahead_north, factor, lam, adjoint, state, back_a, back_b, aux_a, aux_b, wind, sea_in, courant,
    rate, damp, steep, table, out, grad, ghost, low, high, fixed,
):
    sub = sublane()
    south, north = sides(aux_a, aux_b)
    back_south, back_north = sides(back_a, back_b)
    zero = jnp.zeros((SUB, W), F32)

    def full(value):
        return jnp.broadcast_to(value, (SUB, W))

    def held(place, r):
        return state[place : place + 1, pl.ds((r + 1) * W, W)]

    sea, wind0, wind1, steep0, steep1, tend1 = {}, {}, {}, {}, {}, {}
    for r in range(ROWS):
        sea[r] = full(sea_in[:, lanes(r)].astype(F32))
        wind0[r] = full(wind[0:1, lanes(r)])
        tend1[r] = full(held(2, r))
    for r in range(-1, 5):
        steep0[r] = full(held(0, r))
    for r in (0, 1):
        here = slice(r * W, (r + 1) * W)
        for place, aux, back in ((r - 2, south, back_south), (r + 4, north, back_north)):
            wind1[place] = full(aux[1:2, here])
            sea[place] = full(aux[2:3, here])
            steep1[place] = full(back[NF : NF + 1, here])
            tend1[place] = full(back[NF + 1 : NF + 2, here])
    wind0[-1] = full(south[0:1, W : 2 * W])
    wind0[4] = full(north[0:1, 0:W])
    for f in range(NF):
        ghost[f // 2, f % 2 : f % 2 + 1, 0 : 2 * W] = back_south[f : f + 1, :]
        ghost[f // 2, f % 2 : f % 2 + 1, 2 * W : 4 * W] = back_north[f : f + 1, :]

    def coefficients(group, tile):
        rows = pl.ds(pl.multiple_of(group * GROUP + tile * SUB, SUB), SUB)
        return rate[rows, :], damp[rows, :], steep[rows, :]

    def first(group, sums):
        sums = list(sums)
        for tile in range(TILES):
            rows = pl.ds(tile * SUB, SUB)
            centre, along, across = weights(tile, sub, table, courant, group, True)
            grow, fade, heavy = coefficients(group, tile)

            def outer(r, place):
                value = spread_lam(ghost, group, tile, lanes(place), sub) * jnp.exp(grow * wind1[r] - fade * steep1[r])
                return sea[r] * (value + heavy * tend1[r])

            def inner(r):
                value = spread_lam(lam, group, tile, lanes(r), sub) * factor[group, rows, lanes(r)]
                return sea[r] * (value + heavy * tend1[r])

            def side_of(near, far, edge, place, mine, keep, behind, slot):
                value = centre * near + along * side(tile, sub, near, True)
                keep[group, rows, :] = sea[edge] * (value + across * far)
                value = sea[mine] * (across * near)
                value = pick(tile, sub, None, value) if edge < 0 else pick(tile, sub, value, None)
                fixed[group, rows, lanes(place)] = value
                value = value * ahead[group, rows, lanes(mine)]
                sums[slot] = sums[slot] + grow * value
                sums[slot + 1] = sums[slot + 1] - fade * value

            if tile in SOUTH:
                side_of(outer(-1, 1), outer(-2, 0), -1, 0, 0, low, None, 0)
            if tile in NORTH:
                side_of(outer(4, 2), outer(5, 3), 4, 1, 3, high, None, 2)
            if tile in NORTH:
                value = across * inner(0) * ahead_south[group, rows, :]
                value = pick(tile, sub, value, None)
                sums[4] = sums[4] - fade * value
            if tile in SOUTH:
                value = across * inner(3) * ahead_north[group, rows, :]
                value = pick(tile, sub, None, value)
                sums[5] = sums[5] - fade * value
        return tuple(sums)

    sums = lax.fori_loop(0, GROUPS, first, (zero,) * 6)
    sums = [total(value) for value in sums]
    tend0 = {r: held(4, r) for r in range(ROWS)}
    tend0[0] = tend0[0] + sums[1]
    tend0[3] = tend0[3] + sums[3]
    tend0[-1] = back_south[NF + 2 : NF + 3, W : 2 * W] + sea[-1][0:1, :] * sums[4]
    tend0[4] = back_north[NF + 2 : NF + 3, 0:W] + sea[4][0:1, :] * sums[5]
    for r in range(ROWS):
        value = held(5, r)
        if r == 0:
            value = value + sums[0]
        if r == 3:
            value = value + sums[2]
        grad[0:1, lanes(r)] = value
        grad[1:2, lanes(r)] = held(3, r)
    tend0 = {r: full(value) for r, value in tend0.items()}

    def second(group, carry):
        for tile in range(TILES):
            rows = pl.ds(tile * SUB, SUB)
            centre, along, across = weights(tile, sub, table, courant, group, True)
            grow, fade, heavy = coefficients(group, tile)
            cell = {}
            for r in range(-1, 5):
                if r == -1:
                    if tile not in SOUTH:
                        continue
                    value = low[group, rows, :]
                elif r == 4:
                    if tile not in NORTH:
                        continue
                    value = high[group, rows, :]
                else:
                    value = adjoint[group, rows, lanes(r)]
                    if r == 0 and tile in SOUTH:
                        value = value + fixed[group, rows, lanes(0)]
                    if r == 3 and tile in NORTH:
                        value = value + fixed[group, rows, lanes(1)]
                value = value * jnp.exp(grow * wind0[r] - fade * steep0[r]) + heavy * tend0[r]
                cell[r] = sea[r] * value
            for r in range(ROWS):
                value = centre * cell[r] + along * side(tile, sub, cell[r], True)
                value = value + across * pick(tile, sub, cell.get(r + 1), cell.get(r - 1))
                out[group, rows, lanes(r)] = sea[r] * value
        return carry

    lax.fori_loop(0, GROUPS, second, 0)


def backward(*args):
    cells = (GROUPS, GROUP, ROWS * W)
    edge = (GROUPS, GROUP, W)
    specs = [whole()] * len(args)
    specs[13] = whole(pltpu.SMEM)
    return pl.pallas_call(
        backward_kernel,
        in_specs=specs,
        out_specs=[whole()] * 2,
        out_shape=[jax.ShapeDtypeStruct(cells, F32), jax.ShapeDtypeStruct((2, ROWS * W), F32)],
        scratch_shapes=[
            pltpu.VMEM((GROUPS, SUB, ROWS * W), F32),
            pltpu.VMEM(edge, F32),
            pltpu.VMEM(edge, F32),
            pltpu.VMEM((GROUPS, GROUP, 2 * W), F32),
        ],
        compiler_params=params(),
        name="backward",
    )(*args)


def swaps(count):
    near = [(i, i ^ 1) for i in range(count)]
    far = []
    for i in range(1, count - 1, 2):
        far += [(i, i + 1), (i + 1, i)]
    return near, far


def body(
    initial_spectrum,
    wind_forcing,
    sea_mask,
    courant,
    input_rate,
    damping,
    steep_weight,
    obs_owner,
    obs_point,
    obs_value,
    obs_weight,
):
    count = lax.axis_size("geo")
    near, far = swaps(count)
    table = jnp.asarray(direction_tables())
    field = initial_spectrum.reshape(GROUPS, GROUP, ROWS * W)
    sea = sea_mask.reshape(1, ROWS * W)
    north, south = pack(field)
    from_south = lax.ppermute(north, "geo", [(i, i + 1) for i in range(count - 1)])
    from_north = lax.ppermute(south, "geo", [(i + 1, i) for i in range(count - 1)])
    masked, rate, damp, steep, own, send_a, send_b = local(
        field,
        sea,
        wind_forcing,
        courant,
        input_rate.reshape(1, NB),
        damping.reshape(1, NB),
        steep_weight.reshape(1, NB),
        table,
    )
    aux_b = lax.ppermute(send_b, "geo", far)
    aux_a = lax.ppermute(send_a, "geo", near)
    slots = sort(obs_owner, obs_point, obs_value, obs_weight, count)
    arrived = lax.all_to_all(slots, "geo", split_axis=0, concat_axis=0, tiled=True)
    wanted, gain = place(arrived)
    ahead, ahead_south, ahead_north, factor, lam, adjoint, state, send_a, send_b = forward(
        masked, from_south, from_north, aux_a, aux_b, own, wind_forcing, sea, courant, rate, damp, steep, table, wanted, gain
    )
    back_b = lax.ppermute(send_b, "geo", far)
    back_a = lax.ppermute(send_a, "geo", near)
    out, grad = backward(
        ahead, ahead_south, ahead_north, factor, lam, adjoint, state, back_a, back_b, aux_a, aux_b, wind_forcing, sea,
        courant, rate, damp, steep, table,
    )
    return grad, out.reshape(NB, ROWS * W)


def solution(mesh):
    return jax.shard_map(
        body,
        mesh=mesh,
        in_specs=(
            P(None, ("groups", "geo")),
            P(None, ("groups", "geo")),
            P(("groups", "geo")),
            P(),
            P(),
            P(),
            P(),
            P(("groups", "geo"), None),
            P(("groups", "geo")),
            P(("groups", "geo"), None),
            P(("groups", "geo")),
        ),
        out_specs=(P(None, ("groups", "geo")), P(None, ("groups", "geo"))),
        check_vma=False,
    )
```

```python
import math

import jax
import jax.numpy as jnp
import numpy as np
from jax import lax
from jax.experimental import pallas as pl
from jax.experimental.pallas import tpu as pltpu
from jax.sharding import PartitionSpec as P

ND = 36
NF = 36
NB = 1296
W = 128
ROWS = 4
SUB = 8
GROUP = 72
TILES = GROUP // SUB
GROUPS = NB // GROUP
CHUNKS = 6
F32 = jnp.float32
LIMIT = 14 * 1024 * 1024
LOG2E = math.log2(math.e)
LN2 = math.log(2.0)
LAND = 1.0e5

CELLS = (GROUPS, GROUP, ROWS * W)
EDGE = (GROUPS, GROUP, W)
EDGES = (GROUPS, GROUP, 2 * W)
BINS = (NB, W)
STATE = (16, 8 * W)
STEEP0, WIND0, WIND1, SEA, STEEP1, TEND1, GRAD1, TEND0, GRAD0, PASS0 = range(10)

NORTH = (0, 1, 2, 4, 5, 6)
SOUTH = (2, 3, 4, 6, 7, 8)
FROM_WEST = (0, 4, 8)
FROM_EAST = (2, 6)


def direction_tables():
    angle = np.float32(2.0 * math.pi) * np.arange(ND, dtype=np.float32) / np.float32(ND)
    cosine = np.tile(np.cos(angle), 2)[:, None]
    sine = np.tile(np.sin(angle), 2)[:, None]
    lane = np.arange(W)[None, :]
    east = cosine >= 0
    west_ok = (lane > 0).astype(np.float32)
    east_ok = (lane < W - 1).astype(np.float32)
    one = np.ones((1, W), np.float32)
    forward = np.abs(cosine) * np.where(east, west_ok, east_ok)
    backward = np.abs(cosine) * np.where(east, east_ok, west_ok)
    return np.stack(
        [(np.abs(cosine) + np.abs(sine)) * one, np.abs(sine) * one, forward, backward]
    ).astype(np.float32)


def sublane():
    return lax.broadcasted_iota(jnp.int32, (SUB, W), 0)


def north_mask(tile, sub):
    return {2: sub < 2, 4: sub >= 4, 6: sub < 6}.get(tile)


def west_mask(tile, sub):
    return {1: sub < 1, 3: sub >= 3, 5: sub < 5, 7: sub >= 7}.get(tile)


def side(tile, sub, value, reverse):
    west = tile not in (FROM_WEST if reverse else FROM_EAST)
    east = tile not in (FROM_EAST if reverse else FROM_WEST)
    from_west = pltpu.roll(value, 1, 1) if west else None
    from_east = pltpu.roll(value, W - 1, 1) if east else None
    if from_east is None:
        return from_west
    if from_west is None:
        return from_east
    mask = west_mask(tile, sub)
    return jnp.where(mask, from_east, from_west) if reverse else jnp.where(mask, from_west, from_east)


def pick(tile, sub, north, south):
    mask = north_mask(tile, sub)
    if mask is None:
        return north if tile in NORTH else south
    if north is None and south is None:
        return None
    return jnp.where(mask, 0.0 if north is None else north, 0.0 if south is None else south)


def plus(value, other):
    return value if other is None else value + other


def times(factor, value):
    return None if value is None else factor * value


def speed(tile, sub, courant, group):
    first, second = courant[2 * group], courant[2 * group + 1]
    if tile == 4:
        return jnp.where(sub < 4, first, second)
    return jnp.full((SUB, W), first if tile < 4 else second, F32)


def lanes(row):
    return pl.ds(row * W, W)


def column(row):
    return pl.ds((row + 2) * W, W)


def bins(group, tile):
    return pl.ds(pl.multiple_of(group * GROUP + tile * SUB, SUB), SUB)


def total(value):
    return jnp.sum(value, axis=0, keepdims=True)


def full(value):
    return jnp.broadcast_to(value, (SUB, W))


def whole(memory=pltpu.VMEM):
    return pl.BlockSpec(memory_space=memory)


def call(kernel, name, inputs, outputs, scratch=(), smem=(), away=(), out_away=(), aliases=None, cost=0):
    specs, operands = [], []
    for place, (value, resident) in enumerate(inputs):
        specs.append(whole(pltpu.SMEM if place in smem else pl.ANY if place in away else pltpu.VMEM))
        operands.append(pltpu.with_memory_space_constraint(value, pltpu.VMEM) if resident else value)
    shapes = [pltpu.VMEM(shape, F32) if resident else jax.ShapeDtypeStruct(shape, F32) for shape, resident in outputs]
    return pl.pallas_call(
        kernel,
        in_specs=specs,
        out_specs=[whole(pl.ANY if place in out_away else pltpu.VMEM) for place in range(len(outputs))],
        out_shape=shapes,
        scratch_shapes=list(scratch),
        input_output_aliases=aliases or {},
        compiler_params=pltpu.CompilerParams(vmem_limit_bytes=LIMIT),
        cost_estimate=pl.CostEstimate(flops=cost, bytes_accessed=cost, transcendentals=0) if cost else None,
        name=name,
    )(*operands)


def pack_kernel(field, sea_in, north, south):
    sub = sublane()
    both = (sub < 2) | ((sub >= 4) & (sub < 6))
    sea = [full(sea_in[:, lanes(r)].astype(F32)) for r in range(ROWS)]
    for pair in range(field.shape[0] // 2):
        for row in range(2):

            def cell(half, tile, base):
                return field[2 * pair + half, pl.ds(tile * SUB, SUB), lanes(base + row)] * sea[base + row]

            def put(ref, tile, value):
                ref[pair, pl.ds(tile * SUB, SUB), lanes(row)] = value

            rest = []
            for half in range(2):
                sixth = cell(half, 6, 2)
                for place, tile in enumerate((0, 1, 5)):
                    put(north, half * 4 + place, cell(half, tile, 2))
                mixed = jnp.where(sub < 2, cell(half, 2, 2), jnp.where(sub < 4, sixth, cell(half, 4, 2)))
                put(north, half * 4 + 3, mixed)
                rest.append(sixth)
            put(north, 8, jnp.where(both, rest[0], pltpu.roll(rest[1], 2, 0)))
            rest = []
            for half in range(2):
                second = cell(half, 2, 0)
                for place, tile in enumerate((3, 7, 8)):
                    put(south, half * 4 + place, cell(half, tile, 0))
                put(south, half * 4 + 3, jnp.where(sub < 4, cell(half, 4, 0), second))
                rest.append(jnp.where(sub < 4, second, cell(half, 6, 0)))
            put(south, 8, jnp.where(both, pltpu.roll(rest[1], 2, 0), rest[0]))


def pack(field, sea):
    steps = 3
    each = GROUPS // steps
    half = jax.ShapeDtypeStruct((GROUPS // 2, GROUP, 2 * W), F32)
    return pl.pallas_call(
        pack_kernel,
        grid=(steps,),
        in_specs=[pl.BlockSpec((each, GROUP, ROWS * W), lambda i: (i, 0, 0)), whole()],
        out_specs=[pl.BlockSpec((each // 2, GROUP, 2 * W), lambda i: (i, 0, 0))] * 2,
        out_shape=[half, half],
        compiler_params=pltpu.CompilerParams(vmem_limit_bytes=LIMIT),
        name="pack",
    )(pltpu.with_memory_space_constraint(field, pltpu.HBM), sea)


def unpack_north(halo, pair, half, row, sub):
    def get(tile):
        return halo[pair, pl.ds(tile * SUB, SUB), lanes(row)]

    mixed, last = get(half * 4 + 3), get(8)
    if half:
        last = pltpu.roll(last, 6, 0)
    return {
        0: get(half * 4),
        1: get(half * 4 + 1),
        2: mixed,
        4: mixed,
        5: get(half * 4 + 2),
        6: jnp.where((sub >= 2) & (sub < 4), mixed, last),
    }


def unpack_south(halo, pair, half, row, sub):
    def get(tile):
        return halo[pair, pl.ds(tile * SUB, SUB), lanes(row)]

    mixed, last = get(half * 4 + 3), get(8)
    if half:
        last = pltpu.roll(last, 6, 0)
    return {
        2: jnp.where(sub < 4, last, mixed),
        3: get(half * 4),
        4: mixed,
        6: last,
        7: get(half * 4 + 1),
        8: get(half * 4 + 2),
    }


def spread(row_ref, out, scale):
    for start in range(0, NB, W):
        size = min(W, NB - start)
        chunk = row_ref[:, pl.ds(start, size)] * scale
        out[pl.ds(start, size), :] = jnp.transpose(jnp.broadcast_to(chunk, (W, size)))


def layout(rows, ranks):
    lines = max(2, 2 * rows // ranks) // 2
    return lines, -(-(lines + 7) // SUB) * SUB


def sort(owner, point, value, weight, flat, load, ranks):
    rows = owner.shape[0]
    lines, block = layout(rows, ranks)
    flat[...] = jnp.zeros_like(flat)
    flat[0:1, :] = point[...].astype(F32)
    flat[1:2, :] = weight[...]
    columns = jnp.transpose(flat[...])
    load[...] = jnp.zeros_like(load)
    for half in range(2):
        here, base = pl.ds(half * rows, rows), half * (W // 2)
        load[here, pl.ds(base, NF)] = value[...] * columns[:, 1:2]
        load[here, pl.ds(base + NF, 1)] = columns[:, 1:2]
        load[here, pl.ds(base + NF + 1, 1)] = columns[:, 0:1]
    hits = (owner[...] == lax.broadcasted_iota(jnp.int32, (rows, ranks), 1)).astype(F32)
    before = lax.broadcasted_iota(jnp.int32, (rows, rows), 1) < lax.broadcasted_iota(jnp.int32, (rows, rows), 0)
    counts = jnp.dot(before.astype(F32), hits, preferred_element_type=F32)
    order = jnp.sum(counts * hits, axis=1, keepdims=True).astype(jnp.int32)
    target = owner[...] * block + order // 2
    odd = order % 2
    spots = lax.broadcasted_iota(jnp.int32, (rows, ranks * block), 1)
    places = [((target == spots) & (odd == half)).astype(F32) for half in range(2)]
    return lax.dot_general(
        jnp.concatenate(places, axis=0),
        load[...],
        (((0,), (0,)), ((), ())),
        precision=lax.Precision.HIGHEST,
        preferred_element_type=F32,
    )


def local_kernel(
    field, sea_in, wind, courant, rate_in, damp_in, steep_in, table, owner, point, value, weight,
    flow, rate, damp, steep, centre, ahead, back, across, own, slots,
    cells, flat, load, sems, *, ranks,
):
    sub = sublane()
    each = GROUPS // CHUNKS
    copies = [
        pltpu.make_async_copy(field.at[pl.ds(c * each, each)], cells.at[pl.ds(c * each, each)], sems.at[c])
        for c in range(CHUNKS)
    ]
    for copy in copies:
        copy.start()
    spread(rate_in, rate, LOG2E)
    spread(damp_in, damp, LOG2E)
    spread(steep_in, steep, 1.0)
    slots[...] = sort(owner, point, value, weight, flat, load, ranks)
    sea = [full(sea_in[:, lanes(r)].astype(F32)) for r in range(ROWS)]
    zero = jnp.zeros((SUB, W), F32)

    def step(group, sums):
        sums = list(sums)
        for tile in range(TILES):
            rows, spot = pl.ds(tile * SUB, SUB), bins(group, tile)
            pace = speed(tile, sub, courant, group)
            middle = 1.0 - pace * table[0, rows, :]
            over = pace * table[1, rows, :]
            along = pace * table[2, rows, :]
            centre[spot, :] = middle
            across[spot, :] = over
            ahead[spot, :] = along
            back[spot, :] = pace * table[3, rows, :]
            heavy = steep[spot, :]
            cell = {r: cells[group, rows, lanes(r)] * sea[r] for r in range(ROWS)}
            for r in range(ROWS):
                moved = middle * cell[r] + along * side(tile, sub, cell[r], False)
                moved = plus(moved, times(over, pick(tile, sub, cell.get(r - 1), cell.get(r + 1))))
                flow[group, rows, lanes(r)] = moved
                sums[r] = sums[r] + heavy * moved
            gone = heavy * over
            if tile in NORTH:
                sums[ROWS] = sums[ROWS] + pick(tile, sub, gone * cell[ROWS - 1], None)
            if tile in SOUTH:
                sums[ROWS + 1] = sums[ROWS + 1] + pick(tile, sub, None, gone * cell[0])
        return tuple(sums)

    sums = (zero,) * (ROWS + 2)
    for c in range(CHUNKS):
        copies[c].wait()
        sums = lax.fori_loop(c * each, (c + 1) * each, step, sums)
    sums = [total(value) for value in sums]
    own[...] = jnp.zeros_like(own)
    for r in range(ROWS):
        own[0:1, lanes(r)] = sums[r] * sea[r][0:1, :]
    own[1:2, lanes(ROWS - 1)] = sums[ROWS]
    own[1:2, lanes(0)] = sums[ROWS + 1]

    lines, block = layout(owner.shape[0], ranks)
    me = lax.axis_index("geo")

    def hand(near, far, dest):
        last = pl.ds(pl.multiple_of(dest * block + block - SUB, SUB), SUB)
        values = jnp.concatenate(
            [
                slots[last, :][0:1, :],
                wind[0:1, lanes(near)],
                wind[1:2, lanes(far)],
                wind[1:2, lanes(near)],
                sea[far][0:1, :],
                sea[near][0:1, :],
                own[0:1, lanes(near)],
                own[1:2, lanes(near)],
            ],
            axis=0,
        )
        slots[last, :] = values

    @pl.when(me < ranks - 1)
    def _():
        hand(ROWS - 1, ROWS - 2, me + 1)

    @pl.when(me > 0)
    def _():
        hand(0, 1, me - 1)


def local(field, sea, wind, courant, rate, damp, steep, table, owner, point, value, weight, ranks):
    rows = owner.shape[0]
    _, block = layout(rows, ranks)

    def kernel(*refs):
        local_kernel(*refs, ranks=ranks)

    args = (
        pltpu.with_memory_space_constraint(field, pltpu.HBM), sea, wind, courant, rate, damp, steep, table,
        owner, point, value, weight,
    )
    return call(
        kernel,
        "local",
        [(arg, False) for arg in args],
        [(CELLS, True)] + [(BINS, True)] * 7 + [((SUB, ROWS * W), True), ((ranks * block, W), False)],
        [
            pltpu.VMEM(CELLS, F32),
            pltpu.VMEM((SUB, rows), F32),
            pltpu.VMEM((2 * rows, W), F32),
            pltpu.SemaphoreType.DMA((CHUNKS,)),
        ],
        smem=(3,),
        away=(0,),
    )


def place(arrived, ranks, rows, wanted, gain):
    lines, block = layout(rows, ranks)
    size = ranks * block
    held = lax.rem(lax.broadcasted_iota(jnp.int32, (size, W), 0), block) < lines
    load = jnp.where(held, arrived[...], 0.0)
    sums = 0.0
    for half in range(2):
        mine = load[:, half * (W // 2) : (half + 1) * (W // 2)]
        point = mine[:, NF + 1 : NF + 2].astype(jnp.int32)
        hits = (point == lax.broadcasted_iota(jnp.int32, (size, ROWS * W), 1)).astype(F32)
        sums = sums + lax.dot_general(
            mine,
            hits,
            (((0,), (0,)), ((), ())),
            precision=lax.Precision.HIGHEST,
            preferred_element_type=F32,
        )
    for f in range(NF):
        rows_of = slice(4 * (f % 2), 4 * (f % 2) + 4)
        wanted[f // 2, rows_of, :] = jnp.broadcast_to(sums[f : f + 1, :] * (1.0 / ND), (4, ROWS * W))
    gain[...] = jnp.broadcast_to(sums[NF : NF + 1, :] * (1.0 / (ND * ND)), gain.shape)


def early_kernel(
    arrived, flow, own, wind, sea_in, rate, damp, steep, centre, ahead, across, next_, factor, moved, wanted, gain, state,
    *, ranks, rows,
):
    sub = sublane()
    place(arrived, ranks, rows, wanted, gain)
    lines, block = layout(rows, ranks)
    me = lax.axis_index("geo")

    def aux(source, there):
        source = jnp.clip(source, 0, ranks - 1)
        last = pl.ds(pl.multiple_of(source * block + block - SUB, SUB), SUB)
        return jnp.where(there, arrived[last, :], 0.0)

    south, north = aux(me - 1, me > 0), aux(me + 1, me < ranks - 1)
    state[...] = jnp.zeros_like(state)
    for near, far, values in ((-1, -2, south), (4, 5, north)):
        state[WIND0 : WIND0 + 1, column(near)] = values[1:2, :]
        state[WIND1 : WIND1 + 1, column(far)] = values[2:3, :]
        state[WIND1 : WIND1 + 1, column(near)] = values[3:4, :]
        state[SEA : SEA + 1, column(far)] = values[4:5, :]
        state[SEA : SEA + 1, column(near)] = values[5:6, :]
    here = pl.ds(2 * W, ROWS * W)
    state[WIND0 : WIND0 + 1, here] = wind[0:1, :]
    state[WIND1 : WIND1 + 1, here] = wind[1:2, :]
    state[SEA : SEA + 1, here] = sea_in[...].astype(F32)
    steeps = {r: own[0:1, lanes(r)] for r in range(ROWS)}
    steeps[0] = steeps[0] + south[7:8, :]
    steeps[3] = steeps[3] + north[7:8, :]
    steeps[-1] = south[6:7, :] + own[1:2, lanes(0)]
    steeps[4] = north[6:7, :] + own[1:2, lanes(3)]
    for r, value in steeps.items():
        state[STEEP0 : STEEP0 + 1, column(r)] = jnp.where(state[SEA : SEA + 1, column(r)] > 0.5, value, LAND)
    steep0 = [full(state[STEEP0 : STEEP0 + 1, column(r)]) for r in range(ROWS)]
    wind0 = [full(state[WIND0 : WIND0 + 1, column(r)]) for r in range(ROWS)]

    def step(group, sums):
        sums = list(sums)
        for tile in range(TILES):
            rows, spot = pl.ds(tile * SUB, SUB), bins(group, tile)
            grow, fade, heavy = rate[spot, :], damp[spot, :], steep[spot, :]
            middle, along, over = centre[spot, :], ahead[spot, :], across[spot, :]
            cell = {}
            for r in range(ROWS):
                gained = jnp.exp2(grow * wind0[r] - fade * steep0[r])
                factor[group, rows, lanes(r)] = gained
                cell[r] = flow[group, rows, lanes(r)] * gained
                next_[group, rows, lanes(r)] = cell[r]
            for r in range(ROWS):
                value = middle * cell[r] + along * side(tile, sub, cell[r], False)
                value = plus(value, times(over, pick(tile, sub, cell.get(r - 1), cell.get(r + 1))))
                moved[group, rows, lanes(r)] = value
                sums[r] = sums[r] + heavy * value
        return tuple(sums)

    sums = lax.fori_loop(0, GROUPS, step, (jnp.zeros((SUB, W), F32),) * ROWS)
    for r in range(ROWS):
        state[STEEP1 : STEEP1 + 1, column(r)] = total(sums[r])


def early(arrived, flow, own, wind, sea, rate, damp, steep, centre, ahead, across, ranks, rows):
    def kernel(*refs):
        early_kernel(*refs, ranks=ranks, rows=rows)

    inputs = [(arrived, False), (flow, True), (own, True), (wind, False), (sea, False)]
    inputs += [(value, True) for value in (rate, damp, steep, centre, ahead, across)]
    return call(
        kernel,
        "early",
        inputs,
        [(CELLS, True)] * 3 + [((GROUPS, SUB, ROWS * W), True), ((SUB, ROWS * W), True), (STATE, True)],
    )


def split_lam(lam, group, tile, where):
    if tile < 4:
        return lam[group, 0:1, where]
    if tile > 4:
        return lam[group, 4:5, where]
    return lam[group, :, where]


def late_kernel(
    next_in, factor, moved, from_south, from_north, wanted, gain, state_in, rate, damp, steep, centre, ahead, back, across,
    next_, next_south, next_north, source, edges, state, send_a, send_b,
    fixed, growth, lam, halo_south, halo_north, sems,
):
    sub = sublane()
    zero = jnp.zeros((SUB, W), F32)
    each = GROUPS // 2 // 3
    copies = []
    for c in range(3):
        here = pl.ds(c * each, each)
        copies.append(pltpu.make_async_copy(from_south.at[here], halo_south.at[here], sems.at[2 * c]))
        copies.append(pltpu.make_async_copy(from_north.at[here], halo_north.at[here], sems.at[2 * c + 1]))
    for copy in copies:
        copy.start()
    state[...] = state_in[...]

    def held(place, r):
        return full(state[place : place + 1, column(r)])

    steep0 = {r: held(STEEP0, r) for r in (-1, 4)}
    wind0 = {r: held(WIND0, r) for r in (-1, 4)}

    def first(pair, sums):
        sums = list(sums)
        for half in range(2):
            group = 2 * pair + half
            ghosts = {
                -2: unpack_north(halo_south, pair, half, 0, sub),
                -1: unpack_north(halo_south, pair, half, 1, sub),
                4: unpack_south(halo_north, pair, half, 0, sub),
                5: unpack_south(halo_north, pair, half, 1, sub),
            }
            for tile in range(TILES):
                rows, spot = pl.ds(tile * SUB, SUB), bins(group, tile)
                grow, fade, heavy = rate[spot, :], damp[spot, :], steep[spot, :]
                middle, along, over = centre[spot, :], ahead[spot, :], across[spot, :]
                beyond = {}
                changes = {}
                for near, far, mine, second, tiles, north in ((-1, -2, 0, 1, NORTH, True), (4, 5, 3, 2, SOUTH, False)):
                    if tile not in tiles:
                        continue

                    def only(value):
                        return pick(tile, sub, value, None) if north else pick(tile, sub, None, value)

                    cell = ghosts[near][tile]
                    gained = jnp.exp2(grow * wind0[near] - fade * steep0[near])
                    value = middle * cell + along * side(tile, sub, cell, False) + over * ghosts[far][tile]
                    value = value * gained
                    (next_south if north else next_north)[group, rows, :] = value
                    extra = only(over * cell) * factor[group, rows, lanes(mine)]
                    next_[group, rows, lanes(mine)] = next_in[group, rows, lanes(mine)] + extra
                    change = middle * extra + along * side(tile, sub, extra, False) + only(over * value)
                    changes[mine] = plus(change, changes.get(mine))
                    changes[second] = plus(over * extra, changes.get(second))
                for r, change in changes.items():
                    sums[r] = sums[r] + heavy * change
                    fixed[group, rows, lanes(r)] = moved[group, rows, lanes(r)] + change
                for r in range(ROWS):
                    if r not in changes:
                        fixed[group, rows, lanes(r)] = moved[group, rows, lanes(r)]
        return tuple(sums)

    sums = (zero,) * ROWS
    for c in range(3):
        copies[2 * c].wait()
        copies[2 * c + 1].wait()
        sums = lax.fori_loop(c * each, (c + 1) * each, first, sums)
    for r in range(ROWS):
        value = state[STEEP1 : STEEP1 + 1, column(r)] + total(sums[r])
        state[STEEP1 : STEEP1 + 1, column(r)] = jnp.where(state[SEA : SEA + 1, column(r)] > 0.5, value, LAND)
    steep1 = [held(STEEP1, r) for r in range(ROWS)]
    wind1 = [held(WIND1, r) for r in range(ROWS)]
    gains = [gain[:, lanes(r)] for r in range(ROWS)]

    def second(group, sums):
        sums = list(sums)
        means = [[None, None] for _ in range(ROWS)]
        ups = [[None, None] for _ in range(ROWS)]
        downs = [[None, None] for _ in range(ROWS)]
        for tile in range(TILES):
            rows, spot = pl.ds(tile * SUB, SUB), bins(group, tile)
            grow, fade = rate[spot, :], damp[spot, :]
            for r in range(ROWS):
                value = jnp.exp2(grow * wind1[r] - fade * steep1[r])
                growth[group, rows, lanes(r)] = value
                value = value * fixed[group, rows, lanes(r)]
                for parts, term in ((means, value), (ups, grow * value), (downs, fade * value)):
                    if tile == 4:
                        parts[r][0] = plus(jnp.where(sub < 4, term, 0.0), parts[r][0])
                        parts[r][1] = jnp.where(sub < 4, 0.0, term)
                    else:
                        f = 0 if tile < 4 else 1
                        parts[r][f] = plus(term, parts[r][f])
        for r in range(ROWS):
            one, two = means[r]
            one = one + pltpu.roll(one, 4, 0)
            two = two + pltpu.roll(two, 4, 0)
            both = jnp.where(sub < 4, one, two)
            both = both + jnp.where((sub & 2) == 0, pltpu.roll(both, 6, 0), pltpu.roll(both, 2, 0))
            both = both + jnp.where((sub & 1) == 0, pltpu.roll(both, 7, 0), pltpu.roll(both, 1, 0))
            value = gains[r] * both - wanted[group, :, lanes(r)]
            lam[group, :, lanes(r)] = value
            up, down = value[0:1, :], value[4:5, :]
            sums[r] = sums[r] + (up * ups[r][0] + down * ups[r][1])
            sums[ROWS + r] = sums[ROWS + r] + (up * downs[r][0] + down * downs[r][1])
        return tuple(sums)

    sums = lax.fori_loop(0, GROUPS, second, (zero,) * (2 * ROWS))
    for r in range(ROWS):
        state[GRAD1 : GRAD1 + 1, column(r)] = total(sums[r]) * LN2
        state[TEND1 : TEND1 + 1, column(r)] = total(sums[ROWS + r]) * (-LN2)
    tend1 = [held(TEND1, r) for r in range(ROWS)]

    def third(group, sums):
        sums = list(sums)
        for tile in range(TILES):
            rows, spot = pl.ds(tile * SUB, SUB), bins(group, tile)
            grow, fade, heavy = rate[spot, :], damp[spot, :], steep[spot, :]
            middle, along, over = centre[spot, :], back[spot, :], across[spot, :]
            cell = {}
            for r in range(ROWS):
                cell[r] = split_lam(lam, group, tile, lanes(r)) * growth[group, rows, lanes(r)] + heavy * tend1[r]
                source[group, rows, lanes(r)] = cell[r]
            for place, r in enumerate((0, ROWS - 1)):
                value = middle * cell[r] + along * side(tile, sub, cell[r], True)
                value = plus(value, times(over, pick(tile, sub, cell.get(r + 1), cell.get(r - 1))))
                edges[group, rows, lanes(place)] = value
                value = value * next_[group, rows, lanes(r)]
                sums[place] = sums[place] + grow * value
                sums[2 + place] = sums[2 + place] + fade * value
        return tuple(sums)

    sums = lax.fori_loop(0, GROUPS, third, (zero,) * 4)
    for place, r in enumerate((0, ROWS - 1)):
        state[GRAD0 : GRAD0 + 1, column(r)] = total(sums[place]) * LN2
        state[TEND0 : TEND0 + 1, column(r)] = total(sums[2 + place]) * (-LN2)

    def fill(ref, base):
        for f in range(NF):
            ref[f : f + 1, :] = lam[f // 2, 4 * (f % 2) : 4 * (f % 2) + 1, pl.ds(base * W, 2 * W)]
        here = pl.ds((base + 2) * W, 2 * W)
        for place, name in enumerate((STEEP1, TEND1, TEND0, TEND0)):
            ref[NF + place : NF + place + 1, :] = state[name : name + 1, here]

    even = lax.rem(lax.axis_index("geo"), 2) == 0

    @pl.when(even)
    def _():
        fill(send_a, 2)
        fill(send_b, 0)

    @pl.when(jnp.logical_not(even))
    def _():
        fill(send_a, 0)
        fill(send_b, 2)


def late(next_, factor, moved, from_south, from_north, wanted, gain, state, coefficients):
    inputs = [(next_, True), (factor, True), (moved, True), (from_south, False), (from_north, False)]
    inputs += [(value, True) for value in (wanted, gain, state) + coefficients]
    halo = (GROUPS // 2, GROUP, 2 * W)
    return call(
        late_kernel,
        "late",
        inputs,
        [(CELLS, True)] + [(EDGE, True)] * 2 + [(CELLS, True), (EDGES, True), (STATE, True)]
        + [((NF + 4, 2 * W), False)] * 2,
        [
            pltpu.VMEM(CELLS, F32),
            pltpu.VMEM(CELLS, F32),
            pltpu.VMEM((GROUPS, SUB, ROWS * W), F32),
            pltpu.VMEM(halo, F32),
            pltpu.VMEM(halo, F32),
            pltpu.SemaphoreType.DMA((6,)),
        ],
        away=(3, 4),
        aliases={0: 0},
    )


def inner_kernel(
    next_, next_south, next_north, source, state_in, rate, damp, centre, back, across,
    inside, factor_south, factor_north, state,
):
    sub = sublane()
    zero = jnp.zeros((SUB, W), F32)
    state[...] = state_in[...]
    wind0 = {r: full(state[WIND0 : WIND0 + 1, column(r)]) for r in (-1, 4)}
    steep0 = {r: full(state[STEEP0 : STEEP0 + 1, column(r)]) for r in (-1, 4)}

    def step(group, sums):
        sums = list(sums)
        for tile in range(TILES):
            rows, spot = pl.ds(tile * SUB, SUB), bins(group, tile)
            grow, fade = rate[spot, :], damp[spot, :]
            if tile in SOUTH:
                factor_south[group, rows, :] = jnp.exp2(grow * wind0[-1] - fade * steep0[-1])
            if tile in NORTH:
                factor_north[group, rows, :] = jnp.exp2(grow * wind0[4] - fade * steep0[4])
            middle, along, over = centre[spot, :], back[spot, :], across[spot, :]
            cell = {r: source[group, rows, lanes(r)] for r in range(ROWS)}
            for place, r in enumerate((1, 2)):
                value = middle * cell[r] + along * side(tile, sub, cell[r], True)
                value = value + over * pick(tile, sub, cell[r + 1], cell[r - 1])
                inside[group, rows, lanes(place)] = value
                value = value * next_[group, rows, lanes(r)]
                sums[place] = sums[place] + grow * value
                sums[2 + place] = sums[2 + place] + fade * value
            gone = fade * over
            if tile in NORTH:
                value = pick(tile, sub, cell[0] * next_south[group, rows, :], None)
                sums[4] = sums[4] + gone * value
            if tile in SOUTH:
                value = pick(tile, sub, None, cell[3] * next_north[group, rows, :])
                sums[5] = sums[5] + gone * value
        return tuple(sums)

    sums = lax.fori_loop(0, GROUPS, step, (zero,) * 6)
    for place, r in enumerate((1, 2)):
        state[GRAD0 : GRAD0 + 1, column(r)] = total(sums[place]) * LN2
        state[TEND0 : TEND0 + 1, column(r)] = total(sums[2 + place]) * (-LN2)
    state[TEND0 : TEND0 + 1, column(-1)] = total(sums[4]) * (-LN2)
    state[TEND0 : TEND0 + 1, column(4)] = total(sums[5]) * (-LN2)


def inner(*args):
    return call(
        inner_kernel,
        "inner",
        [(arg, True) for arg in args],
        [(EDGES, True), (EDGE, True), (EDGE, True), (STATE, True)],
        cost=1 << 22,
    )


def last_kernel(
    next_, factor, factor_south, factor_north, edges, inside, state, back_a, back_b, rate, damp, steep, centre, back, across,
    out, grad, rims, low, high, ghosts, lam, cells, sems,
):
    sub = sublane()
    zero = jnp.zeros((SUB, W), F32)
    even = lax.rem(lax.axis_index("geo"), 2) == 0
    ghosts[0] = jnp.where(even, back_b[...], back_a[...])
    ghosts[1] = jnp.where(even, back_a[...], back_b[...])
    for group in range(GROUPS):
        for where in range(2):
            for row in range(2):
                one = ghosts[where, 2 * group : 2 * group + 1, lanes(row)]
                two = ghosts[where, 2 * group + 1 : 2 * group + 2, lanes(row)]
                lam[group, :, lanes(2 * where + row)] = jnp.where(sub < 4, one, two)
    sea = {r: full(state[SEA : SEA + 1, column(r)]) for r in range(-2, 6)}
    wind1, steep1, tend1 = {}, {}, {}
    for r in (-2, -1, 4, 5):
        where, here = (0, lanes(r + 2)) if r < 0 else (1, lanes(r - 4))
        wind1[r] = full(state[WIND1 : WIND1 + 1, column(r)])
        value = ghosts[where, NF : NF + 1, here]
        steep1[r] = full(jnp.where(sea[r][0:1, :] > 0.5, value, LAND))
        tend1[r] = full(ghosts[where, NF + 1 : NF + 2, here])

    def first(group, sums):
        sums = list(sums)
        for tile in range(TILES):
            rows, spot = pl.ds(tile * SUB, SUB), bins(group, tile)
            grow, fade, heavy = rate[spot, :], damp[spot, :], steep[spot, :]
            middle, along, over = centre[spot, :], back[spot, :], across[spot, :]

            def ghost(r):
                value = split_lam(lam, group, tile, lanes(r + 2 if r < 0 else r - 2))
                return value * jnp.exp2(grow * wind1[r] - fade * steep1[r]) + heavy * tend1[r]

            for near, far, mine, place, tiles in ((-1, -2, 0, 0, SOUTH), (4, 5, 3, 1, NORTH)):
                if tile not in tiles:
                    continue
                cell = ghost(near)
                value = middle * cell + along * side(tile, sub, cell, True) + over * ghost(far)
                (low if place == 0 else high)[group, rows, :] = value
                value = over * cell
                value = pick(tile, sub, None, value) if place == 0 else pick(tile, sub, value, None)
                rims[group, rows, lanes(place)] = edges[group, rows, lanes(place)] + value
                value = value * next_[group, rows, lanes(mine)]
                sums[place] = sums[place] + grow * value
                sums[2 + place] = sums[2 + place] + fade * value
        return tuple(sums)

    sums = lax.fori_loop(0, GROUPS, first, (zero,) * 4)
    sums = [total(value) * LN2 for value in sums]
    tend0 = {r: state[TEND0 : TEND0 + 1, column(r)] for r in range(-1, 5)}
    grad0 = [state[GRAD0 : GRAD0 + 1, column(r)] for r in range(ROWS)]
    tend0[0], grad0[0] = tend0[0] - sums[2], grad0[0] + sums[0]
    tend0[3], grad0[3] = tend0[3] - sums[3], grad0[3] + sums[1]
    tend0[-1] = tend0[-1] + ghosts[0, NF + 2 : NF + 3, lanes(1)]
    tend0[4] = tend0[4] + ghosts[1, NF + 2 : NF + 3, lanes(0)]
    for r in range(ROWS):
        grad[0:1, lanes(r)] = grad0[r]
        grad[1:2, lanes(r)] = state[GRAD1 : GRAD1 + 1, column(r)]
    tend0 = {r: full(value) for r, value in tend0.items()}

    def second(group, carry):
        for tile in range(TILES):
            rows, spot = pl.ds(tile * SUB, SUB), bins(group, tile)
            heavy = steep[spot, :]
            middle, along, over = centre[spot, :], back[spot, :], across[spot, :]
            cell = {}
            for r in range(-1, 5):
                if r == -1:
                    if tile not in SOUTH:
                        continue
                    value = low[group, rows, :] * factor_south[group, rows, :]
                elif r == 4:
                    if tile not in NORTH:
                        continue
                    value = high[group, rows, :] * factor_north[group, rows, :]
                else:
                    if r == 0:
                        value = (rims if tile in SOUTH else edges)[group, rows, lanes(0)]
                    elif r == 3:
                        value = (rims if tile in NORTH else edges)[group, rows, lanes(1)]
                    else:
                        value = inside[group, rows, lanes(r - 1)]
                    value = value * factor[group, rows, lanes(r)]
                cell[r] = value + heavy * tend0[r]
            for r in range(ROWS):
                value = middle * cell[r] + along * side(tile, sub, cell[r], True)
                value = value + over * pick(tile, sub, cell.get(r + 1), cell.get(r - 1))
                cells[group, rows, lanes(r)] = sea[r] * value
        return carry

    each = GROUPS // CHUNKS
    copies = []
    for c in range(CHUNKS):
        lax.fori_loop(c * each, (c + 1) * each, second, 0)
        here = pl.ds(c * each, each)
        copies.append(pltpu.make_async_copy(cells.at[here], out.at[here], sems.at[c]))
        copies[c].start()
    for copy in copies:
        copy.wait()


def last(next_, factor, factor_south, factor_north, edges, inside, state, back_a, back_b, coefficients):
    inputs = [(value, True) for value in (next_, factor, factor_south, factor_north, edges, inside, state)]
    inputs += [(back_a, False), (back_b, False)]
    inputs += [(value, True) for value in coefficients]
    return call(
        last_kernel,
        "last",
        inputs,
        [(CELLS, False), ((2, ROWS * W), False)],
        [
            pltpu.VMEM(EDGES, F32),
            pltpu.VMEM(EDGE, F32),
            pltpu.VMEM(EDGE, F32),
            pltpu.VMEM((2, NF + 4, 2 * W), F32),
            pltpu.VMEM((GROUPS, SUB, ROWS * W), F32),
            pltpu.VMEM(CELLS, F32),
            pltpu.SemaphoreType.DMA((CHUNKS,)),
        ],
        out_away=(0,),
    )


def swaps(count):
    near = [(i, i ^ 1) for i in range(count)]
    far = []
    for i in range(1, count - 1, 2):
        far += [(i, i + 1), (i + 1, i)]
    return near, far


def body(
    initial_spectrum,
    wind_forcing,
    sea_mask,
    courant,
    input_rate,
    damping,
    steep_weight,
    obs_owner,
    obs_point,
    obs_value,
    obs_weight,
):
    count = lax.axis_size("geo")
    held = obs_point.shape[0]
    near, far = swaps(count)
    field = initial_spectrum.reshape(CELLS)
    sea = sea_mask.reshape(1, ROWS * W)
    north, south = pack(field, sea)
    from_south = lax.ppermute(north, "geo", [(i, i + 1) for i in range(count - 1)])
    from_north = lax.ppermute(south, "geo", [(i + 1, i) for i in range(count - 1)])
    flow, rate, damp, steep, centre, ahead, back, across, own, slots = local(
        field,
        sea,
        wind_forcing,
        courant,
        input_rate.reshape(1, NB),
        damping.reshape(1, NB),
        steep_weight.reshape(1, NB),
        jnp.asarray(direction_tables()),
        obs_owner,
        obs_point.reshape(1, held),
        obs_value,
        obs_weight.reshape(1, held),
        count,
    )
    arrived = lax.all_to_all(slots, "geo", split_axis=0, concat_axis=0, tiled=True)
    next_, factor, moved, wanted, gain, state = early(
        arrived, flow, own, wind_forcing, sea, rate, damp, steep, centre, ahead, across, count, held
    )
    next_, next_south, next_north, source, edges, state, send_a, send_b = late(
        next_, factor, moved, from_south, from_north, wanted, gain, state,
        (rate, damp, steep, centre, ahead, back, across),
    )
    back_b = lax.ppermute(send_b, "geo", far)
    back_a = lax.ppermute(send_a, "geo", near)
    inside, factor_south, factor_north, state = inner(next_, next_south, next_north, source, state, rate, damp, centre, back, across)
    out, grad = last(
        next_, factor, factor_south, factor_north, edges, inside, state, back_a, back_b,
        (rate, damp, steep, centre, back, across),
    )
    return grad, out.reshape(NB, ROWS * W)


def solution(mesh):
    return jax.shard_map(
        body,
        mesh=mesh,
        in_specs=(
            P(None, ("groups", "geo")),
            P(None, ("groups", "geo")),
            P(("groups", "geo")),
            P(),
            P(),
            P(),
            P(),
            P(("groups", "geo"), None),
            P(("groups", "geo")),
            P(("groups", "geo"), None),
            P(("groups", "geo")),
        ),
        out_specs=(P(None, ("groups", "geo")), P(None, ("groups", "geo"))),
        check_vma=False,
    )
```

```python
import math

import jax
import jax.numpy as jnp
import numpy as np
from jax import lax
from jax.experimental import pallas as pl
from jax.experimental.pallas import tpu as pltpu
from jax.sharding import PartitionSpec as P

ND = 36
NF = 36
NB = 1296
W = 128
ROWS = 4
SUB = 8
GROUP = 72
TILES = GROUP // SUB
GROUPS = NB // GROUP
CHUNKS = 6
F32 = jnp.float32
BF16 = jnp.bfloat16
LIMIT = 14 * 1024 * 1024
LOG2E = math.log2(math.e)
LN2 = math.log(2.0)
LAND = 1.0e5

CELLS = (GROUPS, GROUP, ROWS * W)
EDGE = (GROUPS, GROUP, W)
EDGES = (GROUPS, GROUP, 2 * W)
BINS = (NB, W)
HALF = NB // 2
HALO = (HALF + SUB, 2 * W)
LOAD = 40
STATE = (16, 8 * W)
STEEP0, WIND0, WIND1, SEA, STEEP1, TEND1, GRAD1, TEND0, GRAD0, PASS0 = range(10)

NORTH = (0, 1, 2, 4, 5, 6)
SOUTH = (2, 3, 4, 6, 7, 8)
FROM_WEST = (0, 4, 8)
FROM_EAST = (2, 6)


def direction_tables():
    angle = np.float32(2.0 * math.pi) * np.arange(ND, dtype=np.float32) / np.float32(ND)
    cosine = np.tile(np.cos(angle), 2)[:, None]
    sine = np.tile(np.sin(angle), 2)[:, None]
    lane = np.arange(W)[None, :]
    east = cosine >= 0
    west_ok = (lane > 0).astype(np.float32)
    east_ok = (lane < W - 1).astype(np.float32)
    one = np.ones((1, W), np.float32)
    forward = np.abs(cosine) * np.where(east, west_ok, east_ok)
    backward = np.abs(cosine) * np.where(east, east_ok, west_ok)
    return np.stack(
        [(np.abs(cosine) + np.abs(sine)) * one, np.abs(sine) * one, forward, backward]
    ).astype(np.float32)


def sublane():
    return lax.broadcasted_iota(jnp.int32, (SUB, W), 0)


def north_mask(tile, sub):
    return {2: sub < 2, 4: sub >= 4, 6: sub < 6}.get(tile)


def west_mask(tile, sub):
    return {1: sub < 1, 3: sub >= 3, 5: sub < 5, 7: sub >= 7}.get(tile)


def side(tile, sub, value, reverse):
    west = tile not in (FROM_WEST if reverse else FROM_EAST)
    east = tile not in (FROM_EAST if reverse else FROM_WEST)
    from_west = pltpu.roll(value, 1, 1) if west else None
    from_east = pltpu.roll(value, W - 1, 1) if east else None
    if from_east is None:
        return from_west
    if from_west is None:
        return from_east
    mask = west_mask(tile, sub)
    return jnp.where(mask, from_east, from_west) if reverse else jnp.where(mask, from_west, from_east)


def pick(tile, sub, north, south):
    mask = north_mask(tile, sub)
    if mask is None:
        return north if tile in NORTH else south
    if north is None and south is None:
        return None
    return jnp.where(mask, 0.0 if north is None else north, 0.0 if south is None else south)


def plus(value, other):
    return value if other is None else value + other


def times(factor, value):
    return None if value is None else factor * value


def speed(tile, sub, courant, group):
    first, second = courant[2 * group], courant[2 * group + 1]
    if tile == 4:
        return jnp.where(sub < 4, first, second)
    return jnp.full((SUB, W), first if tile < 4 else second, F32)


def lanes(row):
    return pl.ds(row * W, W)


def column(row):
    return pl.ds((row + 2) * W, W)


def bins(group, tile):
    return pl.ds(pl.multiple_of(group * GROUP + tile * SUB, SUB), SUB)


def total(value):
    return jnp.sum(value, axis=0, keepdims=True)


def full(value):
    return jnp.broadcast_to(value, (SUB, W))


def loop(low, high, by, body, init):
    def passes(index, carry):
        for k in range(by):
            carry = body(low + index * by + k, carry)
        return carry

    return lax.fori_loop(0, (high - low) // by, passes, init)


def whole(memory=pltpu.VMEM):
    return pl.BlockSpec(memory_space=memory)


def call(kernel, name, inputs, outputs, scratch=(), smem=(), away=(), out_away=(), aliases=None, cost=0):
    specs, operands = [], []
    for place, (value, resident) in enumerate(inputs):
        specs.append(whole(pltpu.SMEM if place in smem else pl.ANY if place in away else pltpu.VMEM))
        operands.append(pltpu.with_memory_space_constraint(value, pltpu.VMEM) if resident else value)
    shapes = [pltpu.VMEM(shape, F32) if resident else jax.ShapeDtypeStruct(shape, F32) for shape, resident in outputs]
    return pl.pallas_call(
        kernel,
        in_specs=specs,
        out_specs=[whole(pl.ANY if place in out_away else pltpu.VMEM) for place in range(len(outputs))],
        out_shape=shapes,
        scratch_shapes=list(scratch),
        input_output_aliases=aliases or {},
        compiler_params=pltpu.CompilerParams(vmem_limit_bytes=LIMIT),
        cost_estimate=pl.CostEstimate(flops=cost, bytes_accessed=cost, transcendentals=0) if cost else None,
        name=name,
    )(*operands)


def pack_rows(cell, put, sub, north):
    both = (sub < 2) | ((sub >= 4) & (sub < 6))
    for row in range(2):
        rest = []
        for half in range(2):
            for place, tile in enumerate((0, 1, 5) if north else (3, 7, 8)):
                put(half * 4 + place, row, cell(half, tile, row))
            second, fourth, sixth = [cell(half, tile, row) for tile in (2, 4, 6)]
            if north:
                put(half * 4 + 3, row, jnp.where(sub < 2, second, jnp.where(sub < 4, sixth, fourth)))
                rest.append(sixth)
            else:
                put(half * 4 + 3, row, jnp.where(sub < 4, fourth, second))
                rest.append(jnp.where(sub < 4, second, sixth))
        other = pltpu.roll(rest[1], 2, 0)
        put(8, row, jnp.where(both, rest[0], other) if north else jnp.where(both, other, rest[0]))


def pack_all(cells, base, sea, out, low, high, north):
    sub = sublane()

    def step(pair, carry):
        def cell(half, tile, row):
            return cells[2 * pair + half, pl.ds(tile * SUB, SUB), pl.ds(base + row * W, W)] * sea[row]

        def put(tile, row, value):
            out[pl.ds(pl.multiple_of(pair * GROUP + tile * SUB, SUB), SUB), lanes(row)] = value

        pack_rows(cell, put, sub, north)
        return carry

    loop(low, high, 1, step, 0)


def pack_small(out, wind, sea, base):
    here = pl.ds(base * W, 2 * W)
    out[pl.ds(HALF, SUB), :] = jnp.zeros((SUB, 2 * W), F32)
    out[HALF : HALF + 2, :] = wind[:, here]
    out[HALF + 2 : HALF + 3, :] = sea[:, here].astype(F32)


def far_kernel(field, sea_in, wind_in, out, cells, sea, wind, sems):
    even = lax.rem(lax.axis_index("geo"), 2) == 0
    each = GROUPS // 3
    lane = pl.multiple_of(jnp.where(even, 0, 2 * W), 2 * W)
    small = [
        pltpu.make_async_copy(sea_in, sea, sems.at[3]),
        pltpu.make_async_copy(wind_in, wind, sems.at[4]),
    ]
    copies = []
    for c in range(3):
        here = pl.ds(c * each, each)
        copies.append(pltpu.make_async_copy(field.at[here, :, pl.ds(lane, 2 * W)], cells.at[here], sems.at[c]))
    for copy in small + copies:
        copy.start()
    for copy in small:
        copy.wait()
    for c in range(3):
        copies[c].wait()

        @pl.when(even)
        def _():
            mask = [full(sea[:, lanes(r)].astype(F32)) for r in (0, 1)]
            pack_all(cells, 0, mask, out, c * each // 2, (c + 1) * each // 2, False)

        @pl.when(jnp.logical_not(even))
        def _():
            mask = [full(sea[:, lanes(r)].astype(F32)) for r in (2, 3)]
            pack_all(cells, 0, mask, out, c * each // 2, (c + 1) * each // 2, True)

    @pl.when(even)
    def _():
        pack_small(out, wind, sea, 0)

    @pl.when(jnp.logical_not(even))
    def _():
        pack_small(out, wind, sea, 2)


def far_rows(field, sea, wind):
    return call(
        far_kernel,
        "far",
        [(pltpu.with_memory_space_constraint(value, pltpu.HBM), False) for value in (field, sea, wind)],
        [(HALO, False)],
        [
            pltpu.VMEM((GROUPS, GROUP, 2 * W), F32),
            pltpu.VMEM((1, ROWS * W), jnp.int32),
            pltpu.VMEM((2, ROWS * W), F32),
            pltpu.SemaphoreType.DMA((5,)),
        ],
        away=(0, 1, 2),
    )[0]


def unpack_north(halo, pair, half, row, sub):
    def get(tile):
        return halo[pl.ds(pl.multiple_of(pair * GROUP + tile * SUB, SUB), SUB), lanes(row)]

    mixed, last = get(half * 4 + 3), get(8)
    if half:
        last = pltpu.roll(last, 6, 0)
    return {
        0: get(half * 4),
        1: get(half * 4 + 1),
        2: mixed,
        4: mixed,
        5: get(half * 4 + 2),
        6: jnp.where((sub >= 2) & (sub < 4), mixed, last),
    }


def unpack_south(halo, pair, half, row, sub):
    def get(tile):
        return halo[pl.ds(pl.multiple_of(pair * GROUP + tile * SUB, SUB), SUB), lanes(row)]

    mixed, last = get(half * 4 + 3), get(8)
    if half:
        last = pltpu.roll(last, 6, 0)
    return {
        2: jnp.where(sub < 4, last, mixed),
        3: get(half * 4),
        4: mixed,
        6: last,
        7: get(half * 4 + 1),
        8: get(half * 4 + 2),
    }


def pieces(value):
    high = value.astype(BF16)
    value = value - high.astype(F32)
    middle = value.astype(BF16)
    return high, middle, (value - middle.astype(F32)).astype(BF16)


def spread(inputs, outputs, flat):
    flat[...] = jnp.zeros_like(flat)
    for place, (row, scale) in enumerate(inputs):
        for k, piece in enumerate(pieces(row[...] * scale)):
            flat[3 * place + k : 3 * place + k + 1, 0:NB] = piece.astype(F32)
    count = len(outputs)
    shape = (flat.shape[0], count * W)
    row, lane = lax.broadcasted_iota(jnp.int32, shape, 0), lax.broadcasted_iota(jnp.int32, shape, 1)
    mask = jnp.zeros(shape, F32)
    for place in range(count):
        mine = (row >= 3 * place) & (row < 3 * place + 3) & (lane >= place * W) & (lane < place * W + W)
        mask = jnp.where(mine, 1.0, mask)
    wide = lax.dot_general(
        flat[...].astype(BF16), mask.astype(BF16), (((0,), (0,)), ((), ())), preferred_element_type=F32
    )
    for place, out in enumerate(outputs):
        out[...] = wide[0:NB, place * W : (place + 1) * W]


def layout(rows, ranks):
    lines = -(-max(2, 2 * rows // ranks) // 3)
    return lines, -(-(lines + 2) // SUB) * SUB


def sort(owner, point, value, weight, ranks):
    rows = owner.shape[1]
    lines, block = layout(rows, ranks)
    hits = owner[...] == lax.broadcasted_iota(jnp.int32, (ranks, rows), 0)
    before = lax.broadcasted_iota(jnp.int32, (rows, rows), 0) < lax.broadcasted_iota(jnp.int32, (rows, rows), 1)
    counts = jnp.dot(hits.astype(F32).astype(BF16), before.astype(F32).astype(BF16), preferred_element_type=F32)
    order = jnp.sum(jnp.where(hits, counts, 0.0), axis=0, keepdims=True).astype(jnp.int32)
    line = (order * 171) >> 9
    third = order - 3 * line
    target = owner[...] * block + line
    spots = lax.broadcasted_iota(jnp.int32, (ranks * block, rows), 0)
    places = [((target == spots) & (third == k)).astype(F32).astype(BF16) for k in range(3)]
    load = jnp.concatenate(
        [
            value[...] * weight[...],
            weight[...],
            point[...].astype(F32),
            jnp.zeros((LOAD - NF - 2, rows), F32),
        ],
        axis=0,
    )
    loads = [
        jnp.concatenate(
            [jnp.zeros((LOAD * k, rows), F32)] * (k > 0) + [load, jnp.zeros((W - LOAD * (k + 1), rows), F32)], axis=0
        )
        for k in range(3)
    ]
    places = jnp.concatenate(places, axis=1)
    result = 0.0
    for piece in zip(*[pieces(part) for part in loads]):
        result = result + lax.dot_general(
            places, jnp.concatenate(piece, axis=1), (((1,), (1,)), ((), ())), preferred_element_type=F32
        )
    return result


def local_kernel(
    field, sea_in, wind, courant, rate_in, damp_in, steep_in, table, owner, point, value, weight,
    flow, rate, damp, steep, centre, ahead, back, across, own, slots, near_out,
    cells, flat, sems, *, ranks,
):
    sub = sublane()
    each = GROUPS // CHUNKS
    copies = [
        pltpu.make_async_copy(field.at[pl.ds(c * each, each)], cells.at[pl.ds(c * each, each)], sems.at[c])
        for c in range(CHUNKS)
    ]
    for copy in copies:
        copy.start()
    spread(((rate_in, LOG2E), (damp_in, LOG2E), (steep_in, 1.0)), (rate, damp, steep), flat)
    slots[...] = sort(owner, point, value, weight, ranks)
    sea = [full(sea_in[:, lanes(r)].astype(F32)) for r in range(ROWS)]
    zero = jnp.zeros((SUB, W), F32)

    def step(group, sums):
        sums = list(sums)
        for tile in range(TILES):
            rows, spot = pl.ds(tile * SUB, SUB), bins(group, tile)
            pace = speed(tile, sub, courant, group)
            middle = 1.0 - pace * table[0, rows, :]
            over = pace * table[1, rows, :]
            along = pace * table[2, rows, :]
            centre[spot, :] = middle
            across[spot, :] = over
            ahead[spot, :] = along
            back[spot, :] = pace * table[3, rows, :]
            heavy = steep[spot, :]
            cell = {r: cells[group, rows, lanes(r)] * sea[r] for r in range(ROWS)}
            for r in range(ROWS):
                moved = middle * cell[r] + along * side(tile, sub, cell[r], False)
                moved = plus(moved, times(over, pick(tile, sub, cell.get(r - 1), cell.get(r + 1))))
                flow[group, rows, lanes(r)] = moved
                sums[r] = sums[r] + heavy * moved
            gone = heavy * over
            if tile in NORTH:
                sums[ROWS] = sums[ROWS] + pick(tile, sub, gone * cell[ROWS - 1], None)
            if tile in SOUTH:
                sums[ROWS + 1] = sums[ROWS + 1] + pick(tile, sub, None, gone * cell[0])
        return tuple(sums)

    sums = (zero,) * (ROWS + 2)
    for c in range(CHUNKS):
        copies[c].wait()
        sums = loop(c * each, (c + 1) * each, 3, step, sums)
    sums = [total(value) for value in sums]
    own[...] = jnp.zeros_like(own)
    for r in range(ROWS):
        own[0:1, lanes(r)] = sums[r] * sea[r][0:1, :]
    own[1:2, lanes(ROWS - 1)] = sums[ROWS]
    own[1:2, lanes(0)] = sums[ROWS + 1]

    _, block = layout(owner.shape[1], ranks)
    me = lax.axis_index("geo")

    def hand(row, dest):
        last = pl.ds(pl.multiple_of(dest * block + block - SUB, SUB), SUB)
        values = jnp.where(sub == SUB - 2, own[0:1, lanes(row)], slots[last, :])
        slots[last, :] = jnp.where(sub == SUB - 1, own[1:2, lanes(row)], values)

    @pl.when(me < ranks - 1)
    def _():
        hand(ROWS - 1, me + 1)

    @pl.when(me > 0)
    def _():
        hand(0, me - 1)

    even = lax.rem(me, 2) == 0

    @pl.when(even)
    def _():
        pack_all(cells, 2 * W, sea[2:4], near_out, 0, GROUPS // 2, True)
        pack_small(near_out, wind, sea_in, 2)

    @pl.when(jnp.logical_not(even))
    def _():
        pack_all(cells, 0, sea[0:2], near_out, 0, GROUPS // 2, False)
        pack_small(near_out, wind, sea_in, 0)


def local(field, sea, wind, courant, rate, damp, steep, table, owner, point, value, weight, ranks):
    rows = owner.shape[1]
    _, block = layout(rows, ranks)

    def kernel(*refs):
        local_kernel(*refs, ranks=ranks)

    args = (
        pltpu.with_memory_space_constraint(field, pltpu.HBM), sea, wind, courant, rate, damp, steep, table,
        owner, point, value, weight,
    )
    return call(
        kernel,
        "local",
        [(arg, False) for arg in args],
        [(CELLS, True)] + [(BINS, True)] * 7 + [((SUB, ROWS * W), True), ((ranks * block, W), False), (HALO, False)],
        [
            pltpu.VMEM(CELLS, F32),
            pltpu.VMEM((16, 11 * W), F32),
            pltpu.SemaphoreType.DMA((CHUNKS,)),
        ],
        smem=(3,),
        away=(0,),
    )


def place(arrived, ranks, rows, wanted, gain):
    lines, block = layout(rows, ranks)
    size = ranks * block
    shape = (size, W)
    lane = lax.broadcasted_iota(jnp.int32, shape, 1)
    held = lax.rem(lax.broadcasted_iota(jnp.int32, shape, 0), block) < lines
    load = jnp.where(held, arrived[...], 0.0)
    spots = lax.broadcasted_iota(jnp.int32, (size, ROWS * W), 1)
    sums = 0.0
    for k in range(3):
        mine = pltpu.roll(load, W - LOAD * k, 1) if k else load
        point = mine[:, NF + 1 : NF + 2].astype(jnp.int32)
        hits = (point == spots).astype(F32).astype(BF16)
        high, middle, low = [piece.astype(F32) for piece in pieces(jnp.where(lane < LOAD, mine, 0.0))]
        mine = high + pltpu.roll(middle, LOAD, 1) + pltpu.roll(low, 2 * LOAD, 1)
        sums = sums + lax.dot_general(
            mine.astype(BF16), hits, (((0,), (0,)), ((), ())), preferred_element_type=F32
        )
    sums = sums[0:LOAD] + sums[LOAD : 2 * LOAD] + sums[2 * LOAD : 3 * LOAD]
    for f in range(NF):
        rows_of = slice(4 * (f % 2), 4 * (f % 2) + 4)
        wanted[f // 2, rows_of, :] = jnp.broadcast_to(sums[f : f + 1, :] * (1.0 / ND), (4, ROWS * W))
    gain[...] = jnp.broadcast_to(sums[NF : NF + 1, :] * (1.0 / (ND * ND)), gain.shape)


def early_kernel(
    arrived, flow, own, wind, sea_in, rate, damp, steep, centre, ahead, across, next_, factor, moved, wanted, gain, state,
    *, ranks, rows,
):
    sub = sublane()
    place(arrived, ranks, rows, wanted, gain)
    lines, block = layout(rows, ranks)
    me = lax.axis_index("geo")

    def aux(source, there):
        source = jnp.clip(source, 0, ranks - 1)
        last = pl.ds(pl.multiple_of(source * block + block - SUB, SUB), SUB)
        return jnp.where(there, arrived[last, :], 0.0)

    south, north = aux(me - 1, me > 0), aux(me + 1, me < ranks - 1)
    state[...] = jnp.zeros_like(state)
    here = pl.ds(2 * W, ROWS * W)
    state[WIND0 : WIND0 + 1, here] = wind[0:1, :]
    state[WIND1 : WIND1 + 1, here] = wind[1:2, :]
    state[SEA : SEA + 1, here] = sea_in[...].astype(F32)
    steeps = {r: own[0:1, lanes(r)] for r in range(ROWS)}
    steeps[0] = steeps[0] + south[7:8, :]
    steeps[3] = steeps[3] + north[7:8, :]
    for r, value in steeps.items():
        state[STEEP0 : STEEP0 + 1, column(r)] = jnp.where(state[SEA : SEA + 1, column(r)] > 0.5, value, LAND)
    state[STEEP0 : STEEP0 + 1, column(-1)] = south[6:7, :] + own[1:2, lanes(0)]
    state[STEEP0 : STEEP0 + 1, column(4)] = north[6:7, :] + own[1:2, lanes(3)]
    steep0 = [full(state[STEEP0 : STEEP0 + 1, column(r)]) for r in range(ROWS)]
    wind0 = [full(state[WIND0 : WIND0 + 1, column(r)]) for r in range(ROWS)]

    def step(group, sums):
        sums = list(sums)
        for tile in range(TILES):
            rows, spot = pl.ds(tile * SUB, SUB), bins(group, tile)
            grow, fade, heavy = rate[spot, :], damp[spot, :], steep[spot, :]
            middle, along, over = centre[spot, :], ahead[spot, :], across[spot, :]
            cell = {}
            for r in range(ROWS):
                gained = jnp.exp2(grow * wind0[r] - fade * steep0[r])
                factor[group, rows, lanes(r)] = gained
                cell[r] = flow[group, rows, lanes(r)] * gained
                next_[group, rows, lanes(r)] = cell[r]
            for r in range(ROWS):
                value = middle * cell[r] + along * side(tile, sub, cell[r], False)
                value = plus(value, times(over, pick(tile, sub, cell.get(r - 1), cell.get(r + 1))))
                moved[group, rows, lanes(r)] = value
                sums[r] = sums[r] + heavy * value
        return tuple(sums)

    sums = loop(0, GROUPS, 3, step, (jnp.zeros((SUB, W), F32),) * ROWS)
    for r in range(ROWS):
        state[STEEP1 : STEEP1 + 1, column(r)] = total(sums[r])


def early(arrived, flow, own, wind, sea, rate, damp, steep, centre, ahead, across, ranks, rows):
    def kernel(*refs):
        early_kernel(*refs, ranks=ranks, rows=rows)

    inputs = [(arrived, False), (flow, True), (own, True), (wind, False), (sea, False)]
    inputs += [(value, True) for value in (rate, damp, steep, centre, ahead, across)]
    return call(
        kernel,
        "early",
        inputs,
        [(CELLS, True)] * 3 + [((GROUPS, SUB, ROWS * W), True), ((SUB, ROWS * W), True), (STATE, True)],
    )


def split_lam(lam, group, tile, where):
    if tile < 4:
        return lam[group, 0:1, where]
    if tile > 4:
        return lam[group, 4:5, where]
    return lam[group, :, where]


def late_kernel(
    next_in, factor, moved, from_far, from_near, wanted, gain, state_in, rate, damp, steep, centre, ahead, back, across,
    next_, next_south, next_north, source, edges, state, send_a, send_b,
    fixed, growth, lam, halo_south, halo_north, sems,
):
    sub = sublane()
    zero = jnp.zeros((SUB, W), F32)
    even = lax.rem(lax.axis_index("geo"), 2) == 0
    each = HALF // 3
    parts = [pl.ds(HALF, SUB)] + [pl.ds(c * each, each) for c in range(3)]

    def bring(first, second):
        copies = []
        for c, here in enumerate(parts):
            copies.append(pltpu.make_async_copy(first.at[here], halo_south.at[here], sems.at[2 * c]))
            copies.append(pltpu.make_async_copy(second.at[here], halo_north.at[here], sems.at[2 * c + 1]))
        return copies

    @pl.when(even)
    def _():
        for copy in bring(from_far, from_near):
            copy.start()

    @pl.when(jnp.logical_not(even))
    def _():
        for copy in bring(from_near, from_far):
            copy.start()

    copies = bring(from_far, from_near)
    copies[0].wait()
    copies[1].wait()
    state[...] = state_in[...]
    for halo, rows in ((halo_south, (-2, -1)), (halo_north, (4, 5))):
        here = pl.ds((rows[0] + 2) * W, 2 * W)
        for place, name in enumerate((WIND0, WIND1, SEA)):
            state[name : name + 1, here] = halo[HALF + place : HALF + place + 1, :]
    for r in (-1, 4):
        known = state[SEA : SEA + 1, column(r)] > 0.5
        state[STEEP0 : STEEP0 + 1, column(r)] = jnp.where(known, state[STEEP0 : STEEP0 + 1, column(r)], LAND)

    def held(place, r):
        return full(state[place : place + 1, column(r)])

    steep0 = {r: held(STEEP0, r) for r in (-1, 4)}
    wind0 = {r: held(WIND0, r) for r in (-1, 4)}

    def first(pair, sums):
        sums = list(sums)
        for half in range(2):
            group = 2 * pair + half
            ghosts = {
                -2: unpack_north(halo_south, pair, half, 0, sub),
                -1: unpack_north(halo_south, pair, half, 1, sub),
                4: unpack_south(halo_north, pair, half, 0, sub),
                5: unpack_south(halo_north, pair, half, 1, sub),
            }
            for tile in range(TILES):
                rows, spot = pl.ds(tile * SUB, SUB), bins(group, tile)
                grow, fade, heavy = rate[spot, :], damp[spot, :], steep[spot, :]
                middle, along, over = centre[spot, :], ahead[spot, :], across[spot, :]
                beyond = {}
                changes = {}
                for near, far, mine, second, tiles, north in ((-1, -2, 0, 1, NORTH, True), (4, 5, 3, 2, SOUTH, False)):
                    if tile not in tiles:
                        continue

                    def only(value):
                        return pick(tile, sub, value, None) if north else pick(tile, sub, None, value)

                    cell = ghosts[near][tile]
                    gained = jnp.exp2(grow * wind0[near] - fade * steep0[near])
                    value = middle * cell + along * side(tile, sub, cell, False) + over * ghosts[far][tile]
                    value = value * gained
                    (next_south if north else next_north)[group, rows, :] = value
                    extra = only(over * cell) * factor[group, rows, lanes(mine)]
                    next_[group, rows, lanes(mine)] = next_in[group, rows, lanes(mine)] + extra
                    change = middle * extra + along * side(tile, sub, extra, False) + only(over * value)
                    changes[mine] = plus(change, changes.get(mine))
                    changes[second] = plus(over * extra, changes.get(second))
                for r, change in changes.items():
                    sums[r] = sums[r] + heavy * change
                    fixed[group, rows, lanes(r)] = moved[group, rows, lanes(r)] + change
                for r in range(ROWS):
                    if r not in changes:
                        fixed[group, rows, lanes(r)] = moved[group, rows, lanes(r)]
        return tuple(sums)

    sums = (zero,) * ROWS
    for c in range(3):
        copies[2 * c + 2].wait()
        copies[2 * c + 3].wait()
        sums = loop(3 * c, 3 * c + 3, 3, first, sums)
    for r in range(ROWS):
        value = state[STEEP1 : STEEP1 + 1, column(r)] + total(sums[r])
        state[STEEP1 : STEEP1 + 1, column(r)] = jnp.where(state[SEA : SEA + 1, column(r)] > 0.5, value, LAND)
    steep1 = [held(STEEP1, r) for r in range(ROWS)]
    wind1 = [held(WIND1, r) for r in range(ROWS)]
    gains = [gain[:, lanes(r)] for r in range(ROWS)]

    def second(group, sums):
        sums = list(sums)
        means = [[None, None] for _ in range(ROWS)]
        ups = [[None, None] for _ in range(ROWS)]
        downs = [[None, None] for _ in range(ROWS)]
        for tile in range(TILES):
            rows, spot = pl.ds(tile * SUB, SUB), bins(group, tile)
            grow, fade = rate[spot, :], damp[spot, :]
            for r in range(ROWS):
                value = jnp.exp2(grow * wind1[r] - fade * steep1[r])
                growth[group, rows, lanes(r)] = value
                value = value * fixed[group, rows, lanes(r)]
                for parts, term in ((means, value), (ups, grow * value), (downs, fade * value)):
                    if tile == 4:
                        parts[r][0] = plus(jnp.where(sub < 4, term, 0.0), parts[r][0])
                        parts[r][1] = jnp.where(sub < 4, 0.0, term)
                    else:
                        f = 0 if tile < 4 else 1
                        parts[r][f] = plus(term, parts[r][f])
        for r in range(ROWS):
            one, two = means[r]
            one = one + pltpu.roll(one, 4, 0)
            two = two + pltpu.roll(two, 4, 0)
            both = jnp.where(sub < 4, one, two)
            both = both + jnp.where((sub & 2) == 0, pltpu.roll(both, 6, 0), pltpu.roll(both, 2, 0))
            both = both + jnp.where((sub & 1) == 0, pltpu.roll(both, 7, 0), pltpu.roll(both, 1, 0))
            value = gains[r] * both - wanted[group, :, lanes(r)]
            lam[group, :, lanes(r)] = value
            up, down = value[0:1, :], value[4:5, :]
            sums[r] = sums[r] + (up * ups[r][0] + down * ups[r][1])
            sums[ROWS + r] = sums[ROWS + r] + (up * downs[r][0] + down * downs[r][1])
        return tuple(sums)

    sums = loop(0, GROUPS, 1, second, (zero,) * (2 * ROWS))
    for r in range(ROWS):
        state[GRAD1 : GRAD1 + 1, column(r)] = total(sums[r]) * LN2
        state[TEND1 : TEND1 + 1, column(r)] = total(sums[ROWS + r]) * (-LN2)
    tend1 = [held(TEND1, r) for r in range(ROWS)]

    def third(group, sums):
        sums = list(sums)
        for tile in range(TILES):
            rows, spot = pl.ds(tile * SUB, SUB), bins(group, tile)
            grow, fade, heavy = rate[spot, :], damp[spot, :], steep[spot, :]
            middle, along, over = centre[spot, :], back[spot, :], across[spot, :]
            cell = {}
            for r in range(ROWS):
                cell[r] = split_lam(lam, group, tile, lanes(r)) * growth[group, rows, lanes(r)] + heavy * tend1[r]
                source[group, rows, lanes(r)] = cell[r]
            for place, r in enumerate((0, ROWS - 1)):
                value = middle * cell[r] + along * side(tile, sub, cell[r], True)
                value = plus(value, times(over, pick(tile, sub, cell.get(r + 1), cell.get(r - 1))))
                edges[group, rows, lanes(place)] = value
                value = value * next_[group, rows, lanes(r)]
                sums[place] = sums[place] + grow * value
                sums[2 + place] = sums[2 + place] + fade * value
        return tuple(sums)

    sums = loop(0, GROUPS, 3, third, (zero,) * 4)
    for place, r in enumerate((0, ROWS - 1)):
        state[GRAD0 : GRAD0 + 1, column(r)] = total(sums[place]) * LN2
        state[TEND0 : TEND0 + 1, column(r)] = total(sums[2 + place]) * (-LN2)

    def fill(ref, base):
        for f in range(NF):
            ref[f : f + 1, :] = lam[f // 2, 4 * (f % 2) : 4 * (f % 2) + 1, pl.ds(base * W, 2 * W)]
        here = pl.ds((base + 2) * W, 2 * W)
        for place, name in enumerate((STEEP1, TEND1, TEND0, TEND0)):
            ref[NF + place : NF + place + 1, :] = state[name : name + 1, here]

    @pl.when(even)
    def _():
        fill(send_a, 2)
        fill(send_b, 0)

    @pl.when(jnp.logical_not(even))
    def _():
        fill(send_a, 0)
        fill(send_b, 2)


def late(next_, factor, moved, from_far, from_near, wanted, gain, state, coefficients):
    inputs = [(next_, True), (factor, True), (moved, True), (from_far, False), (from_near, False)]
    inputs += [(value, True) for value in (wanted, gain, state) + coefficients]
    return call(
        late_kernel,
        "late",
        inputs,
        [(CELLS, True)] + [(EDGE, True)] * 2 + [(CELLS, True), (EDGES, True), (STATE, True)]
        + [((NF + 4, 2 * W), False)] * 2,
        [
            pltpu.VMEM(CELLS, F32),
            pltpu.VMEM(CELLS, F32),
            pltpu.VMEM((GROUPS, SUB, ROWS * W), F32),
            pltpu.VMEM(HALO, F32),
            pltpu.VMEM(HALO, F32),
            pltpu.SemaphoreType.DMA((8,)),
        ],
        away=(3, 4),
        aliases={0: 0},
    )


def inner_kernel(
    next_, next_south, next_north, source, state_in, rate, damp, centre, back, across,
    inside, factor_south, factor_north, state,
):
    sub = sublane()
    zero = jnp.zeros((SUB, W), F32)
    state[...] = state_in[...]
    wind0 = {r: full(state[WIND0 : WIND0 + 1, column(r)]) for r in (-1, 4)}
    steep0 = {r: full(state[STEEP0 : STEEP0 + 1, column(r)]) for r in (-1, 4)}

    def step(group, sums):
        sums = list(sums)
        for tile in range(TILES):
            rows, spot = pl.ds(tile * SUB, SUB), bins(group, tile)
            grow, fade = rate[spot, :], damp[spot, :]
            if tile in SOUTH:
                factor_south[group, rows, :] = jnp.exp2(grow * wind0[-1] - fade * steep0[-1])
            if tile in NORTH:
                factor_north[group, rows, :] = jnp.exp2(grow * wind0[4] - fade * steep0[4])
            middle, along, over = centre[spot, :], back[spot, :], across[spot, :]
            cell = {r: source[group, rows, lanes(r)] for r in range(ROWS)}
            for place, r in enumerate((1, 2)):
                value = middle * cell[r] + along * side(tile, sub, cell[r], True)
                value = value + over * pick(tile, sub, cell[r + 1], cell[r - 1])
                inside[group, rows, lanes(place)] = value
                value = value * next_[group, rows, lanes(r)]
                sums[place] = sums[place] + grow * value
                sums[2 + place] = sums[2 + place] + fade * value
            gone = fade * over
            if tile in NORTH:
                value = pick(tile, sub, cell[0] * next_south[group, rows, :], None)
                sums[4] = sums[4] + gone * value
            if tile in SOUTH:
                value = pick(tile, sub, None, cell[3] * next_north[group, rows, :])
                sums[5] = sums[5] + gone * value
        return tuple(sums)

    sums = loop(0, GROUPS, 3, step, (zero,) * 6)
    for place, r in enumerate((1, 2)):
        state[GRAD0 : GRAD0 + 1, column(r)] = total(sums[place]) * LN2
        state[TEND0 : TEND0 + 1, column(r)] = total(sums[2 + place]) * (-LN2)
    state[TEND0 : TEND0 + 1, column(-1)] = total(sums[4]) * (-LN2)
    state[TEND0 : TEND0 + 1, column(4)] = total(sums[5]) * (-LN2)


def inner(*args):
    return call(
        inner_kernel,
        "inner",
        [(arg, True) for arg in args],
        [(EDGES, True), (EDGE, True), (EDGE, True), (STATE, True)],
        cost=1 << 22,
    )


def last_kernel(
    next_, factor, factor_south, factor_north, edges, inside, state, back_a, back_b, rate, damp, steep, centre, back, across,
    out, grad, rims, low, high, ghosts, lam, cells, sems,
):
    sub = sublane()
    zero = jnp.zeros((SUB, W), F32)
    even = lax.rem(lax.axis_index("geo"), 2) == 0
    ghosts[0] = jnp.where(even, back_b[...], back_a[...])
    ghosts[1] = jnp.where(even, back_a[...], back_b[...])
    for group in range(GROUPS):
        for where in range(2):
            for row in range(2):
                one = ghosts[where, 2 * group : 2 * group + 1, lanes(row)]
                two = ghosts[where, 2 * group + 1 : 2 * group + 2, lanes(row)]
                lam[group, :, lanes(2 * where + row)] = jnp.where(sub < 4, one, two)
    sea = {r: full(state[SEA : SEA + 1, column(r)]) for r in range(-2, 6)}
    wind1, steep1, tend1 = {}, {}, {}
    for r in (-2, -1, 4, 5):
        where, here = (0, lanes(r + 2)) if r < 0 else (1, lanes(r - 4))
        wind1[r] = full(state[WIND1 : WIND1 + 1, column(r)])
        value = ghosts[where, NF : NF + 1, here]
        steep1[r] = full(jnp.where(sea[r][0:1, :] > 0.5, value, LAND))
        tend1[r] = full(ghosts[where, NF + 1 : NF + 2, here])

    def first(group, sums):
        sums = list(sums)
        for tile in range(TILES):
            rows, spot = pl.ds(tile * SUB, SUB), bins(group, tile)
            grow, fade, heavy = rate[spot, :], damp[spot, :], steep[spot, :]
            middle, along, over = centre[spot, :], back[spot, :], across[spot, :]

            def ghost(r):
                value = split_lam(lam, group, tile, lanes(r + 2 if r < 0 else r - 2))
                return value * jnp.exp2(grow * wind1[r] - fade * steep1[r]) + heavy * tend1[r]

            for near, far, mine, place, tiles in ((-1, -2, 0, 0, SOUTH), (4, 5, 3, 1, NORTH)):
                if tile not in tiles:
                    continue
                cell = ghost(near)
                value = middle * cell + along * side(tile, sub, cell, True) + over * ghost(far)
                (low if place == 0 else high)[group, rows, :] = value
                value = over * cell
                value = pick(tile, sub, None, value) if place == 0 else pick(tile, sub, value, None)
                rims[group, rows, lanes(place)] = edges[group, rows, lanes(place)] + value
                value = value * next_[group, rows, lanes(mine)]
                sums[place] = sums[place] + grow * value
                sums[2 + place] = sums[2 + place] + fade * value
        return tuple(sums)

    sums = loop(0, GROUPS, 3, first, (zero,) * 4)
    sums = [total(value) * LN2 for value in sums]
    tend0 = {r: state[TEND0 : TEND0 + 1, column(r)] for r in range(-1, 5)}
    grad0 = [state[GRAD0 : GRAD0 + 1, column(r)] for r in range(ROWS)]
    tend0[0], grad0[0] = tend0[0] - sums[2], grad0[0] + sums[0]
    tend0[3], grad0[3] = tend0[3] - sums[3], grad0[3] + sums[1]
    tend0[-1] = tend0[-1] + ghosts[0, NF + 2 : NF + 3, lanes(1)]
    tend0[4] = tend0[4] + ghosts[1, NF + 2 : NF + 3, lanes(0)]
    for r in range(ROWS):
        grad[0:1, lanes(r)] = grad0[r]
        grad[1:2, lanes(r)] = state[GRAD1 : GRAD1 + 1, column(r)]
    tend0 = {r: full(value) for r, value in tend0.items()}

    def second(group, carry):
        for tile in range(TILES):
            rows, spot = pl.ds(tile * SUB, SUB), bins(group, tile)
            heavy = steep[spot, :]
            middle, along, over = centre[spot, :], back[spot, :], across[spot, :]
            cell = {}
            for r in range(-1, 5):
                if r == -1:
                    if tile not in SOUTH:
                        continue
                    value = low[group, rows, :] * factor_south[group, rows, :]
                elif r == 4:
                    if tile not in NORTH:
                        continue
                    value = high[group, rows, :] * factor_north[group, rows, :]
                else:
                    if r == 0:
                        value = (rims if tile in SOUTH else edges)[group, rows, lanes(0)]
                    elif r == 3:
                        value = (rims if tile in NORTH else edges)[group, rows, lanes(1)]
                    else:
                        value = inside[group, rows, lanes(r - 1)]
                    value = value * factor[group, rows, lanes(r)]
                cell[r] = value + heavy * tend0[r]
            for r in range(ROWS):
                value = middle * cell[r] + along * side(tile, sub, cell[r], True)
                value = value + over * pick(tile, sub, cell.get(r + 1), cell.get(r - 1))
                cells[group, rows, lanes(r)] = sea[r] * value
        return carry

    each = GROUPS // CHUNKS
    copies = []
    for c in range(CHUNKS):
        loop(c * each, (c + 1) * each, 3, second, 0)
        here = pl.ds(c * each, each)
        copies.append(pltpu.make_async_copy(cells.at[here], out.at[here], sems.at[c]))
        copies[c].start()
    for copy in copies:
        copy.wait()


def last(next_, factor, factor_south, factor_north, edges, inside, state, back_a, back_b, coefficients):
    inputs = [(value, True) for value in (next_, factor, factor_south, factor_north, edges, inside, state)]
    inputs += [(back_a, False), (back_b, False)]
    inputs += [(value, True) for value in coefficients]
    return call(
        last_kernel,
        "last",
        inputs,
        [(CELLS, False), ((2, ROWS * W), False)],
        [
            pltpu.VMEM(EDGES, F32),
            pltpu.VMEM(EDGE, F32),
            pltpu.VMEM(EDGE, F32),
            pltpu.VMEM((2, NF + 4, 2 * W), F32),
            pltpu.VMEM((GROUPS, SUB, ROWS * W), F32),
            pltpu.VMEM(CELLS, F32),
            pltpu.SemaphoreType.DMA((CHUNKS,)),
        ],
        out_away=(0,),
    )


def swaps(count):
    near = [(i, i ^ 1) for i in range(count)]
    far = []
    for i in range(1, count - 1, 2):
        far += [(i, i + 1), (i + 1, i)]
    return near, far


def body(
    initial_spectrum,
    wind_forcing,
    sea_mask,
    courant,
    input_rate,
    damping,
    steep_weight,
    obs_owner,
    obs_point,
    obs_value,
    obs_weight,
):
    count = lax.axis_size("geo")
    held = obs_point.shape[0]
    near, far = swaps(count)
    field = initial_spectrum.reshape(CELLS)
    sea = sea_mask.reshape(1, ROWS * W)
    from_far = lax.ppermute(far_rows(field, sea, wind_forcing), "geo", far)
    flow, rate, damp, steep, centre, ahead, back, across, own, slots, rows = local(
        field,
        sea,
        wind_forcing,
        courant,
        input_rate.reshape(1, NB),
        damping.reshape(1, NB),
        steep_weight.reshape(1, NB),
        jnp.asarray(direction_tables()),
        obs_owner.reshape(1, held),
        obs_point.reshape(1, held),
        obs_value.T,
        obs_weight.reshape(1, held),
        count,
    )
    from_near = lax.ppermute(rows, "geo", near)
    arrived = lax.all_to_all(slots, "geo", split_axis=0, concat_axis=0, tiled=True)
    next_, factor, moved, wanted, gain, state = early(
        arrived, flow, own, wind_forcing, sea, rate, damp, steep, centre, ahead, across, count, held
    )
    next_, next_south, next_north, source, edges, state, send_a, send_b = late(
        next_, factor, moved, from_far, from_near, wanted, gain, state,
        (rate, damp, steep, centre, ahead, back, across),
    )
    back_b = lax.ppermute(send_b, "geo", far)
    back_a = lax.ppermute(send_a, "geo", near)
    inside, factor_south, factor_north, state = inner(next_, next_south, next_north, source, state, rate, damp, centre, back, across)
    out, grad = last(
        next_, factor, factor_south, factor_north, edges, inside, state, back_a, back_b,
        (rate, damp, steep, centre, back, across),
    )
    return grad, out.reshape(NB, ROWS * W)


def solution(mesh):
    return jax.shard_map(
        body,
        mesh=mesh,
        in_specs=(
            P(None, ("groups", "geo")),
            P(None, ("groups", "geo")),
            P(("groups", "geo")),
            P(),
            P(),
            P(),
            P(),
            P(("groups", "geo"), None),
            P(("groups", "geo")),
            P(("groups", "geo"), None),
            P(("groups", "geo")),
        ),
        out_specs=(P(None, ("groups", "geo")), P(None, ("groups", "geo"))),
        check_vma=False,
    )
```

```python
import math

import jax
import jax.numpy as jnp
import numpy as np
from jax import lax
from jax.experimental import pallas as pl
from jax.experimental.pallas import tpu as pltpu
from jax.sharding import PartitionSpec as P

ND = 36
NF = 36
NB = 1296
W = 128
ROWS = 4
SUB = 8
GROUP = 72
TILES = GROUP // SUB
GROUPS = NB // GROUP
CHUNKS = 6
F32 = jnp.float32
BF16 = jnp.bfloat16
LIMIT = 14 * 1024 * 1024
LOG2E = math.log2(math.e)
LN2 = math.log(2.0)
LAND = 1.0e5

CELLS = (GROUPS, GROUP, ROWS * W)
EDGE = (GROUPS, GROUP, W)
EDGES = (GROUPS, GROUP, 2 * W)
BINS = (NB, W)
HALF = NB // 2
HALO = (HALF + SUB, 2 * W)
LOAD = 40
STATE = (16, 8 * W)
STEEP0, WIND0, WIND1, SEA, STEEP1, TEND1, GRAD1, TEND0, GRAD0, PASS0 = range(10)

NORTH = (0, 1, 2, 4, 5, 6)
SOUTH = (2, 3, 4, 6, 7, 8)
FROM_WEST = (0, 4, 8)
FROM_EAST = (2, 6)


def direction_tables():
    angle = np.float32(2.0 * math.pi) * np.arange(ND, dtype=np.float32) / np.float32(ND)
    cosine = np.tile(np.cos(angle), 2)[:, None]
    sine = np.tile(np.sin(angle), 2)[:, None]
    lane = np.arange(W)[None, :]
    east = cosine >= 0
    west_ok = (lane > 0).astype(np.float32)
    east_ok = (lane < W - 1).astype(np.float32)
    one = np.ones((1, W), np.float32)
    forward = np.abs(cosine) * np.where(east, west_ok, east_ok)
    backward = np.abs(cosine) * np.where(east, east_ok, west_ok)
    return np.stack(
        [(np.abs(cosine) + np.abs(sine)) * one, np.abs(sine) * one, forward, backward]
    ).astype(np.float32)


def sublane():
    return lax.broadcasted_iota(jnp.int32, (SUB, W), 0)


def north_mask(tile, sub):
    return {2: sub < 2, 4: sub >= 4, 6: sub < 6}.get(tile)


def west_mask(tile, sub):
    return {1: sub < 1, 3: sub >= 3, 5: sub < 5, 7: sub >= 7}.get(tile)


def side(tile, sub, value, reverse):
    west = tile not in (FROM_WEST if reverse else FROM_EAST)
    east = tile not in (FROM_EAST if reverse else FROM_WEST)
    from_west = pltpu.roll(value, 1, 1) if west else None
    from_east = pltpu.roll(value, W - 1, 1) if east else None
    if from_east is None:
        return from_west
    if from_west is None:
        return from_east
    mask = west_mask(tile, sub)
    return jnp.where(mask, from_east, from_west) if reverse else jnp.where(mask, from_west, from_east)


def pick(tile, sub, north, south):
    mask = north_mask(tile, sub)
    if mask is None:
        return north if tile in NORTH else south
    if north is None and south is None:
        return None
    return jnp.where(mask, 0.0 if north is None else north, 0.0 if south is None else south)


def plus(value, other):
    return value if other is None else value + other


def times(factor, value):
    return None if value is None else factor * value


def speed(tile, sub, courant, group):
    first, second = courant[2 * group], courant[2 * group + 1]
    if tile == 4:
        return jnp.where(sub < 4, first, second)
    return jnp.full((SUB, W), first if tile < 4 else second, F32)


def lanes(row):
    return pl.ds(row * W, W)


def column(row):
    return pl.ds((row + 2) * W, W)


def bins(group, tile):
    return pl.ds(pl.multiple_of(group * GROUP + tile * SUB, SUB), SUB)


def total(value):
    return jnp.sum(value, axis=0, keepdims=True)


def full(value):
    return jnp.broadcast_to(value, (SUB, W))


def loop(low, high, by, body, init):
    def passes(index, carry):
        for k in range(by):
            carry = body(low + index * by + k, carry)
        return carry

    return lax.fori_loop(0, (high - low) // by, passes, init)


def whole(memory=pltpu.VMEM):
    return pl.BlockSpec(memory_space=memory)


def call(kernel, name, inputs, outputs, scratch=(), smem=(), away=(), out_away=(), aliases=None, cost=0):
    specs, operands = [], []
    for place, (value, resident) in enumerate(inputs):
        specs.append(whole(pltpu.SMEM if place in smem else pl.ANY if place in away else pltpu.VMEM))
        operands.append(pltpu.with_memory_space_constraint(value, pltpu.VMEM) if resident else value)
    shapes = [pltpu.VMEM(shape, F32) if resident else jax.ShapeDtypeStruct(shape, F32) for shape, resident in outputs]
    return pl.pallas_call(
        kernel,
        in_specs=specs,
        out_specs=[whole(pl.ANY if place in out_away else pltpu.VMEM) for place in range(len(outputs))],
        out_shape=shapes,
        scratch_shapes=list(scratch),
        input_output_aliases=aliases or {},
        compiler_params=pltpu.CompilerParams(vmem_limit_bytes=LIMIT),
        cost_estimate=pl.CostEstimate(flops=cost, bytes_accessed=cost, transcendentals=0) if cost else None,
        name=name,
    )(*operands)


def pack_rows(cell, put, sub, north):
    both = (sub < 2) | ((sub >= 4) & (sub < 6))
    for row in range(2):
        rest = []
        for half in range(2):
            for place, tile in enumerate((0, 1, 5) if north else (3, 7, 8)):
                put(half * 4 + place, row, cell(half, tile, row))
            second, fourth, sixth = [cell(half, tile, row) for tile in (2, 4, 6)]
            if north:
                put(half * 4 + 3, row, jnp.where(sub < 2, second, jnp.where(sub < 4, sixth, fourth)))
                rest.append(sixth)
            else:
                put(half * 4 + 3, row, jnp.where(sub < 4, fourth, second))
                rest.append(jnp.where(sub < 4, second, sixth))
        other = pltpu.roll(rest[1], 2, 0)
        put(8, row, jnp.where(both, rest[0], other) if north else jnp.where(both, other, rest[0]))


def pack_all(cells, base, sea, out, low, high, north):
    sub = sublane()

    def step(pair, carry):
        def cell(half, tile, row):
            return cells[2 * pair + half, pl.ds(tile * SUB, SUB), pl.ds(base + row * W, W)] * sea[row]

        def put(tile, row, value):
            out[pl.ds(pl.multiple_of(pair * GROUP + tile * SUB, SUB), SUB), lanes(row)] = value

        pack_rows(cell, put, sub, north)
        return carry

    loop(low, high, 1, step, 0)


def pack_small(out, wind, sea, base):
    here = pl.ds(base * W, 2 * W)
    out[pl.ds(HALF, SUB), :] = jnp.zeros((SUB, 2 * W), F32)
    out[HALF : HALF + 2, :] = wind[:, here]
    out[HALF + 2 : HALF + 3, :] = sea[:, here].astype(F32)


def far_kernel(field, sea_in, wind_in, out, cells, sea, wind, sems):
    even = lax.rem(lax.axis_index("geo"), 2) == 0
    each = GROUPS // 3
    small = [
        pltpu.make_async_copy(sea_in, sea, sems.at[6]),
        pltpu.make_async_copy(wind_in, wind, sems.at[7]),
    ]

    def bring(first, lane):
        copies = []
        for c in range(3):
            for run in range(2):
                here, rows = pl.ds(c * each, each), pl.ds((first + 4 * run) * SUB, 3 * SUB)
                copies.append(
                    pltpu.make_async_copy(
                        field.at[here, rows, pl.ds(lane, 2 * W)], cells.at[here, rows], sems.at[2 * c + run]
                    )
                )
        return copies

    @pl.when(even)
    def _():
        for copy in bring(2, 0):
            copy.start()

    @pl.when(jnp.logical_not(even))
    def _():
        for copy in bring(0, 2 * W):
            copy.start()

    copies = bring(0, 0)
    for copy in small:
        copy.start()
    for copy in small:
        copy.wait()
    for c in range(3):
        copies[2 * c].wait()
        copies[2 * c + 1].wait()

        @pl.when(even)
        def _():
            mask = [full(sea[:, lanes(r)].astype(F32)) for r in (0, 1)]
            pack_all(cells, 0, mask, out, c * each // 2, (c + 1) * each // 2, False)

        @pl.when(jnp.logical_not(even))
        def _():
            mask = [full(sea[:, lanes(r)].astype(F32)) for r in (2, 3)]
            pack_all(cells, 0, mask, out, c * each // 2, (c + 1) * each // 2, True)

    @pl.when(even)
    def _():
        pack_small(out, wind, sea, 0)

    @pl.when(jnp.logical_not(even))
    def _():
        pack_small(out, wind, sea, 2)


def far_rows(field, sea, wind):
    return call(
        far_kernel,
        "far",
        [(pltpu.with_memory_space_constraint(value, pltpu.HBM), False) for value in (field, sea, wind)],
        [(HALO, False)],
        [
            pltpu.VMEM((GROUPS, GROUP, 2 * W), F32),
            pltpu.VMEM((1, ROWS * W), jnp.int32),
            pltpu.VMEM((2, ROWS * W), F32),
            pltpu.SemaphoreType.DMA((8,)),
        ],
        away=(0, 1, 2),
    )[0]


def near_kernel(cells, sea_in, wind, after, out):
    even = lax.rem(lax.axis_index("geo"), 2) == 0

    def rows(base, north):
        mask = [full(sea_in[:, lanes(base + r)].astype(F32)) for r in range(2)]
        pack_all(cells, base * W, mask, out, 0, GROUPS // 2, north)
        pack_small(out, wind, sea_in, base)

    @pl.when(even)
    def _():
        rows(2, True)

    @pl.when(jnp.logical_not(even))
    def _():
        rows(0, False)


def near_rows(field, sea, wind, after):
    return call(near_kernel, "near", [(field, True), (sea, False), (wind, False), (after, True)], [(HALO, False)])[0]


def unpack_north(halo, pair, half, row, sub):
    def get(tile):
        return halo[pl.ds(pl.multiple_of(pair * GROUP + tile * SUB, SUB), SUB), lanes(row)]

    mixed, last = get(half * 4 + 3), get(8)
    if half:
        last = pltpu.roll(last, 6, 0)
    return {
        0: get(half * 4),
        1: get(half * 4 + 1),
        2: mixed,
        4: mixed,
        5: get(half * 4 + 2),
        6: jnp.where((sub >= 2) & (sub < 4), mixed, last),
    }


def unpack_south(halo, pair, half, row, sub):
    def get(tile):
        return halo[pl.ds(pl.multiple_of(pair * GROUP + tile * SUB, SUB), SUB), lanes(row)]

    mixed, last = get(half * 4 + 3), get(8)
    if half:
        last = pltpu.roll(last, 6, 0)
    return {
        2: jnp.where(sub < 4, last, mixed),
        3: get(half * 4),
        4: mixed,
        6: last,
        7: get(half * 4 + 1),
        8: get(half * 4 + 2),
    }


def pieces(value):
    high = value.astype(BF16)
    value = value - high.astype(F32)
    middle = value.astype(BF16)
    return high, middle, (value - middle.astype(F32)).astype(BF16)


def spread(inputs, outputs, flat):
    flat[...] = jnp.zeros_like(flat)
    for place, (row, scale) in enumerate(inputs):
        for k, piece in enumerate(pieces(row[...] * scale)):
            flat[3 * place + k : 3 * place + k + 1, 0:NB] = piece.astype(F32)
    count = len(outputs)
    shape = (flat.shape[0], count * W)
    row, lane = lax.broadcasted_iota(jnp.int32, shape, 0), lax.broadcasted_iota(jnp.int32, shape, 1)
    mask = jnp.zeros(shape, F32)
    for place in range(count):
        mine = (row >= 3 * place) & (row < 3 * place + 3) & (lane >= place * W) & (lane < place * W + W)
        mask = jnp.where(mine, 1.0, mask)
    wide = lax.dot_general(
        flat[...].astype(BF16), mask.astype(BF16), (((0,), (0,)), ((), ())), preferred_element_type=F32
    )
    for place, out in enumerate(outputs):
        out[...] = wide[0:NB, place * W : (place + 1) * W]


def layout(rows, ranks):
    lines = -(-max(2, 2 * rows // ranks) // 3)
    return lines, -(-(lines + 2) // SUB) * SUB


def sort(owner, point, value, weight, ranks):
    rows = owner.shape[1]
    lines, block = layout(rows, ranks)
    hits = owner[...] == lax.broadcasted_iota(jnp.int32, (ranks, rows), 0)
    before = lax.broadcasted_iota(jnp.int32, (rows, rows), 0) < lax.broadcasted_iota(jnp.int32, (rows, rows), 1)
    counts = jnp.dot(hits.astype(F32).astype(BF16), before.astype(F32).astype(BF16), preferred_element_type=F32)
    order = jnp.sum(jnp.where(hits, counts, 0.0), axis=0, keepdims=True).astype(jnp.int32)
    line = (order * 171) >> 9
    third = order - 3 * line
    target = owner[...] * block + line
    spots = lax.broadcasted_iota(jnp.int32, (ranks * block, rows), 0)
    places = [((target == spots) & (third == k)).astype(F32).astype(BF16) for k in range(3)]
    load = jnp.concatenate(
        [
            value[...] * weight[...],
            weight[...],
            point[...].astype(F32),
            jnp.zeros((LOAD - NF - 2, rows), F32),
        ],
        axis=0,
    )
    loads = [
        jnp.concatenate(
            [jnp.zeros((LOAD * k, rows), F32)] * (k > 0) + [load, jnp.zeros((W - LOAD * (k + 1), rows), F32)], axis=0
        )
        for k in range(3)
    ]
    places = jnp.concatenate(places, axis=1)
    result = 0.0
    for piece in zip(*[pieces(part) for part in loads]):
        result = result + lax.dot_general(
            places, jnp.concatenate(piece, axis=1), (((1,), (1,)), ((), ())), preferred_element_type=F32
        )
    return result


def local_kernel(
    cells, sea_in, courant, rate_in, damp_in, steep_in, table, owner, point, value, weight,
    flow, rate, damp, steep, centre, ahead, back, across, own, slots, flat, *, ranks,
):
    sub = sublane()
    spread(((rate_in, LOG2E), (damp_in, LOG2E), (steep_in, 1.0)), (rate, damp, steep), flat)
    slots[...] = sort(owner, point, value, weight, ranks)
    sea = [full(sea_in[:, lanes(r)].astype(F32)) for r in range(ROWS)]
    zero = jnp.zeros((SUB, W), F32)

    def step(group, sums):
        sums = list(sums)
        for tile in range(TILES):
            rows, spot = pl.ds(tile * SUB, SUB), bins(group, tile)
            pace = speed(tile, sub, courant, group)
            middle = 1.0 - pace * table[0, rows, :]
            over = pace * table[1, rows, :]
            along = pace * table[2, rows, :]
            centre[spot, :] = middle
            across[spot, :] = over
            ahead[spot, :] = along
            back[spot, :] = pace * table[3, rows, :]
            heavy = steep[spot, :]
            cell = {r: cells[group, rows, lanes(r)] * sea[r] for r in range(ROWS)}
            for r in range(ROWS):
                moved = middle * cell[r] + along * side(tile, sub, cell[r], False)
                moved = plus(moved, times(over, pick(tile, sub, cell.get(r - 1), cell.get(r + 1))))
                flow[group, rows, lanes(r)] = moved
                sums[r] = sums[r] + heavy * moved
            gone = heavy * over
            if tile in NORTH:
                sums[ROWS] = sums[ROWS] + pick(tile, sub, gone * cell[ROWS - 1], None)
            if tile in SOUTH:
                sums[ROWS + 1] = sums[ROWS + 1] + pick(tile, sub, None, gone * cell[0])
        return tuple(sums)

    sums = loop(0, GROUPS, 3, step, (zero,) * (ROWS + 2))
    sums = [total(value) for value in sums]
    own[...] = jnp.zeros_like(own)
    for r in range(ROWS):
        own[0:1, lanes(r)] = sums[r] * sea[r][0:1, :]
    own[1:2, lanes(ROWS - 1)] = sums[ROWS]
    own[1:2, lanes(0)] = sums[ROWS + 1]

    _, block = layout(owner.shape[1], ranks)
    me = lax.axis_index("geo")

    def hand(row, dest):
        last = pl.ds(pl.multiple_of(dest * block + block - SUB, SUB), SUB)
        values = jnp.where(sub == SUB - 2, own[0:1, lanes(row)], slots[last, :])
        slots[last, :] = jnp.where(sub == SUB - 1, own[1:2, lanes(row)], values)

    @pl.when(me < ranks - 1)
    def _():
        hand(ROWS - 1, me + 1)

    @pl.when(me > 0)
    def _():
        hand(0, me - 1)


def local(field, sea, courant, rate, damp, steep, table, owner, point, value, weight, ranks):
    rows = owner.shape[1]
    _, block = layout(rows, ranks)

    def kernel(*refs):
        local_kernel(*refs, ranks=ranks)

    args = (sea, courant, rate, damp, steep, table, owner, point, value, weight)
    return call(
        kernel,
        "local",
        [(field, True)] + [(arg, False) for arg in args],
        [(CELLS, True)] + [(BINS, True)] * 7 + [((SUB, ROWS * W), True), ((ranks * block, W), False)],
        [pltpu.VMEM((16, 11 * W), F32)],
        smem=(2,),
    )


def place(arrived, ranks, rows, wanted, gain):
    lines, block = layout(rows, ranks)
    size = ranks * block
    shape = (size, W)
    lane = lax.broadcasted_iota(jnp.int32, shape, 1)
    held = lax.rem(lax.broadcasted_iota(jnp.int32, shape, 0), block) < lines
    load = jnp.where(held, arrived[...], 0.0)
    spots = lax.broadcasted_iota(jnp.int32, (size, ROWS * W), 1)
    sums = 0.0
    for k in range(3):
        mine = pltpu.roll(load, W - LOAD * k, 1) if k else load
        point = mine[:, NF + 1 : NF + 2].astype(jnp.int32)
        hits = (point == spots).astype(F32).astype(BF16)
        high, middle, low = [piece.astype(F32) for piece in pieces(jnp.where(lane < LOAD, mine, 0.0))]
        mine = high + pltpu.roll(middle, LOAD, 1) + pltpu.roll(low, 2 * LOAD, 1)
        sums = sums + lax.dot_general(
            mine.astype(BF16), hits, (((0,), (0,)), ((), ())), preferred_element_type=F32
        )
    sums = sums[0:LOAD] + sums[LOAD : 2 * LOAD] + sums[2 * LOAD : 3 * LOAD]
    for f in range(NF):
        rows_of = slice(4 * (f % 2), 4 * (f % 2) + 4)
        wanted[f // 2, rows_of, :] = jnp.broadcast_to(sums[f : f + 1, :] * (1.0 / ND), (4, ROWS * W))
    gain[...] = jnp.broadcast_to(sums[NF : NF + 1, :] * (1.0 / (ND * ND)), gain.shape)


def early_kernel(
    arrived, flow, own, wind, sea_in, rate, damp, steep, centre, ahead, across, next_, factor, moved, wanted, gain, state,
    *, ranks, rows,
):
    sub = sublane()
    place(arrived, ranks, rows, wanted, gain)
    lines, block = layout(rows, ranks)
    me = lax.axis_index("geo")

    def aux(source, there):
        source = jnp.clip(source, 0, ranks - 1)
        last = pl.ds(pl.multiple_of(source * block + block - SUB, SUB), SUB)
        return jnp.where(there, arrived[last, :], 0.0)

    south, north = aux(me - 1, me > 0), aux(me + 1, me < ranks - 1)
    state[...] = jnp.zeros_like(state)
    here = pl.ds(2 * W, ROWS * W)
    state[WIND0 : WIND0 + 1, here] = wind[0:1, :]
    state[WIND1 : WIND1 + 1, here] = wind[1:2, :]
    state[SEA : SEA + 1, here] = sea_in[...].astype(F32)
    steeps = {r: own[0:1, lanes(r)] for r in range(ROWS)}
    steeps[0] = steeps[0] + south[7:8, :]
    steeps[3] = steeps[3] + north[7:8, :]
    for r, value in steeps.items():
        state[STEEP0 : STEEP0 + 1, column(r)] = jnp.where(state[SEA : SEA + 1, column(r)] > 0.5, value, LAND)
    state[STEEP0 : STEEP0 + 1, column(-1)] = south[6:7, :] + own[1:2, lanes(0)]
    state[STEEP0 : STEEP0 + 1, column(4)] = north[6:7, :] + own[1:2, lanes(3)]
    steep0 = [full(state[STEEP0 : STEEP0 + 1, column(r)]) for r in range(ROWS)]
    wind0 = [full(state[WIND0 : WIND0 + 1, column(r)]) for r in range(ROWS)]

    def step(group, sums):
        sums = list(sums)
        for tile in range(TILES):
            rows, spot = pl.ds(tile * SUB, SUB), bins(group, tile)
            grow, fade, heavy = rate[spot, :], damp[spot, :], steep[spot, :]
            middle, along, over = centre[spot, :], ahead[spot, :], across[spot, :]
            cell = {}
            for r in range(ROWS):
                gained = jnp.exp2(grow * wind0[r] - fade * steep0[r])
                factor[group, rows, lanes(r)] = gained
                cell[r] = flow[group, rows, lanes(r)] * gained
                next_[group, rows, lanes(r)] = cell[r]
            for r in range(ROWS):
                value = middle * cell[r] + along * side(tile, sub, cell[r], False)
                value = plus(value, times(over, pick(tile, sub, cell.get(r - 1), cell.get(r + 1))))
                moved[group, rows, lanes(r)] = value
                sums[r] = sums[r] + heavy * value
        return tuple(sums)

    sums = loop(0, GROUPS, 3, step, (jnp.zeros((SUB, W), F32),) * ROWS)
    for r in range(ROWS):
        state[STEEP1 : STEEP1 + 1, column(r)] = total(sums[r])


def early(arrived, flow, own, wind, sea, rate, damp, steep, centre, ahead, across, ranks, rows):
    def kernel(*refs):
        early_kernel(*refs, ranks=ranks, rows=rows)

    inputs = [(arrived, False), (flow, True), (own, True), (wind, False), (sea, False)]
    inputs += [(value, True) for value in (rate, damp, steep, centre, ahead, across)]
    return call(
        kernel,
        "early",
        inputs,
        [(CELLS, True)] * 3 + [((GROUPS, SUB, ROWS * W), True), ((SUB, ROWS * W), True), (STATE, True)],
    )


def split_lam(lam, group, tile, where):
    if tile < 4:
        return lam[group, 0:1, where]
    if tile > 4:
        return lam[group, 4:5, where]
    return lam[group, :, where]


def late_kernel(
    next_in, factor, moved_in, from_far, from_near, wanted, gain, state_in, rate, damp, steep, centre, ahead, back, across,
    next_, next_south, next_north, source, edges, state, send_a, send_b, moved, growth, lam, partial,
):
    sub = sublane()
    zero = jnp.zeros((SUB, W), F32)
    even = lax.rem(lax.axis_index("geo"), 2) == 0
    state[...] = state_in[...]

    def held(place, r):
        return full(state[place : place + 1, column(r)])

    def first(pair, sums, halo_south, halo_north, steep0, wind0):
        sums = list(sums)
        for half in range(2):
            group = 2 * pair + half
            ghosts = {
                -2: unpack_north(halo_south, pair, half, 0, sub),
                -1: unpack_north(halo_south, pair, half, 1, sub),
                4: unpack_south(halo_north, pair, half, 0, sub),
                5: unpack_south(halo_north, pair, half, 1, sub),
            }
            for tile in range(TILES):
                rows, spot = pl.ds(tile * SUB, SUB), bins(group, tile)
                grow, fade, heavy = rate[spot, :], damp[spot, :], steep[spot, :]
                middle, along, over = centre[spot, :], ahead[spot, :], across[spot, :]
                beyond = {}
                changes = {}
                for near, far, mine, second, tiles, north in ((-1, -2, 0, 1, NORTH, True), (4, 5, 3, 2, SOUTH, False)):
                    if tile not in tiles:
                        continue

                    def only(value):
                        return pick(tile, sub, value, None) if north else pick(tile, sub, None, value)

                    cell = ghosts[near][tile]
                    gained = jnp.exp2(grow * wind0[near] - fade * steep0[near])
                    value = middle * cell + along * side(tile, sub, cell, False) + over * ghosts[far][tile]
                    value = value * gained
                    (next_south if north else next_north)[group, rows, :] = value
                    extra = only(over * cell) * factor[group, rows, lanes(mine)]
                    next_[group, rows, lanes(mine)] = next_in[group, rows, lanes(mine)] + extra
                    change = middle * extra + along * side(tile, sub, extra, False) + only(over * value)
                    changes[mine] = plus(change, changes.get(mine))
                    changes[second] = plus(over * extra, changes.get(second))
                for r, change in changes.items():
                    sums[r] = sums[r] + heavy * change
                    moved[group, rows, lanes(r)] = moved_in[group, rows, lanes(r)] + change
        return tuple(sums)

    def halo_terms(halo_south, halo_north):
        for halo, rows in ((halo_south, (-2, -1)), (halo_north, (4, 5))):
            here = pl.ds((rows[0] + 2) * W, 2 * W)
            for place, name in enumerate((WIND0, WIND1, SEA)):
                state[name : name + 1, here] = halo[HALF + place : HALF + place + 1, :]
        for r in (-1, 4):
            known = state[SEA : SEA + 1, column(r)] > 0.5
            state[STEEP0 : STEEP0 + 1, column(r)] = jnp.where(known, state[STEEP0 : STEEP0 + 1, column(r)], LAND)
        steep0 = {r: held(STEEP0, r) for r in (-1, 4)}
        wind0 = {r: held(WIND0, r) for r in (-1, 4)}

        def step(pair, sums):
            return first(pair, sums, halo_south, halo_north, steep0, wind0)

        sums = loop(0, GROUPS // 2, 3, step, (zero,) * ROWS)
        for r in range(ROWS):
            partial[r] = sums[r]

    @pl.when(even)
    def _():
        halo_terms(from_far, from_near)

    @pl.when(jnp.logical_not(even))
    def _():
        halo_terms(from_near, from_far)

    for r in range(ROWS):
        value = state[STEEP1 : STEEP1 + 1, column(r)] + total(partial[r])
        state[STEEP1 : STEEP1 + 1, column(r)] = jnp.where(state[SEA : SEA + 1, column(r)] > 0.5, value, LAND)
    steep1 = [held(STEEP1, r) for r in range(ROWS)]
    wind1 = [held(WIND1, r) for r in range(ROWS)]
    gains = [gain[:, lanes(r)] for r in range(ROWS)]

    def second(group, sums):
        sums = list(sums)
        means = [[None, None] for _ in range(ROWS)]
        ups = [[None, None] for _ in range(ROWS)]
        downs = [[None, None] for _ in range(ROWS)]
        for tile in range(TILES):
            rows, spot = pl.ds(tile * SUB, SUB), bins(group, tile)
            grow, fade = rate[spot, :], damp[spot, :]
            for r in range(ROWS):
                value = jnp.exp2(grow * wind1[r] - fade * steep1[r])
                growth[group, rows, lanes(r)] = value
                value = value * moved[group, rows, lanes(r)]
                for parts, term in ((means, value), (ups, grow * value), (downs, fade * value)):
                    if tile == 4:
                        parts[r][0] = plus(jnp.where(sub < 4, term, 0.0), parts[r][0])
                        parts[r][1] = jnp.where(sub < 4, 0.0, term)
                    else:
                        f = 0 if tile < 4 else 1
                        parts[r][f] = plus(term, parts[r][f])
        for r in range(ROWS):
            one, two = means[r]
            one = one + pltpu.roll(one, 4, 0)
            two = two + pltpu.roll(two, 4, 0)
            both = jnp.where(sub < 4, one, two)
            both = both + jnp.where((sub & 2) == 0, pltpu.roll(both, 6, 0), pltpu.roll(both, 2, 0))
            both = both + jnp.where((sub & 1) == 0, pltpu.roll(both, 7, 0), pltpu.roll(both, 1, 0))
            value = gains[r] * both - wanted[group, :, lanes(r)]
            lam[group, :, lanes(r)] = value
            up, down = value[0:1, :], value[4:5, :]
            sums[r] = sums[r] + (up * ups[r][0] + down * ups[r][1])
            sums[ROWS + r] = sums[ROWS + r] + (up * downs[r][0] + down * downs[r][1])
        return tuple(sums)

    sums = loop(0, GROUPS, 1, second, (zero,) * (2 * ROWS))
    for r in range(ROWS):
        state[GRAD1 : GRAD1 + 1, column(r)] = total(sums[r]) * LN2
        state[TEND1 : TEND1 + 1, column(r)] = total(sums[ROWS + r]) * (-LN2)
    tend1 = [held(TEND1, r) for r in range(ROWS)]

    def third(group, sums):
        sums = list(sums)
        for tile in range(TILES):
            rows, spot = pl.ds(tile * SUB, SUB), bins(group, tile)
            grow, fade, heavy = rate[spot, :], damp[spot, :], steep[spot, :]
            middle, along, over = centre[spot, :], back[spot, :], across[spot, :]
            cell = {}
            for r in range(ROWS):
                cell[r] = split_lam(lam, group, tile, lanes(r)) * growth[group, rows, lanes(r)] + heavy * tend1[r]
                source[group, rows, lanes(r)] = cell[r]
            for place, r in enumerate((0, ROWS - 1)):
                value = middle * cell[r] + along * side(tile, sub, cell[r], True)
                value = plus(value, times(over, pick(tile, sub, cell.get(r + 1), cell.get(r - 1))))
                edges[group, rows, lanes(place)] = value
                value = value * next_[group, rows, lanes(r)]
                sums[place] = sums[place] + grow * value
                sums[2 + place] = sums[2 + place] + fade * value
        return tuple(sums)

    sums = loop(0, GROUPS, 3, third, (zero,) * 4)
    for place, r in enumerate((0, ROWS - 1)):
        state[GRAD0 : GRAD0 + 1, column(r)] = total(sums[place]) * LN2
        state[TEND0 : TEND0 + 1, column(r)] = total(sums[2 + place]) * (-LN2)

    def fill(ref, base):
        for f in range(NF):
            ref[f : f + 1, :] = lam[f // 2, 4 * (f % 2) : 4 * (f % 2) + 1, pl.ds(base * W, 2 * W)]
        here = pl.ds((base + 2) * W, 2 * W)
        for place, name in enumerate((STEEP1, TEND1, TEND0, TEND0)):
            ref[NF + place : NF + place + 1, :] = state[name : name + 1, here]

    @pl.when(even)
    def _():
        fill(send_a, 2)
        fill(send_b, 0)

    @pl.when(jnp.logical_not(even))
    def _():
        fill(send_a, 0)
        fill(send_b, 2)


def late(next_, factor, moved, from_far, from_near, wanted, gain, state, coefficients):
    inputs = [(next_, True), (factor, True), (moved, True), (from_far, True), (from_near, True)]
    inputs += [(value, True) for value in (wanted, gain, state) + coefficients]
    return call(
        late_kernel,
        "late",
        inputs,
        [(CELLS, True)] + [(EDGE, True)] * 2 + [(CELLS, True), (EDGES, True), (STATE, True)]
        + [((NF + 4, 2 * W), False)] * 2 + [(CELLS, True)],
        [
            pltpu.VMEM(CELLS, F32),
            pltpu.VMEM((GROUPS, SUB, ROWS * W), F32),
            pltpu.VMEM((ROWS, SUB, W), F32),
        ],
        aliases={0: 0, 2: 8},
    )


def inner_kernel(
    next_, next_south, next_north, source, state_in, rate, damp, centre, back, across,
    inside, factor_south, factor_north, state,
):
    sub = sublane()
    zero = jnp.zeros((SUB, W), F32)
    state[...] = state_in[...]
    wind0 = {r: full(state[WIND0 : WIND0 + 1, column(r)]) for r in (-1, 4)}
    steep0 = {r: full(state[STEEP0 : STEEP0 + 1, column(r)]) for r in (-1, 4)}

    def step(group, sums):
        sums = list(sums)
        for tile in range(TILES):
            rows, spot = pl.ds(tile * SUB, SUB), bins(group, tile)
            grow, fade = rate[spot, :], damp[spot, :]
            if tile in SOUTH:
                factor_south[group, rows, :] = jnp.exp2(grow * wind0[-1] - fade * steep0[-1])
            if tile in NORTH:
                factor_north[group, rows, :] = jnp.exp2(grow * wind0[4] - fade * steep0[4])
            middle, along, over = centre[spot, :], back[spot, :], across[spot, :]
            cell = {r: source[group, rows, lanes(r)] for r in range(ROWS)}
            for place, r in enumerate((1, 2)):
                value = middle * cell[r] + along * side(tile, sub, cell[r], True)
                value = value + over * pick(tile, sub, cell[r + 1], cell[r - 1])
                inside[group, rows, lanes(place)] = value
                value = value * next_[group, rows, lanes(r)]
                sums[place] = sums[place] + grow * value
                sums[2 + place] = sums[2 + place] + fade * value
            gone = fade * over
            if tile in NORTH:
                value = pick(tile, sub, cell[0] * next_south[group, rows, :], None)
                sums[4] = sums[4] + gone * value
            if tile in SOUTH:
                value = pick(tile, sub, None, cell[3] * next_north[group, rows, :])
                sums[5] = sums[5] + gone * value
        return tuple(sums)

    sums = loop(0, GROUPS, 3, step, (zero,) * 6)
    for place, r in enumerate((1, 2)):
        state[GRAD0 : GRAD0 + 1, column(r)] = total(sums[place]) * LN2
        state[TEND0 : TEND0 + 1, column(r)] = total(sums[2 + place]) * (-LN2)
    state[TEND0 : TEND0 + 1, column(-1)] = total(sums[4]) * (-LN2)
    state[TEND0 : TEND0 + 1, column(4)] = total(sums[5]) * (-LN2)


def inner(*args):
    return call(
        inner_kernel,
        "inner",
        [(arg, True) for arg in args],
        [(EDGES, True), (EDGE, True), (EDGE, True), (STATE, True)],
        cost=1 << 22,
    )


def last_kernel(
    next_, factor, factor_south, factor_north, edges, inside, state, back_a, back_b, rate, damp, steep, centre, back, across,
    out, grad, rims, low, high, ghosts, lam, cells, sems,
):
    sub = sublane()
    zero = jnp.zeros((SUB, W), F32)
    even = lax.rem(lax.axis_index("geo"), 2) == 0
    ghosts[0] = jnp.where(even, back_b[...], back_a[...])
    ghosts[1] = jnp.where(even, back_a[...], back_b[...])
    for group in range(GROUPS):
        for where in range(2):
            for row in range(2):
                one = ghosts[where, 2 * group : 2 * group + 1, lanes(row)]
                two = ghosts[where, 2 * group + 1 : 2 * group + 2, lanes(row)]
                lam[group, :, lanes(2 * where + row)] = jnp.where(sub < 4, one, two)
    sea = {r: full(state[SEA : SEA + 1, column(r)]) for r in range(-2, 6)}
    wind1, steep1, tend1 = {}, {}, {}
    for r in (-2, -1, 4, 5):
        where, here = (0, lanes(r + 2)) if r < 0 else (1, lanes(r - 4))
        wind1[r] = full(state[WIND1 : WIND1 + 1, column(r)])
        value = ghosts[where, NF : NF + 1, here]
        steep1[r] = full(jnp.where(sea[r][0:1, :] > 0.5, value, LAND))
        tend1[r] = full(ghosts[where, NF + 1 : NF + 2, here])

    def first(group, sums):
        sums = list(sums)
        for tile in range(TILES):
            rows, spot = pl.ds(tile * SUB, SUB), bins(group, tile)
            grow, fade, heavy = rate[spot, :], damp[spot, :], steep[spot, :]
            middle, along, over = centre[spot, :], back[spot, :], across[spot, :]

            def ghost(r):
                value = split_lam(lam, group, tile, lanes(r + 2 if r < 0 else r - 2))
                return value * jnp.exp2(grow * wind1[r] - fade * steep1[r]) + heavy * tend1[r]

            for near, far, mine, place, tiles in ((-1, -2, 0, 0, SOUTH), (4, 5, 3, 1, NORTH)):
                if tile not in tiles:
                    continue
                cell = ghost(near)
                value = middle * cell + along * side(tile, sub, cell, True) + over * ghost(far)
                (low if place == 0 else high)[group, rows, :] = value
                value = over * cell
                value = pick(tile, sub, None, value) if place == 0 else pick(tile, sub, value, None)
                rims[group, rows, lanes(place)] = edges[group, rows, lanes(place)] + value
                value = value * next_[group, rows, lanes(mine)]
                sums[place] = sums[place] + grow * value
                sums[2 + place] = sums[2 + place] + fade * value
        return tuple(sums)

    sums = loop(0, GROUPS, 3, first, (zero,) * 4)
    sums = [total(value) * LN2 for value in sums]
    tend0 = {r: state[TEND0 : TEND0 + 1, column(r)] for r in range(-1, 5)}
    grad0 = [state[GRAD0 : GRAD0 + 1, column(r)] for r in range(ROWS)]
    tend0[0], grad0[0] = tend0[0] - sums[2], grad0[0] + sums[0]
    tend0[3], grad0[3] = tend0[3] - sums[3], grad0[3] + sums[1]
    tend0[-1] = tend0[-1] + ghosts[0, NF + 2 : NF + 3, lanes(1)]
    tend0[4] = tend0[4] + ghosts[1, NF + 2 : NF + 3, lanes(0)]
    for r in range(ROWS):
        grad[0:1, lanes(r)] = grad0[r]
        grad[1:2, lanes(r)] = state[GRAD1 : GRAD1 + 1, column(r)]
    tend0 = {r: full(value) for r, value in tend0.items()}

    def second(group, carry):
        for tile in range(TILES):
            rows, spot = pl.ds(tile * SUB, SUB), bins(group, tile)
            heavy = steep[spot, :]
            middle, along, over = centre[spot, :], back[spot, :], across[spot, :]
            cell = {}
            for r in range(-1, 5):
                if r == -1:
                    if tile not in SOUTH:
                        continue
                    value = low[group, rows, :] * factor_south[group, rows, :]
                elif r == 4:
                    if tile not in NORTH:
                        continue
                    value = high[group, rows, :] * factor_north[group, rows, :]
                else:
                    if r == 0:
                        value = (rims if tile in SOUTH else edges)[group, rows, lanes(0)]
                    elif r == 3:
                        value = (rims if tile in NORTH else edges)[group, rows, lanes(1)]
                    else:
                        value = inside[group, rows, lanes(r - 1)]
                    value = value * factor[group, rows, lanes(r)]
                cell[r] = value + heavy * tend0[r]
            for r in range(ROWS):
                value = middle * cell[r] + along * side(tile, sub, cell[r], True)
                value = value + over * pick(tile, sub, cell.get(r + 1), cell.get(r - 1))
                cells[group, rows, lanes(r)] = sea[r] * value
        return carry

    each = GROUPS // CHUNKS
    copies = []
    for c in range(CHUNKS):
        loop(c * each, (c + 1) * each, 3, second, 0)
        here = pl.ds(c * each, each)
        copies.append(pltpu.make_async_copy(cells.at[here], out.at[here], sems.at[c]))
        copies[c].start()
    for copy in copies:
        copy.wait()


def last(next_, factor, factor_south, factor_north, edges, inside, state, back_a, back_b, coefficients):
    inputs = [(value, True) for value in (next_, factor, factor_south, factor_north, edges, inside, state)]
    inputs += [(back_a, False), (back_b, False)]
    inputs += [(value, True) for value in coefficients]
    return call(
        last_kernel,
        "last",
        inputs,
        [(CELLS, False), ((2, ROWS * W), False)],
        [
            pltpu.VMEM(EDGES, F32),
            pltpu.VMEM(EDGE, F32),
            pltpu.VMEM(EDGE, F32),
            pltpu.VMEM((2, NF + 4, 2 * W), F32),
            pltpu.VMEM((GROUPS, SUB, ROWS * W), F32),
            pltpu.VMEM(CELLS, F32),
            pltpu.SemaphoreType.DMA((CHUNKS,)),
        ],
        out_away=(0,),
    )


def swaps(count):
    near = [(i, i ^ 1) for i in range(count)]
    far = []
    for i in range(1, count - 1, 2):
        far += [(i, i + 1), (i + 1, i)]
    return near, far


def body(
    initial_spectrum,
    wind_forcing,
    sea_mask,
    courant,
    input_rate,
    damping,
    steep_weight,
    obs_owner,
    obs_point,
    obs_value,
    obs_weight,
):
    count = lax.axis_size("geo")
    held = obs_point.shape[0]
    near, far = swaps(count)
    field = initial_spectrum.reshape(CELLS)
    sea = sea_mask.reshape(1, ROWS * W)
    from_far = lax.ppermute(far_rows(field, sea, wind_forcing), "geo", far)
    flow, rate, damp, steep, centre, ahead, back, across, own, slots = local(
        field,
        sea,
        courant,
        input_rate.reshape(1, NB),
        damping.reshape(1, NB),
        steep_weight.reshape(1, NB),
        jnp.asarray(direction_tables()),
        obs_owner.reshape(1, held),
        obs_point.reshape(1, held),
        obs_value.T,
        obs_weight.reshape(1, held),
        count,
    )
    from_near = lax.ppermute(near_rows(field, sea, wind_forcing, own), "geo", near)
    arrived = lax.all_to_all(slots, "geo", split_axis=0, concat_axis=0, tiled=True)
    next_, factor, moved, wanted, gain, state = early(
        arrived, flow, own, wind_forcing, sea, rate, damp, steep, centre, ahead, across, count, held
    )
    next_, next_south, next_north, source, edges, state, send_a, send_b, _ = late(
        next_, factor, moved, from_far, from_near, wanted, gain, state,
        (rate, damp, steep, centre, ahead, back, across),
    )
    back_b = lax.ppermute(send_b, "geo", far)
    back_a = lax.ppermute(send_a, "geo", near)
    inside, factor_south, factor_north, state = inner(next_, next_south, next_north, source, state, rate, damp, centre, back, across)
    out, grad = last(
        next_, factor, factor_south, factor_north, edges, inside, state, back_a, back_b,
        (rate, damp, steep, centre, back, across),
    )
    return grad, out.reshape(NB, ROWS * W)


def solution(mesh):
    return jax.shard_map(
        body,
        mesh=mesh,
        in_specs=(
            P(None, ("groups", "geo")),
            P(None, ("groups", "geo")),
            P(("groups", "geo")),
            P(),
            P(),
            P(),
            P(),
            P(("groups", "geo"), None),
            P(("groups", "geo")),
            P(("groups", "geo"), None),
            P(("groups", "geo")),
        ),
        out_specs=(P(None, ("groups", "geo")), P(None, ("groups", "geo"))),
        check_vma=False,
    )
```

```python
import math

import jax
import jax.numpy as jnp
import numpy as np
from jax import lax
from jax.experimental import pallas as pl
from jax.experimental.pallas import tpu as pltpu
from jax.sharding import PartitionSpec as P

ND = 36
NF = 36
NB = 1296
W = 128
ROWS = 4
SUB = 8
GROUP = 72
TILES = GROUP // SUB
GROUPS = NB // GROUP
CHUNKS = 6
F32 = jnp.float32
BF16 = jnp.bfloat16
LIMIT = 7 * 1024 * 1024
LOG2E = math.log2(math.e)
LN2 = math.log(2.0)
LAND = 1.0e5

CELLS = (GROUPS, GROUP, ROWS * W)
EDGE = (GROUPS, GROUP, W)
EDGES = (GROUPS, GROUP, 2 * W)
BINS = (NB, W)
HALF = NB // 2
HALO = (HALF + SUB, 2 * W)
LOAD = 40
STATE = (16, 8 * W)
STEEP0, WIND0, WIND1, SEA, STEEP1, TEND1, GRAD1, TEND0, GRAD0, PASS0 = range(10)

NORTH = (0, 1, 2, 4, 5, 6)
SOUTH = (2, 3, 4, 6, 7, 8)
FROM_WEST = (0, 4, 8)
FROM_EAST = (2, 6)


def direction_tables():
    angle = np.float32(2.0 * math.pi) * np.arange(ND, dtype=np.float32) / np.float32(ND)
    cosine = np.tile(np.cos(angle), 2)[:, None]
    sine = np.tile(np.sin(angle), 2)[:, None]
    lane = np.arange(W)[None, :]
    east = cosine >= 0
    west_ok = (lane > 0).astype(np.float32)
    east_ok = (lane < W - 1).astype(np.float32)
    one = np.ones((1, W), np.float32)
    forward = np.abs(cosine) * np.where(east, west_ok, east_ok)
    backward = np.abs(cosine) * np.where(east, east_ok, west_ok)
    return np.stack(
        [(np.abs(cosine) + np.abs(sine)) * one, np.abs(sine) * one, forward, backward]
    ).astype(np.float32)


def sublane():
    return lax.broadcasted_iota(jnp.int32, (SUB, W), 0)


def north_mask(tile, sub):
    return {2: sub < 2, 4: sub >= 4, 6: sub < 6}.get(tile)


def west_mask(tile, sub):
    return {1: sub < 1, 3: sub >= 3, 5: sub < 5, 7: sub >= 7}.get(tile)


def side(tile, sub, value, reverse):
    west = tile not in (FROM_WEST if reverse else FROM_EAST)
    east = tile not in (FROM_EAST if reverse else FROM_WEST)
    from_west = pltpu.roll(value, 1, 1) if west else None
    from_east = pltpu.roll(value, W - 1, 1) if east else None
    if from_east is None:
        return from_west
    if from_west is None:
        return from_east
    mask = west_mask(tile, sub)
    return jnp.where(mask, from_east, from_west) if reverse else jnp.where(mask, from_west, from_east)


def pick(tile, sub, north, south):
    mask = north_mask(tile, sub)
    if mask is None:
        return north if tile in NORTH else south
    if north is None and south is None:
        return None
    return jnp.where(mask, 0.0 if north is None else north, 0.0 if south is None else south)


def plus(value, other):
    return value if other is None else value + other


def times(factor, value):
    return None if value is None else factor * value


def speed(tile, sub, courant, group):
    first, second = courant[2 * group], courant[2 * group + 1]
    if tile == 4:
        return jnp.where(sub < 4, first, second)
    return jnp.full((SUB, W), first if tile < 4 else second, F32)


def lanes(row):
    return pl.ds(row * W, W)


def column(row):
    return pl.ds((row + 2) * W, W)


def bins(group, tile):
    return pl.ds(pl.multiple_of(group * GROUP + tile * SUB, SUB), SUB)


def total(value):
    return jnp.sum(value, axis=0, keepdims=True)


def full(value):
    return jnp.broadcast_to(value, (SUB, W))


def loop(low, high, by, body, init):
    def passes(index, carry):
        for k in range(by):
            carry = body(low + index * by + k, carry)
        return carry

    return lax.fori_loop(0, (high - low) // by, passes, init)


def whole(memory=pltpu.VMEM):
    return pl.BlockSpec(memory_space=memory)


def call(kernel, name, inputs, outputs, scratch=(), smem=(), away=(), out_away=(), aliases=None, cost=0):
    specs, operands = [], []
    for place, (value, resident) in enumerate(inputs):
        specs.append(whole(pltpu.SMEM if place in smem else pl.ANY if place in away else pltpu.VMEM))
        operands.append(pltpu.with_memory_space_constraint(value, pltpu.VMEM) if resident else value)
    shapes = [pltpu.VMEM(shape, F32) if resident else jax.ShapeDtypeStruct(shape, F32) for shape, resident in outputs]
    return pl.pallas_call(
        kernel,
        in_specs=specs,
        out_specs=[whole(pl.ANY if place in out_away else pltpu.VMEM) for place in range(len(outputs))],
        out_shape=shapes,
        scratch_shapes=list(scratch),
        input_output_aliases=aliases or {},
        compiler_params=pltpu.CompilerParams(vmem_limit_bytes=LIMIT),
        cost_estimate=pl.CostEstimate(flops=cost, bytes_accessed=cost, transcendentals=0) if cost else None,
        name=name,
    )(*operands)


def pack_rows(cell, put, sub, north):
    both = (sub < 2) | ((sub >= 4) & (sub < 6))
    for row in range(2):
        rest = []
        for half in range(2):
            for place, tile in enumerate((0, 1, 5) if north else (3, 7, 8)):
                put(half * 4 + place, row, cell(half, tile, row))
            second, fourth, sixth = [cell(half, tile, row) for tile in (2, 4, 6)]
            if north:
                put(half * 4 + 3, row, jnp.where(sub < 2, second, jnp.where(sub < 4, sixth, fourth)))
                rest.append(sixth)
            else:
                put(half * 4 + 3, row, jnp.where(sub < 4, fourth, second))
                rest.append(jnp.where(sub < 4, second, sixth))
        other = pltpu.roll(rest[1], 2, 0)
        put(8, row, jnp.where(both, rest[0], other) if north else jnp.where(both, other, rest[0]))


def pack_all(cells, base, sea, out, low, high, north):
    sub = sublane()

    def step(pair, carry):
        def cell(half, tile, row):
            return cells[2 * pair + half, pl.ds(tile * SUB, SUB), pl.ds(base + row * W, W)] * sea[row]

        def put(tile, row, value):
            out[pl.ds(pl.multiple_of(pair * GROUP + tile * SUB, SUB), SUB), lanes(row)] = value

        pack_rows(cell, put, sub, north)
        return carry

    loop(low, high, 1, step, 0)


def pack_small(out, wind, sea, base):
    here = pl.ds(base * W, 2 * W)
    out[pl.ds(HALF, SUB), :] = jnp.zeros((SUB, 2 * W), F32)
    out[HALF : HALF + 2, :] = wind[:, here]
    out[HALF + 2 : HALF + 3, :] = sea[:, here].astype(F32)


def far_kernel(field, sea_in, wind_in, out, cells, sea, wind, sems):
    even = lax.rem(lax.axis_index("geo"), 2) == 0
    each = GROUPS // 3
    small = [
        pltpu.make_async_copy(sea_in, sea, sems.at[6]),
        pltpu.make_async_copy(wind_in, wind, sems.at[7]),
    ]

    def bring(first, lane):
        copies = []
        for c in range(3):
            for run in range(2):
                here, rows = pl.ds(c * each, each), pl.ds((first + 4 * run) * SUB, 3 * SUB)
                copies.append(
                    pltpu.make_async_copy(
                        field.at[here, rows, pl.ds(lane, 2 * W)], cells.at[here, rows], sems.at[2 * c + run]
                    )
                )
        return copies

    @pl.when(even)
    def _():
        for copy in bring(2, 0):
            copy.start()

    @pl.when(jnp.logical_not(even))
    def _():
        for copy in bring(0, 2 * W):
            copy.start()

    copies = bring(0, 0)
    for copy in small:
        copy.start()
    for copy in small:
        copy.wait()
    for c in range(3):
        copies[2 * c].wait()
        copies[2 * c + 1].wait()

        @pl.when(even)
        def _():
            mask = [full(sea[:, lanes(r)].astype(F32)) for r in (0, 1)]
            pack_all(cells, 0, mask, out, c * each // 2, (c + 1) * each // 2, False)

        @pl.when(jnp.logical_not(even))
        def _():
            mask = [full(sea[:, lanes(r)].astype(F32)) for r in (2, 3)]
            pack_all(cells, 0, mask, out, c * each // 2, (c + 1) * each // 2, True)

    @pl.when(even)
    def _():
        pack_small(out, wind, sea, 0)

    @pl.when(jnp.logical_not(even))
    def _():
        pack_small(out, wind, sea, 2)


def far_rows(field, sea, wind):
    return call(
        far_kernel,
        "far",
        [(pltpu.with_memory_space_constraint(value, pltpu.HBM), False) for value in (field, sea, wind)],
        [(HALO, False)],
        [
            pltpu.VMEM((GROUPS, GROUP, 2 * W), F32),
            pltpu.VMEM((1, ROWS * W), jnp.int32),
            pltpu.VMEM((2, ROWS * W), F32),
            pltpu.SemaphoreType.DMA((8,)),
        ],
        away=(0, 1, 2),
    )[0]


def near_kernel(cells, sea_in, wind, after, out):
    even = lax.rem(lax.axis_index("geo"), 2) == 0

    def rows(base, north):
        mask = [full(sea_in[:, lanes(base + r)].astype(F32)) for r in range(2)]
        pack_all(cells, base * W, mask, out, 0, GROUPS // 2, north)
        pack_small(out, wind, sea_in, base)

    @pl.when(even)
    def _():
        rows(2, True)

    @pl.when(jnp.logical_not(even))
    def _():
        rows(0, False)


def near_rows(field, sea, wind, own):
    return call(near_kernel, "near", [(field, True), (sea, False), (wind, False), (own, True)], [(HALO, False)])[0]


def unpack_north(halo, pair, half, row, sub):
    def get(tile):
        return halo[pl.ds(pl.multiple_of(pair * GROUP + tile * SUB, SUB), SUB), lanes(row)]

    mixed, last = get(half * 4 + 3), get(8)
    if half:
        last = pltpu.roll(last, 6, 0)
    return {
        0: get(half * 4),
        1: get(half * 4 + 1),
        2: mixed,
        4: mixed,
        5: get(half * 4 + 2),
        6: jnp.where((sub >= 2) & (sub < 4), mixed, last),
    }


def unpack_south(halo, pair, half, row, sub):
    def get(tile):
        return halo[pl.ds(pl.multiple_of(pair * GROUP + tile * SUB, SUB), SUB), lanes(row)]

    mixed, last = get(half * 4 + 3), get(8)
    if half:
        last = pltpu.roll(last, 6, 0)
    return {
        2: jnp.where(sub < 4, last, mixed),
        3: get(half * 4),
        4: mixed,
        6: last,
        7: get(half * 4 + 1),
        8: get(half * 4 + 2),
    }


def pieces(value):
    high = value.astype(BF16)
    value = value - high.astype(F32)
    middle = value.astype(BF16)
    return high, middle, (value - middle.astype(F32)).astype(BF16)


def spread(inputs, outputs, flat):
    flat[...] = jnp.zeros_like(flat)
    for place, (row, scale) in enumerate(inputs):
        for k, piece in enumerate(pieces(row[...] * scale)):
            flat[3 * place + k : 3 * place + k + 1, 0:NB] = piece.astype(F32)
    count = len(outputs)
    shape = (flat.shape[0], count * W)
    row, lane = lax.broadcasted_iota(jnp.int32, shape, 0), lax.broadcasted_iota(jnp.int32, shape, 1)
    mask = jnp.zeros(shape, F32)
    for place in range(count):
        mine = (row >= 3 * place) & (row < 3 * place + 3) & (lane >= place * W) & (lane < place * W + W)
        mask = jnp.where(mine, 1.0, mask)
    wide = lax.dot_general(
        flat[...].astype(BF16), mask.astype(BF16), (((0,), (0,)), ((), ())), preferred_element_type=F32
    )
    for place, out in enumerate(outputs):
        out[...] = wide[0:NB, place * W : (place + 1) * W]


def layout(rows, ranks):
    lines = -(-max(2, 2 * rows // ranks) // 3)
    return lines, -(-(lines + 2) // SUB) * SUB


def sort(owner, point, value, weight, ranks):
    rows = owner.shape[1]
    lines, block = layout(rows, ranks)
    hits = owner[...] == lax.broadcasted_iota(jnp.int32, (ranks, rows), 0)
    before = lax.broadcasted_iota(jnp.int32, (rows, rows), 0) < lax.broadcasted_iota(jnp.int32, (rows, rows), 1)
    counts = jnp.dot(hits.astype(F32).astype(BF16), before.astype(F32).astype(BF16), preferred_element_type=F32)
    order = jnp.sum(jnp.where(hits, counts, 0.0), axis=0, keepdims=True).astype(jnp.int32)
    line = (order * 171) >> 9
    third = order - 3 * line
    target = owner[...] * block + line
    spots = lax.broadcasted_iota(jnp.int32, (ranks * block, rows), 0)
    places = [((target == spots) & (third == k)).astype(F32).astype(BF16) for k in range(3)]
    load = jnp.concatenate(
        [
            value[...] * weight[...],
            weight[...],
            point[...].astype(F32),
            jnp.zeros((LOAD - NF - 2, rows), F32),
        ],
        axis=0,
    )
    loads = [
        jnp.concatenate(
            [jnp.zeros((LOAD * k, rows), F32)] * (k > 0) + [load, jnp.zeros((W - LOAD * (k + 1), rows), F32)], axis=0
        )
        for k in range(3)
    ]
    places = jnp.concatenate(places, axis=1)
    result = 0.0
    for piece in zip(*[pieces(part) for part in loads]):
        result = result + lax.dot_general(
            places, jnp.concatenate(piece, axis=1), (((1,), (1,)), ((), ())), preferred_element_type=F32
        )
    return result


def local_kernel(
    cells, sea_in, courant, rate_in, damp_in, steep_in, table,
    flow, rate, damp, steep, centre, ahead, back, across, own, flat,
):
    sub = sublane()
    spread(((rate_in, LOG2E), (damp_in, LOG2E), (steep_in, 1.0)), (rate, damp, steep), flat)
    sea = [full(sea_in[:, lanes(r)].astype(F32)) for r in range(ROWS)]
    zero = jnp.zeros((SUB, W), F32)

    def step(group, sums):
        sums = list(sums)
        for tile in range(TILES):
            rows, spot = pl.ds(tile * SUB, SUB), bins(group, tile)
            pace = speed(tile, sub, courant, group)
            middle = 1.0 - pace * table[0, rows, :]
            over = pace * table[1, rows, :]
            along = pace * table[2, rows, :]
            centre[spot, :] = middle
            across[spot, :] = over
            ahead[spot, :] = along
            back[spot, :] = pace * table[3, rows, :]
            heavy = steep[spot, :]
            cell = {r: cells[group, rows, lanes(r)] * sea[r] for r in range(ROWS)}
            for r in range(ROWS):
                moved = middle * cell[r] + along * side(tile, sub, cell[r], False)
                moved = plus(moved, times(over, pick(tile, sub, cell.get(r - 1), cell.get(r + 1))))
                flow[group, rows, lanes(r)] = moved
                sums[r] = sums[r] + heavy * moved
            gone = heavy * over
            if tile in NORTH:
                sums[ROWS] = sums[ROWS] + pick(tile, sub, gone * cell[ROWS - 1], None)
            if tile in SOUTH:
                sums[ROWS + 1] = sums[ROWS + 1] + pick(tile, sub, None, gone * cell[0])
        return tuple(sums)

    sums = loop(0, GROUPS, 3, step, (zero,) * (ROWS + 2))
    sums = [total(value) for value in sums]
    own[...] = jnp.zeros_like(own)
    for r in range(ROWS):
        own[0:1, lanes(r)] = sums[r] * sea[r][0:1, :]
    own[1:2, lanes(ROWS - 1)] = sums[ROWS]
    own[1:2, lanes(0)] = sums[ROWS + 1]


def local(field, sea, courant, rate, damp, steep, table):
    return call(
        local_kernel,
        "local",
        [(field, True)] + [(arg, False) for arg in (sea, courant, rate, damp, steep, table)],
        [(CELLS, True)] + [(BINS, True)] * 7 + [((SUB, ROWS * W), True)],
        [pltpu.VMEM((16, 11 * W), F32)],
        smem=(2,),
    )


def settle(arrived, wanted, gain, ranks, rows):
    lines, block = layout(rows, ranks)
    size = ranks * block
    shape = (size, W)
    lane = lax.broadcasted_iota(jnp.int32, shape, 1)
    held = lax.rem(lax.broadcasted_iota(jnp.int32, shape, 0), block) < lines
    load = jnp.where(held, arrived[...], 0.0)
    spots = lax.broadcasted_iota(jnp.int32, (size, ROWS * W), 1)
    sums = 0.0
    for k in range(3):
        mine = pltpu.roll(load, W - LOAD * k, 1) if k else load
        point = mine[:, NF + 1 : NF + 2].astype(jnp.int32)
        hits = (point == spots).astype(F32).astype(BF16)
        high, middle, low = [piece.astype(F32) for piece in pieces(jnp.where(lane < LOAD, mine, 0.0))]
        mine = high + pltpu.roll(middle, LOAD, 1) + pltpu.roll(low, 2 * LOAD, 1)
        sums = sums + lax.dot_general(
            mine.astype(BF16), hits, (((0,), (0,)), ((), ())), preferred_element_type=F32
        )
    sums = sums[0:LOAD] + sums[LOAD : 2 * LOAD] + sums[2 * LOAD : 3 * LOAD]
    for f in range(NF):
        rows_of = slice(4 * (f % 2), 4 * (f % 2) + 4)
        wanted[f // 2, rows_of, :] = jnp.broadcast_to(sums[f : f + 1, :] * (1.0 / ND), (4, ROWS * W))
    gain[...] = jnp.broadcast_to(sums[NF : NF + 1, :] * (1.0 / (ND * ND)), gain.shape)


def middle_kernel(
    flow, own, wind, sea_in, rate, damp, steep, centre, ahead, across, owner, point, value, weight, after,
    next_, factor, moved, state, slots, *, ranks,
):
    sub = sublane()
    slots[...] = sort(owner, point, value, weight, ranks)
    _, block = layout(owner.shape[1], ranks)
    me = lax.axis_index("geo")

    def hand(row, dest):
        last = pl.ds(pl.multiple_of(dest * block + block - SUB, SUB), SUB)
        values = jnp.where(sub == SUB - 2, own[0:1, lanes(row)], slots[last, :])
        slots[last, :] = jnp.where(sub == SUB - 1, own[1:2, lanes(row)], values)

    @pl.when(me < ranks - 1)
    def _():
        hand(ROWS - 1, me + 1)

    @pl.when(me > 0)
    def _():
        hand(0, me - 1)

    state[...] = jnp.zeros_like(state)
    here = pl.ds(2 * W, ROWS * W)
    state[WIND0 : WIND0 + 1, here] = wind[0:1, :]
    state[WIND1 : WIND1 + 1, here] = wind[1:2, :]
    state[SEA : SEA + 1, here] = sea_in[...].astype(F32)
    state[STEEP0 : STEEP0 + 1, here] = jnp.where(state[SEA : SEA + 1, here] > 0.5, own[0:1, :], LAND)
    steep0 = {r: full(state[STEEP0 : STEEP0 + 1, column(r)]) for r in (1, 2)}
    wind0 = {r: full(state[WIND0 : WIND0 + 1, column(r)]) for r in (1, 2)}

    def step(group, sums):
        sums = list(sums)
        for tile in range(TILES):
            rows, spot = pl.ds(tile * SUB, SUB), bins(group, tile)
            grow, fade, heavy = rate[spot, :], damp[spot, :], steep[spot, :]
            middle, along, over = centre[spot, :], ahead[spot, :], across[spot, :]
            cell, new = {}, {}
            for r in (1, 2):
                gained = jnp.exp2(grow * wind0[r] - fade * steep0[r])
                factor[group, rows, lanes(r)] = gained
                cell[r] = flow[group, rows, lanes(r)] * gained
                next_[group, rows, lanes(r)] = cell[r]
                new[r] = middle * cell[r] + along * side(tile, sub, cell[r], False)
            new[1] = plus(new[1], pick(tile, sub, None, over * cell[2]))
            new[2] = plus(new[2], pick(tile, sub, over * cell[1], None))
            if tile in SOUTH:
                new[0] = pick(tile, sub, None, over * cell[1])
            if tile in NORTH:
                new[3] = pick(tile, sub, over * cell[2], None)
            for r, value in new.items():
                moved[group, rows, lanes(r)] = value
                sums[r] = sums[r] + heavy * value
        return tuple(sums)

    sums = loop(0, GROUPS, 3, step, (jnp.zeros((SUB, W), F32),) * ROWS)
    for r in range(ROWS):
        state[STEEP1 : STEEP1 + 1, column(r)] = total(sums[r])


def middle(flow, own, wind, sea, coefficients, observed, after, ranks):
    _, block = layout(observed[0].shape[1], ranks)

    def kernel(*refs):
        middle_kernel(*refs, ranks=ranks)

    inputs = [(flow, True), (own, True), (wind, False), (sea, False)]
    inputs += [(value, True) for value in coefficients] + [(value, False) for value in observed + (after,)]
    return call(
        kernel,
        "middle",
        inputs,
        [(CELLS, True)] * 3 + [(STATE, True), ((ranks * block, W), False)],
        away=(len(inputs) - 1,),
        aliases={0: 0},
    )


def split_lam(lam, group, tile, where):
    if tile < 4:
        return lam[group, 0:1, where]
    if tile > 4:
        return lam[group, 4:5, where]
    return lam[group, :, where]


def late_kernel(
    next_in, factor_in, moved_in, from_far, from_near, arrived, own, state_in,
    rate, damp, steep, centre, ahead, back, across,
    next_, factor, moved, next_south, next_north, edges, state, send_b, lam, growth, partial, wanted, gain,
    *, ranks, held_rows,
):
    sub = sublane()
    zero = jnp.zeros((SUB, W), F32)
    even = lax.rem(lax.axis_index("geo"), 2) == 0
    state[...] = state_in[...]
    settle(arrived, wanted, gain, ranks, held_rows)

    def held(place, r):
        return full(state[place : place + 1, column(r)])

    def first(pair, sums, halo_south, halo_north, steep0, wind0):
        sums = list(sums)
        for half in range(2):
            group = 2 * pair + half
            ghosts = {
                -2: unpack_north(halo_south, pair, half, 0, sub),
                -1: unpack_north(halo_south, pair, half, 1, sub),
                4: unpack_south(halo_north, pair, half, 0, sub),
                5: unpack_south(halo_north, pair, half, 1, sub),
            }
            for tile in range(TILES):
                rows, spot = pl.ds(tile * SUB, SUB), bins(group, tile)
                grow, fade, heavy = rate[spot, :], damp[spot, :], steep[spot, :]
                middle, along, over = centre[spot, :], ahead[spot, :], across[spot, :]
                for near, far, mine, second, north in ((-1, -2, 0, 1, True), (4, 5, 3, 2, False)):
                    inward = tile in (NORTH if north else SOUTH)
                    held_back = tile in (SOUTH if north else NORTH)

                    def only(value):
                        return pick(tile, sub, value, None) if north else pick(tile, sub, None, value)

                    here = next_in[group, rows, lanes(mine)]
                    if inward:
                        cell = ghosts[near][tile]
                        gained = jnp.exp2(grow * wind0[near] - fade * steep0[near])
                        value = middle * cell + along * side(tile, sub, cell, False) + over * ghosts[far][tile]
                        value = value * gained
                        (next_south if north else next_north)[group, rows, :] = value
                        here = here + only(over * cell)
                    gained = jnp.exp2(grow * wind0[mine] - fade * steep0[mine])
                    factor[group, rows, lanes(mine)] = gained
                    here = here * gained
                    next_[group, rows, lanes(mine)] = here
                    change = middle * here + along * side(tile, sub, here, False)
                    if inward:
                        change = change + only(over * value)
                    sums[mine] = sums[mine] + heavy * change
                    if held_back:
                        change = change + moved_in[group, rows, lanes(mine)]
                    moved[group, rows, lanes(mine)] = change
                    if inward:
                        change = only(over * here)
                        sums[second] = sums[second] + heavy * change
                        moved[group, rows, lanes(second)] = moved_in[group, rows, lanes(second)] + change
        return tuple(sums)

    def halo_terms(halo_south, halo_north, south, north):
        for halo, rows in ((halo_south, (-2, -1)), (halo_north, (4, 5))):
            here = pl.ds((rows[0] + 2) * W, 2 * W)
            for place, name in enumerate((WIND0, WIND1, SEA)):
                state[name : name + 1, here] = halo[HALF + place : HALF + place + 1, :]
        steeps = {
            -1: south[0] + own[1:2, lanes(0)],
            0: own[0:1, lanes(0)] + south[1],
            3: own[0:1, lanes(3)] + north[1],
            4: north[0] + own[1:2, lanes(3)],
        }
        for r, value in steeps.items():
            known = state[SEA : SEA + 1, column(r)] > 0.5
            state[STEEP0 : STEEP0 + 1, column(r)] = jnp.where(known, value, LAND)
        steep0 = {r: held(STEEP0, r) for r in steeps}
        wind0 = {r: held(WIND0, r) for r in steeps}

        def step(pair, sums):
            return first(pair, sums, halo_south, halo_north, steep0, wind0)

        sums = loop(0, GROUPS // 2, 3, step, (zero,) * ROWS)
        for r in range(ROWS):
            partial[r] = sums[r]

    _, block = layout(held_rows, ranks)
    me = lax.axis_index("geo")

    def sent(source, there):
        source = jnp.clip(source, 0, ranks - 1)
        last = pl.ds(pl.multiple_of(source * block + block - SUB, SUB), SUB)
        values = jnp.where(there, arrived[last, :], 0.0)
        return values[SUB - 2 : SUB - 1, :], values[SUB - 1 : SUB, :]

    @pl.when(even)
    def _():
        halo_terms(from_far, from_near, sent(me - 1, me > 0), sent(me + 1, me < ranks - 1))

    @pl.when(jnp.logical_not(even))
    def _():
        halo_terms(from_near, from_far, sent(me - 1, me > 0), sent(me + 1, me < ranks - 1))

    for r in range(ROWS):
        value = state[STEEP1 : STEEP1 + 1, column(r)] + total(partial[r])
        state[STEEP1 : STEEP1 + 1, column(r)] = jnp.where(state[SEA : SEA + 1, column(r)] > 0.5, value, LAND)
    steep1 = [held(STEEP1, r) for r in range(ROWS)]
    wind1 = [held(WIND1, r) for r in range(ROWS)]
    gains = [gain[:, lanes(r)] for r in range(ROWS)]

    def second(group, sums):
        sums = list(sums)
        means = [[None, None] for _ in range(ROWS)]
        ups = [[None, None] for _ in range(ROWS)]
        downs = [[None, None] for _ in range(ROWS)]
        for tile in range(TILES):
            rows, spot = pl.ds(tile * SUB, SUB), bins(group, tile)
            grow, fade = rate[spot, :], damp[spot, :]
            for r in range(ROWS):
                value = jnp.exp2(grow * wind1[r] - fade * steep1[r])
                growth[group, rows, lanes(r)] = value
                value = value * moved[group, rows, lanes(r)]
                for parts, term in ((means, value), (ups, grow * value), (downs, fade * value)):
                    if tile == 4:
                        parts[r][0] = plus(jnp.where(sub < 4, term, 0.0), parts[r][0])
                        parts[r][1] = jnp.where(sub < 4, 0.0, term)
                    else:
                        f = 0 if tile < 4 else 1
                        parts[r][f] = plus(term, parts[r][f])
        for r in range(ROWS):
            one, two = means[r]
            one = one + pltpu.roll(one, 4, 0)
            two = two + pltpu.roll(two, 4, 0)
            both = jnp.where(sub < 4, one, two)
            both = both + jnp.where((sub & 2) == 0, pltpu.roll(both, 6, 0), pltpu.roll(both, 2, 0))
            both = both + jnp.where((sub & 1) == 0, pltpu.roll(both, 7, 0), pltpu.roll(both, 1, 0))
            value = gains[r] * both - wanted[group, :, lanes(r)]
            lam[group, :, lanes(r)] = value
            up, down = value[0:1, :], value[4:5, :]
            sums[r] = sums[r] + (up * ups[r][0] + down * ups[r][1])
            sums[ROWS + r] = sums[ROWS + r] + (up * downs[r][0] + down * downs[r][1])
        return tuple(sums)

    sums = loop(0, GROUPS, 1, second, (zero,) * (2 * ROWS))
    for r in range(ROWS):
        state[GRAD1 : GRAD1 + 1, column(r)] = total(sums[r]) * LN2
        state[TEND1 : TEND1 + 1, column(r)] = total(sums[ROWS + r]) * (-LN2)
    tend1 = [held(TEND1, r) for r in range(ROWS)]

    def third(group, sums):
        sums = list(sums)
        for tile in range(TILES):
            rows, spot = pl.ds(tile * SUB, SUB), bins(group, tile)
            grow, fade, heavy = rate[spot, :], damp[spot, :], steep[spot, :]
            middle, along, over = centre[spot, :], back[spot, :], across[spot, :]
            cell = {}
            for r in range(ROWS):
                cell[r] = split_lam(lam, group, tile, lanes(r)) * growth[group, rows, lanes(r)] + heavy * tend1[r]
                moved[group, rows, lanes(r)] = cell[r]
            for place, r in enumerate((0, ROWS - 1)):
                value = middle * cell[r] + along * side(tile, sub, cell[r], True)
                value = plus(value, times(over, pick(tile, sub, cell.get(r + 1), cell.get(r - 1))))
                edges[group, rows, lanes(place)] = value
                value = value * next_[group, rows, lanes(r)]
                sums[place] = sums[place] + grow * value
                sums[2 + place] = sums[2 + place] + fade * value
        return tuple(sums)

    sums = loop(0, GROUPS, 3, third, (zero,) * 4)
    for place, r in enumerate((0, ROWS - 1)):
        state[GRAD0 : GRAD0 + 1, column(r)] = total(sums[place]) * LN2
        state[TEND0 : TEND0 + 1, column(r)] = total(sums[2 + place]) * (-LN2)

    @pl.when(even)
    def _():
        fill(send_b, lam, state, 0)

    @pl.when(jnp.logical_not(even))
    def _():
        fill(send_b, lam, state, 2)


def fill(ref, lam, state, base):
    for f in range(NF):
        ref[f : f + 1, :] = lam[f // 2, 4 * (f % 2) : 4 * (f % 2) + 1, pl.ds(base * W, 2 * W)]
    here = pl.ds((base + 2) * W, 2 * W)
    for place, name in enumerate((STEEP1, TEND1, TEND0, TEND0)):
        ref[NF + place : NF + place + 1, :] = state[name : name + 1, here]


def late(next_, factor, moved, from_far, from_near, arrived, own, state, coefficients, ranks, rows):
    def kernel(*refs):
        late_kernel(*refs, ranks=ranks, held_rows=rows)

    inputs = (next_, factor, moved, from_far, from_near, arrived, own, state) + coefficients
    return call(
        kernel,
        "late",
        [(value, True) for value in inputs],
        [(CELLS, True)] * 3 + [(EDGE, True)] * 2 + [(EDGES, True), (STATE, True), ((NF + 4, 2 * W), False)]
        + [((GROUPS, SUB, ROWS * W), True)],
        [
            pltpu.VMEM(CELLS, F32),
            pltpu.VMEM((ROWS, SUB, W), F32),
            pltpu.VMEM((GROUPS, SUB, ROWS * W), F32),
            pltpu.VMEM((SUB, ROWS * W), F32),
        ],
        aliases={0: 0, 1: 1, 2: 2},
    )


def inner_kernel(
    next_, next_south, next_north, source, state_in, lam, rate, damp, centre, back, across,
    inside, factor_south, factor_north, state, send_a,
):
    sub = sublane()
    zero = jnp.zeros((SUB, W), F32)
    state[...] = state_in[...]
    even = lax.rem(lax.axis_index("geo"), 2) == 0

    @pl.when(even)
    def _():
        fill(send_a, lam, state, 2)

    @pl.when(jnp.logical_not(even))
    def _():
        fill(send_a, lam, state, 0)

    wind0 = {r: full(state[WIND0 : WIND0 + 1, column(r)]) for r in (-1, 4)}
    steep0 = {r: full(state[STEEP0 : STEEP0 + 1, column(r)]) for r in (-1, 4)}

    def step(group, sums):
        sums = list(sums)
        for tile in range(TILES):
            rows, spot = pl.ds(tile * SUB, SUB), bins(group, tile)
            grow, fade = rate[spot, :], damp[spot, :]
            if tile in SOUTH:
                factor_south[group, rows, :] = jnp.exp2(grow * wind0[-1] - fade * steep0[-1])
            if tile in NORTH:
                factor_north[group, rows, :] = jnp.exp2(grow * wind0[4] - fade * steep0[4])
            middle, along, over = centre[spot, :], back[spot, :], across[spot, :]
            cell = {r: source[group, rows, lanes(r)] for r in range(ROWS)}
            for place, r in enumerate((1, 2)):
                value = middle * cell[r] + along * side(tile, sub, cell[r], True)
                value = value + over * pick(tile, sub, cell[r + 1], cell[r - 1])
                inside[group, rows, lanes(place)] = value
                value = value * next_[group, rows, lanes(r)]
                sums[place] = sums[place] + grow * value
                sums[2 + place] = sums[2 + place] + fade * value
            gone = fade * over
            if tile in NORTH:
                value = pick(tile, sub, cell[0] * next_south[group, rows, :], None)
                sums[4] = sums[4] + gone * value
            if tile in SOUTH:
                value = pick(tile, sub, None, cell[3] * next_north[group, rows, :])
                sums[5] = sums[5] + gone * value
        return tuple(sums)

    sums = loop(0, GROUPS, 3, step, (zero,) * 6)
    for place, r in enumerate((1, 2)):
        state[GRAD0 : GRAD0 + 1, column(r)] = total(sums[place]) * LN2
        state[TEND0 : TEND0 + 1, column(r)] = total(sums[2 + place]) * (-LN2)
    state[TEND0 : TEND0 + 1, column(-1)] = total(sums[4]) * (-LN2)
    state[TEND0 : TEND0 + 1, column(4)] = total(sums[5]) * (-LN2)


def inner(*args):
    return call(
        inner_kernel,
        "inner",
        [(arg, True) for arg in args],
        [(EDGES, True), (EDGE, True), (EDGE, True), (STATE, True), ((NF + 4, 2 * W), False)],
        cost=1 << 22,
    )


def last_kernel(
    next_, factor, factor_south, factor_north, edges, inside, state, back_a, back_b, rate, damp, steep, centre, back, across,
    out, grad, rims, low, high, ghosts, lam, cells, sems,
):
    sub = sublane()
    zero = jnp.zeros((SUB, W), F32)
    even = lax.rem(lax.axis_index("geo"), 2) == 0
    ghosts[0] = jnp.where(even, back_b[...], back_a[...])
    ghosts[1] = jnp.where(even, back_a[...], back_b[...])
    for group in range(GROUPS):
        for where in range(2):
            for row in range(2):
                one = ghosts[where, 2 * group : 2 * group + 1, lanes(row)]
                two = ghosts[where, 2 * group + 1 : 2 * group + 2, lanes(row)]
                lam[group, :, lanes(2 * where + row)] = jnp.where(sub < 4, one, two)
    sea = {r: full(state[SEA : SEA + 1, column(r)]) for r in range(-2, 6)}
    wind1, steep1, tend1 = {}, {}, {}
    for r in (-2, -1, 4, 5):
        where, here = (0, lanes(r + 2)) if r < 0 else (1, lanes(r - 4))
        wind1[r] = full(state[WIND1 : WIND1 + 1, column(r)])
        value = ghosts[where, NF : NF + 1, here]
        steep1[r] = full(jnp.where(sea[r][0:1, :] > 0.5, value, LAND))
        tend1[r] = full(ghosts[where, NF + 1 : NF + 2, here])

    def first(group, sums):
        sums = list(sums)
        for tile in range(TILES):
            rows, spot = pl.ds(tile * SUB, SUB), bins(group, tile)
            grow, fade, heavy = rate[spot, :], damp[spot, :], steep[spot, :]
            middle, along, over = centre[spot, :], back[spot, :], across[spot, :]

            def ghost(r):
                value = split_lam(lam, group, tile, lanes(r + 2 if r < 0 else r - 2))
                return value * jnp.exp2(grow * wind1[r] - fade * steep1[r]) + heavy * tend1[r]

            for near, far, mine, place, tiles in ((-1, -2, 0, 0, SOUTH), (4, 5, 3, 1, NORTH)):
                if tile not in tiles:
                    continue
                cell = ghost(near)
                value = middle * cell + along * side(tile, sub, cell, True) + over * ghost(far)
                (low if place == 0 else high)[group, rows, :] = value
                value = over * cell
                value = pick(tile, sub, None, value) if place == 0 else pick(tile, sub, value, None)
                rims[group, rows, lanes(place)] = edges[group, rows, lanes(place)] + value
                value = value * next_[group, rows, lanes(mine)]
                sums[place] = sums[place] + grow * value
                sums[2 + place] = sums[2 + place] + fade * value
        return tuple(sums)

    sums = loop(0, GROUPS, 3, first, (zero,) * 4)
    sums = [total(value) * LN2 for value in sums]
    tend0 = {r: state[TEND0 : TEND0 + 1, column(r)] for r in range(-1, 5)}
    grad0 = [state[GRAD0 : GRAD0 + 1, column(r)] for r in range(ROWS)]
    tend0[0], grad0[0] = tend0[0] - sums[2], grad0[0] + sums[0]
    tend0[3], grad0[3] = tend0[3] - sums[3], grad0[3] + sums[1]
    tend0[-1] = tend0[-1] + ghosts[0, NF + 2 : NF + 3, lanes(1)]
    tend0[4] = tend0[4] + ghosts[1, NF + 2 : NF + 3, lanes(0)]
    for r in range(ROWS):
        grad[0:1, lanes(r)] = grad0[r]
        grad[1:2, lanes(r)] = state[GRAD1 : GRAD1 + 1, column(r)]
    tend0 = {r: full(value) for r, value in tend0.items()}

    def second(group, carry):
        for tile in range(TILES):
            rows, spot = pl.ds(tile * SUB, SUB), bins(group, tile)
            heavy = steep[spot, :]
            middle, along, over = centre[spot, :], back[spot, :], across[spot, :]
            cell = {}
            for r in range(-1, 5):
                if r == -1:
                    if tile not in SOUTH:
                        continue
                    value = low[group, rows, :] * factor_south[group, rows, :]
                elif r == 4:
                    if tile not in NORTH:
                        continue
                    value = high[group, rows, :] * factor_north[group, rows, :]
                else:
                    if r == 0:
                        value = (rims if tile in SOUTH else edges)[group, rows, lanes(0)]
                    elif r == 3:
                        value = (rims if tile in NORTH else edges)[group, rows, lanes(1)]
                    else:
                        value = inside[group, rows, lanes(r - 1)]
                    value = value * factor[group, rows, lanes(r)]
                cell[r] = value + heavy * tend0[r]
            for r in range(ROWS):
                value = middle * cell[r] + along * side(tile, sub, cell[r], True)
                value = value + over * pick(tile, sub, cell.get(r + 1), cell.get(r - 1))
                cells[group, rows, lanes(r)] = sea[r] * value
        return carry

    each = GROUPS // CHUNKS
    copies = []
    for c in range(CHUNKS):
        loop(c * each, (c + 1) * each, 3, second, 0)
        here = pl.ds(c * each, each)
        copies.append(pltpu.make_async_copy(cells.at[here], out.at[here], sems.at[c]))
        copies[c].start()
    for copy in copies:
        copy.wait()


def last(next_, factor, factor_south, factor_north, edges, inside, state, back_a, back_b, coefficients):
    inputs = [(value, True) for value in (next_, factor, factor_south, factor_north, edges, inside, state)]
    inputs += [(back_a, False), (back_b, False)]
    inputs += [(value, True) for value in coefficients]
    return call(
        last_kernel,
        "last",
        inputs,
        [(CELLS, False), ((2, ROWS * W), False)],
        [
            pltpu.VMEM(EDGES, F32),
            pltpu.VMEM(EDGE, F32),
            pltpu.VMEM(EDGE, F32),
            pltpu.VMEM((2, NF + 4, 2 * W), F32),
            pltpu.VMEM((GROUPS, SUB, ROWS * W), F32),
            pltpu.VMEM(CELLS, F32),
            pltpu.SemaphoreType.DMA((CHUNKS,)),
        ],
        out_away=(0,),
    )


def swaps(count):
    near = [(i, i ^ 1) for i in range(count)]
    far = []
    for i in range(1, count - 1, 2):
        far += [(i, i + 1), (i + 1, i)]
    return near, far


def body(
    initial_spectrum,
    wind_forcing,
    sea_mask,
    courant,
    input_rate,
    damping,
    steep_weight,
    obs_owner,
    obs_point,
    obs_value,
    obs_weight,
):
    count = lax.axis_size("geo")
    held = obs_point.shape[0]
    near, far = swaps(count)
    field = initial_spectrum.reshape(CELLS)
    sea = sea_mask.reshape(1, ROWS * W)
    from_far = lax.ppermute(far_rows(field, sea, wind_forcing), "geo", far)
    flow, rate, damp, steep, centre, ahead, back, across, own = local(
        field,
        sea,
        courant,
        input_rate.reshape(1, NB),
        damping.reshape(1, NB),
        steep_weight.reshape(1, NB),
        jnp.asarray(direction_tables()),
    )
    rows = near_rows(field, sea, wind_forcing, own)
    from_near = lax.ppermute(rows, "geo", near)
    next_, factor, moved, state, slots = middle(
        flow, own, wind_forcing, sea, (rate, damp, steep, centre, ahead, across),
        (obs_owner.reshape(1, held), obs_point.reshape(1, held), obs_value.T, obs_weight.reshape(1, held)), rows, count,
    )
    arrived = lax.all_to_all(slots, "geo", split_axis=0, concat_axis=0, tiled=True)
    next_, factor, source, next_south, next_north, edges, state, send_b, lam = late(
        next_, factor, moved, from_far, from_near, arrived, own, state,
        (rate, damp, steep, centre, ahead, back, across), count, held,
    )
    back_b = lax.ppermute(send_b, "geo", far)
    inside, factor_south, factor_north, state, send_a = inner(
        next_, next_south, next_north, source, state, lam, rate, damp, centre, back, across
    )
    back_a = lax.ppermute(send_a, "geo", near)
    out, grad = last(
        next_, factor, factor_south, factor_north, edges, inside, state, back_a, back_b,
        (rate, damp, steep, centre, back, across),
    )
    return grad, out.reshape(NB, ROWS * W)


def solution(mesh):
    return jax.shard_map(
        body,
        mesh=mesh,
        in_specs=(
            P(None, ("groups", "geo")),
            P(None, ("groups", "geo")),
            P(("groups", "geo")),
            P(),
            P(),
            P(),
            P(),
            P(("groups", "geo"), None),
            P(("groups", "geo")),
            P(("groups", "geo"), None),
            P(("groups", "geo")),
        ),
        out_specs=(P(None, ("groups", "geo")), P(None, ("groups", "geo"))),
        check_vma=False,
    )
```

```python
import math

import jax
import jax.numpy as jnp
import numpy as np
from jax import lax
from jax.experimental import pallas as pl
from jax.experimental.pallas import tpu as pltpu
from jax.sharding import PartitionSpec as P

ND = 36
NF = 36
NB = 1296
W = 128
ROWS = 4
SUB = 8
GROUP = 72
TILES = GROUP // SUB
GROUPS = NB // GROUP
CHUNKS = 6
F32 = jnp.float32
BF16 = jnp.bfloat16
LIMIT = 7 * 1024 * 1024
LOG2E = math.log2(math.e)
LN2 = math.log(2.0)
LAND = 1.0e5

CELLS = (GROUPS, GROUP, ROWS * W)
EDGE = (GROUPS, GROUP, W)
EDGES = (GROUPS, GROUP, 2 * W)
BINS = (NB, W)
HALF = NB // 2
HALO = (HALF + SUB, 2 * W)
LOAD = 40
STATE = (16, 8 * W)
STEEP0, WIND0, WIND1, SEA, STEEP1, TEND1, GRAD1, TEND0, GRAD0, PASS0 = range(10)

NORTH = (0, 1, 2, 4, 5, 6)
SOUTH = (2, 3, 4, 6, 7, 8)
FROM_WEST = (0, 4, 8)
FROM_EAST = (2, 6)


def direction_tables():
    angle = np.float32(2.0 * math.pi) * np.arange(ND, dtype=np.float32) / np.float32(ND)
    cosine = np.tile(np.cos(angle), 2)[:, None]
    sine = np.tile(np.sin(angle), 2)[:, None]
    lane = np.arange(W)[None, :]
    east = cosine >= 0
    west_ok = (lane > 0).astype(np.float32)
    east_ok = (lane < W - 1).astype(np.float32)
    one = np.ones((1, W), np.float32)
    forward = np.abs(cosine) * np.where(east, west_ok, east_ok)
    backward = np.abs(cosine) * np.where(east, east_ok, west_ok)
    return np.stack(
        [(np.abs(cosine) + np.abs(sine)) * one, np.abs(sine) * one, forward, backward]
    ).astype(np.float32)


def sublane():
    return lax.broadcasted_iota(jnp.int32, (SUB, W), 0)


def north_mask(tile, sub):
    return {2: sub < 2, 4: sub >= 4, 6: sub < 6}.get(tile)


def west_mask(tile, sub):
    return {1: sub < 1, 3: sub >= 3, 5: sub < 5, 7: sub >= 7}.get(tile)


def side(tile, sub, value, reverse):
    west = tile not in (FROM_WEST if reverse else FROM_EAST)
    east = tile not in (FROM_EAST if reverse else FROM_WEST)
    from_west = pltpu.roll(value, 1, 1) if west else None
    from_east = pltpu.roll(value, W - 1, 1) if east else None
    if from_east is None:
        return from_west
    if from_west is None:
        return from_east
    mask = west_mask(tile, sub)
    return jnp.where(mask, from_east, from_west) if reverse else jnp.where(mask, from_west, from_east)


def pick(tile, sub, north, south):
    mask = north_mask(tile, sub)
    if mask is None:
        return north if tile in NORTH else south
    if north is None and south is None:
        return None
    return jnp.where(mask, 0.0 if north is None else north, 0.0 if south is None else south)


def plus(value, other):
    return value if other is None else value + other


def times(factor, value):
    return None if value is None else factor * value


def speed(tile, sub, courant, group):
    first, second = courant[2 * group], courant[2 * group + 1]
    if tile == 4:
        return jnp.where(sub < 4, first, second)
    return jnp.full((SUB, W), first if tile < 4 else second, F32)


def lanes(row):
    return pl.ds(row * W, W)


def column(row):
    return pl.ds((row + 2) * W, W)


def bins(group, tile):
    return pl.ds(pl.multiple_of(group * GROUP + tile * SUB, SUB), SUB)


def total(value):
    return jnp.sum(value, axis=0, keepdims=True)


def full(value):
    return jnp.broadcast_to(value, (SUB, W))


def loop(low, high, by, body, init):
    def passes(index, carry):
        for k in range(by):
            carry = body(low + index * by + k, carry)
        return carry

    return lax.fori_loop(0, (high - low) // by, passes, init)


def whole(memory=pltpu.VMEM):
    return pl.BlockSpec(memory_space=memory)


def call(kernel, name, inputs, outputs, scratch=(), smem=(), away=(), out_away=(), aliases=None, cost=0):
    specs, operands = [], []
    for place, (value, resident) in enumerate(inputs):
        specs.append(whole(pltpu.SMEM if place in smem else pl.ANY if place in away else pltpu.VMEM))
        operands.append(pltpu.with_memory_space_constraint(value, pltpu.VMEM) if resident else value)
    shapes = [pltpu.VMEM(shape, F32) if resident else jax.ShapeDtypeStruct(shape, F32) for shape, resident in outputs]
    return pl.pallas_call(
        kernel,
        in_specs=specs,
        out_specs=[whole(pl.ANY if place in out_away else pltpu.VMEM) for place in range(len(outputs))],
        out_shape=shapes,
        scratch_shapes=list(scratch),
        input_output_aliases=aliases or {},
        compiler_params=pltpu.CompilerParams(vmem_limit_bytes=LIMIT),
        cost_estimate=pl.CostEstimate(flops=cost, bytes_accessed=cost, transcendentals=0) if cost else None,
        name=name,
    )(*operands)


def pack_rows(cell, put, sub, north):
    both = (sub < 2) | ((sub >= 4) & (sub < 6))
    for row in range(2):
        rest = []
        for half in range(2):
            for place, tile in enumerate((0, 1, 5) if north else (3, 7, 8)):
                put(half * 4 + place, row, cell(half, tile, row))
            second, fourth, sixth = [cell(half, tile, row) for tile in (2, 4, 6)]
            if north:
                put(half * 4 + 3, row, jnp.where(sub < 2, second, jnp.where(sub < 4, sixth, fourth)))
                rest.append(sixth)
            else:
                put(half * 4 + 3, row, jnp.where(sub < 4, fourth, second))
                rest.append(jnp.where(sub < 4, second, sixth))
        other = pltpu.roll(rest[1], 2, 0)
        put(8, row, jnp.where(both, rest[0], other) if north else jnp.where(both, other, rest[0]))


def pack_all(cells, base, sea, out, low, high, north):
    sub = sublane()

    def step(pair, carry):
        def cell(half, tile, row):
            return cells[2 * pair + half, pl.ds(tile * SUB, SUB), pl.ds(base + row * W, W)] * sea[row]

        def put(tile, row, value):
            out[pl.ds(pl.multiple_of(pair * GROUP + tile * SUB, SUB), SUB), lanes(row)] = value

        pack_rows(cell, put, sub, north)
        return carry

    loop(low, high, high - low, step, 0)


def pack_small(out, wind, sea, base):
    here = pl.ds(base * W, 2 * W)
    out[pl.ds(HALF, SUB), :] = jnp.zeros((SUB, 2 * W), F32)
    out[HALF : HALF + 2, :] = wind[:, here]
    out[HALF + 2 : HALF + 3, :] = sea[:, here].astype(F32)


def far_kernel(field, sea_in, wind_in, out, cells, sea, wind, sems):
    even = lax.rem(lax.axis_index("geo"), 2) == 0
    each = GROUPS // 3
    small = [
        pltpu.make_async_copy(sea_in, sea, sems.at[6]),
        pltpu.make_async_copy(wind_in, wind, sems.at[7]),
    ]

    def bring(first, lane):
        copies = []
        for c in range(3):
            for run in range(2):
                here, rows = pl.ds(c * each, each), pl.ds((first + 4 * run) * SUB, 3 * SUB)
                copies.append(
                    pltpu.make_async_copy(
                        field.at[here, rows, pl.ds(lane, 2 * W)], cells.at[here, rows], sems.at[2 * c + run]
                    )
                )
        return copies

    @pl.when(even)
    def _():
        for copy in bring(2, 0):
            copy.start()

    @pl.when(jnp.logical_not(even))
    def _():
        for copy in bring(0, 2 * W):
            copy.start()

    copies = bring(0, 0)
    for copy in small:
        copy.start()
    for copy in small:
        copy.wait()
    for c in range(3):
        copies[2 * c].wait()
        copies[2 * c + 1].wait()

        @pl.when(even)
        def _():
            mask = [full(sea[:, lanes(r)].astype(F32)) for r in (0, 1)]
            pack_all(cells, 0, mask, out, c * each // 2, (c + 1) * each // 2, False)

        @pl.when(jnp.logical_not(even))
        def _():
            mask = [full(sea[:, lanes(r)].astype(F32)) for r in (2, 3)]
            pack_all(cells, 0, mask, out, c * each // 2, (c + 1) * each // 2, True)

    @pl.when(even)
    def _():
        pack_small(out, wind, sea, 0)

    @pl.when(jnp.logical_not(even))
    def _():
        pack_small(out, wind, sea, 2)


def far_rows(field, sea, wind):
    return call(
        far_kernel,
        "far",
        [(pltpu.with_memory_space_constraint(value, pltpu.HBM), False) for value in (field, sea, wind)],
        [(HALO, False)],
        [
            pltpu.VMEM((GROUPS, GROUP, 2 * W), F32),
            pltpu.VMEM((1, ROWS * W), jnp.int32),
            pltpu.VMEM((2, ROWS * W), F32),
            pltpu.SemaphoreType.DMA((8,)),
        ],
        away=(0, 1, 2),
    )[0]


def near_kernel(cells, sea_in, wind, after, out):
    even = lax.rem(lax.axis_index("geo"), 2) == 0

    def rows(base, north):
        mask = [full(sea_in[:, lanes(base + r)].astype(F32)) for r in range(2)]
        pack_all(cells, base * W, mask, out, 0, GROUPS // 2, north)
        pack_small(out, wind, sea_in, base)

    @pl.when(even)
    def _():
        rows(2, True)

    @pl.when(jnp.logical_not(even))
    def _():
        rows(0, False)


def near_rows(field, sea, wind, own):
    return call(near_kernel, "near", [(field, True), (sea, False), (wind, False), (own, True)], [(HALO, False)])[0]


def unpack_north(halo, pair, half, row, sub):
    def get(tile):
        return halo[pl.ds(pl.multiple_of(pair * GROUP + tile * SUB, SUB), SUB), lanes(row)]

    mixed, last = get(half * 4 + 3), get(8)
    if half:
        last = pltpu.roll(last, 6, 0)
    return {
        0: get(half * 4),
        1: get(half * 4 + 1),
        2: mixed,
        4: mixed,
        5: get(half * 4 + 2),
        6: jnp.where((sub >= 2) & (sub < 4), mixed, last),
    }


def unpack_south(halo, pair, half, row, sub):
    def get(tile):
        return halo[pl.ds(pl.multiple_of(pair * GROUP + tile * SUB, SUB), SUB), lanes(row)]

    mixed, last = get(half * 4 + 3), get(8)
    if half:
        last = pltpu.roll(last, 6, 0)
    return {
        2: jnp.where(sub < 4, last, mixed),
        3: get(half * 4),
        4: mixed,
        6: last,
        7: get(half * 4 + 1),
        8: get(half * 4 + 2),
    }


def pieces(value):
    high = value.astype(BF16)
    value = value - high.astype(F32)
    middle = value.astype(BF16)
    return high, middle, (value - middle.astype(F32)).astype(BF16)


def spread(inputs, outputs, flat):
    flat[...] = jnp.zeros_like(flat)
    for place, (row, scale) in enumerate(inputs):
        for k, piece in enumerate(pieces(row[...] * scale)):
            flat[3 * place + k : 3 * place + k + 1, 0:NB] = piece.astype(F32)
    count = len(outputs)
    shape = (flat.shape[0], count * W)
    row, lane = lax.broadcasted_iota(jnp.int32, shape, 0), lax.broadcasted_iota(jnp.int32, shape, 1)
    mask = jnp.zeros(shape, F32)
    for place in range(count):
        mine = (row >= 3 * place) & (row < 3 * place + 3) & (lane >= place * W) & (lane < place * W + W)
        mask = jnp.where(mine, 1.0, mask)
    wide = lax.dot_general(
        flat[...].astype(BF16), mask.astype(BF16), (((0,), (0,)), ((), ())), preferred_element_type=F32
    )
    for place, out in enumerate(outputs):
        out[...] = wide[0:NB, place * W : (place + 1) * W]


def layout(rows, ranks):
    lines = -(-max(2, 2 * rows // ranks) // 3)
    return lines, -(-(lines + 2) // SUB) * SUB


def sort(owner, point, value, weight, ranks):
    rows = owner.shape[1]
    lines, block = layout(rows, ranks)
    hits = owner[...] == lax.broadcasted_iota(jnp.int32, (ranks, rows), 0)
    before = lax.broadcasted_iota(jnp.int32, (rows, rows), 0) < lax.broadcasted_iota(jnp.int32, (rows, rows), 1)
    counts = jnp.dot(hits.astype(F32).astype(BF16), before.astype(F32).astype(BF16), preferred_element_type=F32)
    order = jnp.sum(jnp.where(hits, counts, 0.0), axis=0, keepdims=True).astype(jnp.int32)
    line = (order * 171) >> 9
    third = order - 3 * line
    target = owner[...] * block + line
    spots = lax.broadcasted_iota(jnp.int32, (ranks * block, rows), 0)
    places = [((target == spots) & (third == k)).astype(F32).astype(BF16) for k in range(3)]
    load = jnp.concatenate(
        [
            value[...] * weight[...],
            weight[...],
            point[...].astype(F32),
            jnp.zeros((LOAD - NF - 2, rows), F32),
        ],
        axis=0,
    )
    loads = [
        jnp.concatenate(
            [jnp.zeros((LOAD * k, rows), F32)] * (k > 0) + [load, jnp.zeros((W - LOAD * (k + 1), rows), F32)], axis=0
        )
        for k in range(3)
    ]
    places = jnp.concatenate(places, axis=1)
    result = 0.0
    for piece in zip(*[pieces(part) for part in loads]):
        result = result + lax.dot_general(
            places, jnp.concatenate(piece, axis=1), (((1,), (1,)), ((), ())), preferred_element_type=F32
        )
    return result


def local_kernel(
    cells, sea_in, courant, rate_in, damp_in, steep_in, table,
    flow, rate, damp, steep, centre, ahead, back, across, own, flat,
):
    sub = sublane()
    spread(((rate_in, LOG2E), (damp_in, LOG2E), (steep_in, 1.0)), (rate, damp, steep), flat)
    sea = [full(sea_in[:, lanes(r)].astype(F32)) for r in range(ROWS)]
    zero = jnp.zeros((SUB, W), F32)

    def step(group, sums):
        sums = list(sums)
        for tile in range(TILES):
            rows, spot = pl.ds(tile * SUB, SUB), bins(group, tile)
            pace = speed(tile, sub, courant, group)
            middle = 1.0 - pace * table[0, rows, :]
            over = pace * table[1, rows, :]
            along = pace * table[2, rows, :]
            centre[spot, :] = middle
            across[spot, :] = over
            ahead[spot, :] = along
            back[spot, :] = pace * table[3, rows, :]
            heavy = steep[spot, :]
            cell = {r: cells[group, rows, lanes(r)] * sea[r] for r in range(ROWS)}
            for r in range(ROWS):
                moved = middle * cell[r] + along * side(tile, sub, cell[r], False)
                moved = plus(moved, times(over, pick(tile, sub, cell.get(r - 1), cell.get(r + 1))))
                flow[group, rows, lanes(r)] = moved
                sums[r] = sums[r] + heavy * moved
            gone = heavy * over
            if tile in NORTH:
                sums[ROWS] = sums[ROWS] + pick(tile, sub, gone * cell[ROWS - 1], None)
            if tile in SOUTH:
                sums[ROWS + 1] = sums[ROWS + 1] + pick(tile, sub, None, gone * cell[0])
        return tuple(sums)

    sums = loop(0, GROUPS, 6, step, (zero,) * (ROWS + 2))
    sums = [total(value) for value in sums]
    own[...] = jnp.zeros_like(own)
    for r in range(ROWS):
        own[0:1, lanes(r)] = sums[r] * sea[r][0:1, :]
    own[1:2, lanes(ROWS - 1)] = sums[ROWS]
    own[1:2, lanes(0)] = sums[ROWS + 1]


def local(field, sea, courant, rate, damp, steep, table):
    return call(
        local_kernel,
        "local",
        [(field, True)] + [(arg, False) for arg in (sea, courant, rate, damp, steep, table)],
        [(CELLS, True)] + [(BINS, True)] * 7 + [((SUB, ROWS * W), True)],
        [pltpu.VMEM((16, 11 * W), F32)],
        smem=(2,),
    )


def settle(arrived, wanted, gain, ranks, rows):
    lines, block = layout(rows, ranks)
    size = ranks * block
    shape = (size, W)
    lane = lax.broadcasted_iota(jnp.int32, shape, 1)
    held = lax.rem(lax.broadcasted_iota(jnp.int32, shape, 0), block) < lines
    load = jnp.where(held, arrived[...], 0.0)
    spots = lax.broadcasted_iota(jnp.int32, (size, ROWS * W), 1)
    sums = 0.0
    for k in range(3):
        mine = pltpu.roll(load, W - LOAD * k, 1) if k else load
        point = mine[:, NF + 1 : NF + 2].astype(jnp.int32)
        hits = (point == spots).astype(F32).astype(BF16)
        high, middle, low = [piece.astype(F32) for piece in pieces(jnp.where(lane < LOAD, mine, 0.0))]
        mine = high + pltpu.roll(middle, LOAD, 1) + pltpu.roll(low, 2 * LOAD, 1)
        sums = sums + lax.dot_general(
            mine.astype(BF16), hits, (((0,), (0,)), ((), ())), preferred_element_type=F32
        )
    sums = sums[0:LOAD] + sums[LOAD : 2 * LOAD] + sums[2 * LOAD : 3 * LOAD]
    for f in range(NF):
        rows_of = slice(4 * (f % 2), 4 * (f % 2) + 4)
        wanted[f // 2, rows_of, :] = jnp.broadcast_to(sums[f : f + 1, :] * (1.0 / ND), (4, ROWS * W))
    gain[...] = jnp.broadcast_to(sums[NF : NF + 1, :] * (1.0 / (ND * ND)), gain.shape)


def middle_kernel(
    flow, own, wind, sea_in, rate, damp, steep, centre, ahead, across, owner, point, value, weight, after,
    next_, factor, moved, state, slots, *, ranks,
):
    sub = sublane()
    slots[...] = sort(owner, point, value, weight, ranks)
    _, block = layout(owner.shape[1], ranks)
    me = lax.axis_index("geo")

    def hand(row, dest):
        last = pl.ds(pl.multiple_of(dest * block + block - SUB, SUB), SUB)
        values = jnp.where(sub == SUB - 2, own[0:1, lanes(row)], slots[last, :])
        slots[last, :] = jnp.where(sub == SUB - 1, own[1:2, lanes(row)], values)

    @pl.when(me < ranks - 1)
    def _():
        hand(ROWS - 1, me + 1)

    @pl.when(me > 0)
    def _():
        hand(0, me - 1)

    state[...] = jnp.zeros_like(state)
    here = pl.ds(2 * W, ROWS * W)
    state[WIND0 : WIND0 + 1, here] = wind[0:1, :]
    state[WIND1 : WIND1 + 1, here] = wind[1:2, :]
    state[SEA : SEA + 1, here] = sea_in[...].astype(F32)
    state[STEEP0 : STEEP0 + 1, here] = jnp.where(state[SEA : SEA + 1, here] > 0.5, own[0:1, :], LAND)
    steep0 = {r: full(state[STEEP0 : STEEP0 + 1, column(r)]) for r in (1, 2)}
    wind0 = {r: full(state[WIND0 : WIND0 + 1, column(r)]) for r in (1, 2)}

    def step(group, sums):
        sums = list(sums)
        for tile in range(TILES):
            rows, spot = pl.ds(tile * SUB, SUB), bins(group, tile)
            grow, fade, heavy = rate[spot, :], damp[spot, :], steep[spot, :]
            middle, along, over = centre[spot, :], ahead[spot, :], across[spot, :]
            cell, new = {}, {}
            for r in (1, 2):
                gained = jnp.exp2(grow * wind0[r] - fade * steep0[r])
                factor[group, rows, lanes(r)] = gained
                cell[r] = flow[group, rows, lanes(r)] * gained
                next_[group, rows, lanes(r)] = cell[r]
                new[r] = middle * cell[r] + along * side(tile, sub, cell[r], False)
            new[1] = plus(new[1], pick(tile, sub, None, over * cell[2]))
            new[2] = plus(new[2], pick(tile, sub, over * cell[1], None))
            if tile in SOUTH:
                new[0] = pick(tile, sub, None, over * cell[1])
            if tile in NORTH:
                new[3] = pick(tile, sub, over * cell[2], None)
            for r, value in new.items():
                moved[group, rows, lanes(r)] = value
                sums[r] = sums[r] + heavy * value
        return tuple(sums)

    sums = loop(0, GROUPS, 6, step, (jnp.zeros((SUB, W), F32),) * ROWS)
    for r in range(ROWS):
        state[STEEP1 : STEEP1 + 1, column(r)] = total(sums[r])


def middle(flow, own, wind, sea, coefficients, observed, after, ranks):
    _, block = layout(observed[0].shape[1], ranks)

    def kernel(*refs):
        middle_kernel(*refs, ranks=ranks)

    inputs = [(flow, True), (own, True), (wind, False), (sea, False)]
    inputs += [(value, True) for value in coefficients] + [(value, False) for value in observed + (after,)]
    return call(
        kernel,
        "middle",
        inputs,
        [(CELLS, True)] * 3 + [(STATE, True), ((ranks * block, W), False)],
        away=(len(inputs) - 1,),
        aliases={0: 0},
    )


def split_lam(lam, group, tile, where):
    if tile < 4:
        return lam[group, 0:1, where]
    if tile > 4:
        return lam[group, 4:5, where]
    return lam[group, :, where]


def late_kernel(
    next_in, factor_in, moved_in, from_far, from_near, arrived, own, state_in,
    rate, damp, steep, centre, ahead, back, across,
    next_, factor, moved, next_south, next_north, edges, state, send_b, lam, growth, partial, wanted, gain,
    *, ranks, held_rows,
):
    sub = sublane()
    zero = jnp.zeros((SUB, W), F32)
    even = lax.rem(lax.axis_index("geo"), 2) == 0
    state[...] = state_in[...]
    settle(arrived, wanted, gain, ranks, held_rows)

    def held(place, r):
        return full(state[place : place + 1, column(r)])

    def first(pair, sums, halo_south, halo_north, steep0, wind0):
        sums = list(sums)
        for half in range(2):
            group = 2 * pair + half
            ghosts = {
                -2: unpack_north(halo_south, pair, half, 0, sub),
                -1: unpack_north(halo_south, pair, half, 1, sub),
                4: unpack_south(halo_north, pair, half, 0, sub),
                5: unpack_south(halo_north, pair, half, 1, sub),
            }
            for tile in range(TILES):
                rows, spot = pl.ds(tile * SUB, SUB), bins(group, tile)
                grow, fade, heavy = rate[spot, :], damp[spot, :], steep[spot, :]
                middle, along, over = centre[spot, :], ahead[spot, :], across[spot, :]
                for near, far, mine, second, north in ((-1, -2, 0, 1, True), (4, 5, 3, 2, False)):
                    inward = tile in (NORTH if north else SOUTH)
                    held_back = tile in (SOUTH if north else NORTH)

                    def only(value):
                        return pick(tile, sub, value, None) if north else pick(tile, sub, None, value)

                    here = next_in[group, rows, lanes(mine)]
                    if inward:
                        cell = ghosts[near][tile]
                        gained = jnp.exp2(grow * wind0[near] - fade * steep0[near])
                        value = middle * cell + along * side(tile, sub, cell, False) + over * ghosts[far][tile]
                        value = value * gained
                        (next_south if north else next_north)[group, rows, :] = value
                        here = here + only(over * cell)
                    gained = jnp.exp2(grow * wind0[mine] - fade * steep0[mine])
                    factor[group, rows, lanes(mine)] = gained
                    here = here * gained
                    next_[group, rows, lanes(mine)] = here
                    change = middle * here + along * side(tile, sub, here, False)
                    if inward:
                        change = change + only(over * value)
                    sums[mine] = sums[mine] + heavy * change
                    if held_back:
                        change = change + moved_in[group, rows, lanes(mine)]
                    moved[group, rows, lanes(mine)] = change
                    if inward:
                        change = only(over * here)
                        sums[second] = sums[second] + heavy * change
                        moved[group, rows, lanes(second)] = moved_in[group, rows, lanes(second)] + change
        return tuple(sums)

    def halo_terms(halo_south, halo_north, south, north):
        for halo, rows in ((halo_south, (-2, -1)), (halo_north, (4, 5))):
            here = pl.ds((rows[0] + 2) * W, 2 * W)
            for place, name in enumerate((WIND0, WIND1, SEA)):
                state[name : name + 1, here] = halo[HALF + place : HALF + place + 1, :]
        steeps = {
            -1: south[0] + own[1:2, lanes(0)],
            0: own[0:1, lanes(0)] + south[1],
            3: own[0:1, lanes(3)] + north[1],
            4: north[0] + own[1:2, lanes(3)],
        }
        for r, value in steeps.items():
            known = state[SEA : SEA + 1, column(r)] > 0.5
            state[STEEP0 : STEEP0 + 1, column(r)] = jnp.where(known, value, LAND)
        steep0 = {r: held(STEEP0, r) for r in steeps}
        wind0 = {r: held(WIND0, r) for r in steeps}

        def step(pair, sums):
            return first(pair, sums, halo_south, halo_north, steep0, wind0)

        sums = loop(0, GROUPS // 2, 9, step, (zero,) * ROWS)
        for r in range(ROWS):
            partial[r] = sums[r]

    _, block = layout(held_rows, ranks)
    me = lax.axis_index("geo")

    def sent(source, there):
        source = jnp.clip(source, 0, ranks - 1)
        last = pl.ds(pl.multiple_of(source * block + block - SUB, SUB), SUB)
        values = jnp.where(there, arrived[last, :], 0.0)
        return values[SUB - 2 : SUB - 1, :], values[SUB - 1 : SUB, :]

    @pl.when(even)
    def _():
        halo_terms(from_far, from_near, sent(me - 1, me > 0), sent(me + 1, me < ranks - 1))

    @pl.when(jnp.logical_not(even))
    def _():
        halo_terms(from_near, from_far, sent(me - 1, me > 0), sent(me + 1, me < ranks - 1))

    for r in range(ROWS):
        value = state[STEEP1 : STEEP1 + 1, column(r)] + total(partial[r])
        state[STEEP1 : STEEP1 + 1, column(r)] = jnp.where(state[SEA : SEA + 1, column(r)] > 0.5, value, LAND)
    steep1 = [held(STEEP1, r) for r in range(ROWS)]
    wind1 = [held(WIND1, r) for r in range(ROWS)]
    gains = [gain[:, lanes(r)] for r in range(ROWS)]

    def second(group, sums):
        sums = list(sums)
        means = [[None, None] for _ in range(ROWS)]
        ups = [[None, None] for _ in range(ROWS)]
        downs = [[None, None] for _ in range(ROWS)]
        for tile in range(TILES):
            rows, spot = pl.ds(tile * SUB, SUB), bins(group, tile)
            grow, fade = rate[spot, :], damp[spot, :]
            for r in range(ROWS):
                value = jnp.exp2(grow * wind1[r] - fade * steep1[r])
                growth[group, rows, lanes(r)] = value
                value = value * moved[group, rows, lanes(r)]
                for parts, term in ((means, value), (ups, grow * value), (downs, fade * value)):
                    if tile == 4:
                        parts[r][0] = plus(jnp.where(sub < 4, term, 0.0), parts[r][0])
                        parts[r][1] = jnp.where(sub < 4, 0.0, term)
                    else:
                        f = 0 if tile < 4 else 1
                        parts[r][f] = plus(term, parts[r][f])
        for r in range(ROWS):
            one, two = means[r]
            one = one + pltpu.roll(one, 4, 0)
            two = two + pltpu.roll(two, 4, 0)
            both = jnp.where(sub < 4, one, two)
            both = both + jnp.where((sub & 2) == 0, pltpu.roll(both, 6, 0), pltpu.roll(both, 2, 0))
            both = both + jnp.where((sub & 1) == 0, pltpu.roll(both, 7, 0), pltpu.roll(both, 1, 0))
            value = gains[r] * both - wanted[group, :, lanes(r)]
            lam[group, :, lanes(r)] = value
            up, down = value[0:1, :], value[4:5, :]
            sums[r] = sums[r] + (up * ups[r][0] + down * ups[r][1])
            sums[ROWS + r] = sums[ROWS + r] + (up * downs[r][0] + down * downs[r][1])
        return tuple(sums)

    sums = loop(0, GROUPS, 6, second, (zero,) * (2 * ROWS))
    for r in range(ROWS):
        state[GRAD1 : GRAD1 + 1, column(r)] = total(sums[r]) * LN2
        state[TEND1 : TEND1 + 1, column(r)] = total(sums[ROWS + r]) * (-LN2)
    tend1 = [held(TEND1, r) for r in range(ROWS)]

    def third(group, sums):
        sums = list(sums)
        for tile in range(TILES):
            rows, spot = pl.ds(tile * SUB, SUB), bins(group, tile)
            grow, fade, heavy = rate[spot, :], damp[spot, :], steep[spot, :]
            middle, along, over = centre[spot, :], back[spot, :], across[spot, :]
            cell = {}
            for r in range(ROWS):
                cell[r] = split_lam(lam, group, tile, lanes(r)) * growth[group, rows, lanes(r)] + heavy * tend1[r]
                moved[group, rows, lanes(r)] = cell[r]
            for place, r in enumerate((0, ROWS - 1)):
                value = middle * cell[r] + along * side(tile, sub, cell[r], True)
                value = plus(value, times(over, pick(tile, sub, cell.get(r + 1), cell.get(r - 1))))
                edges[group, rows, lanes(place)] = value
                value = value * next_[group, rows, lanes(r)]
                sums[place] = sums[place] + grow * value
                sums[2 + place] = sums[2 + place] + fade * value
        return tuple(sums)

    sums = loop(0, GROUPS, 6, third, (zero,) * 4)
    for place, r in enumerate((0, ROWS - 1)):
        state[GRAD0 : GRAD0 + 1, column(r)] = total(sums[place]) * LN2
        state[TEND0 : TEND0 + 1, column(r)] = total(sums[2 + place]) * (-LN2)

    @pl.when(even)
    def _():
        fill(send_b, lam, state, 0)

    @pl.when(jnp.logical_not(even))
    def _():
        fill(send_b, lam, state, 2)


def fill(ref, lam, state, base):
    for f in range(NF):
        ref[f : f + 1, :] = lam[f // 2, 4 * (f % 2) : 4 * (f % 2) + 1, pl.ds(base * W, 2 * W)]
    here = pl.ds((base + 2) * W, 2 * W)
    for place, name in enumerate((STEEP1, TEND1, TEND0, TEND0)):
        ref[NF + place : NF + place + 1, :] = state[name : name + 1, here]


def late(next_, factor, moved, from_far, from_near, arrived, own, state, coefficients, ranks, rows):
    def kernel(*refs):
        late_kernel(*refs, ranks=ranks, held_rows=rows)

    inputs = (next_, factor, moved, from_far, from_near, arrived, own, state) + coefficients
    return call(
        kernel,
        "late",
        [(value, True) for value in inputs],
        [(CELLS, True)] * 3 + [(EDGE, True)] * 2 + [(EDGES, True), (STATE, True), ((NF + 4, 2 * W), False)]
        + [((GROUPS, SUB, ROWS * W), True)],
        [
            pltpu.VMEM(CELLS, F32),
            pltpu.VMEM((ROWS, SUB, W), F32),
            pltpu.VMEM((GROUPS, SUB, ROWS * W), F32),
            pltpu.VMEM((SUB, ROWS * W), F32),
        ],
        aliases={0: 0, 1: 1, 2: 2},
    )


def inner_kernel(
    next_, next_south, next_north, source, state_in, lam, rate, damp, centre, back, across,
    inside, factor_south, factor_north, state, send_a,
):
    sub = sublane()
    zero = jnp.zeros((SUB, W), F32)
    state[...] = state_in[...]
    even = lax.rem(lax.axis_index("geo"), 2) == 0

    @pl.when(even)
    def _():
        fill(send_a, lam, state, 2)

    @pl.when(jnp.logical_not(even))
    def _():
        fill(send_a, lam, state, 0)

    wind0 = {r: full(state[WIND0 : WIND0 + 1, column(r)]) for r in (-1, 4)}
    steep0 = {r: full(state[STEEP0 : STEEP0 + 1, column(r)]) for r in (-1, 4)}

    def step(group, sums):
        sums = list(sums)
        for tile in range(TILES):
            rows, spot = pl.ds(tile * SUB, SUB), bins(group, tile)
            grow, fade = rate[spot, :], damp[spot, :]
            if tile in SOUTH:
                factor_south[group, rows, :] = jnp.exp2(grow * wind0[-1] - fade * steep0[-1])
            if tile in NORTH:
                factor_north[group, rows, :] = jnp.exp2(grow * wind0[4] - fade * steep0[4])
            middle, along, over = centre[spot, :], back[spot, :], across[spot, :]
            cell = {r: source[group, rows, lanes(r)] for r in range(ROWS)}
            for place, r in enumerate((1, 2)):
                value = middle * cell[r] + along * side(tile, sub, cell[r], True)
                value = value + over * pick(tile, sub, cell[r + 1], cell[r - 1])
                inside[group, rows, lanes(place)] = value
                value = value * next_[group, rows, lanes(r)]
                sums[place] = sums[place] + grow * value
                sums[2 + place] = sums[2 + place] + fade * value
            gone = fade * over
            if tile in NORTH:
                value = pick(tile, sub, cell[0] * next_south[group, rows, :], None)
                sums[4] = sums[4] + gone * value
            if tile in SOUTH:
                value = pick(tile, sub, None, cell[3] * next_north[group, rows, :])
                sums[5] = sums[5] + gone * value
        return tuple(sums)

    sums = loop(0, GROUPS, 6, step, (zero,) * 6)
    for place, r in enumerate((1, 2)):
        state[GRAD0 : GRAD0 + 1, column(r)] = total(sums[place]) * LN2
        state[TEND0 : TEND0 + 1, column(r)] = total(sums[2 + place]) * (-LN2)
    state[TEND0 : TEND0 + 1, column(-1)] = total(sums[4]) * (-LN2)
    state[TEND0 : TEND0 + 1, column(4)] = total(sums[5]) * (-LN2)


def inner(*args):
    return call(
        inner_kernel,
        "inner",
        [(arg, True) for arg in args],
        [(EDGES, True), (EDGE, True), (EDGE, True), (STATE, True), ((NF + 4, 2 * W), False)],
        cost=1 << 22,
    )


def last_kernel(
    next_, factor, factor_south, factor_north, edges, inside, state, back_a, back_b, rate, damp, steep, centre, back, across,
    out, grad, rims, low, high, ghosts, lam, cells, sems,
):
    sub = sublane()
    zero = jnp.zeros((SUB, W), F32)
    even = lax.rem(lax.axis_index("geo"), 2) == 0
    ghosts[0] = jnp.where(even, back_b[...], back_a[...])
    ghosts[1] = jnp.where(even, back_a[...], back_b[...])
    for group in range(GROUPS):
        for where in range(2):
            for row in range(2):
                one = ghosts[where, 2 * group : 2 * group + 1, lanes(row)]
                two = ghosts[where, 2 * group + 1 : 2 * group + 2, lanes(row)]
                lam[group, :, lanes(2 * where + row)] = jnp.where(sub < 4, one, two)
    sea = {r: full(state[SEA : SEA + 1, column(r)]) for r in range(-2, 6)}
    wind1, steep1, tend1 = {}, {}, {}
    for r in (-2, -1, 4, 5):
        where, here = (0, lanes(r + 2)) if r < 0 else (1, lanes(r - 4))
        wind1[r] = full(state[WIND1 : WIND1 + 1, column(r)])
        value = ghosts[where, NF : NF + 1, here]
        steep1[r] = full(jnp.where(sea[r][0:1, :] > 0.5, value, LAND))
        tend1[r] = full(ghosts[where, NF + 1 : NF + 2, here])

    def first(group, sums):
        sums = list(sums)
        for tile in range(TILES):
            rows, spot = pl.ds(tile * SUB, SUB), bins(group, tile)
            grow, fade, heavy = rate[spot, :], damp[spot, :], steep[spot, :]
            middle, along, over = centre[spot, :], back[spot, :], across[spot, :]

            def ghost(r):
                value = split_lam(lam, group, tile, lanes(r + 2 if r < 0 else r - 2))
                return value * jnp.exp2(grow * wind1[r] - fade * steep1[r]) + heavy * tend1[r]

            for near, far, mine, place, tiles in ((-1, -2, 0, 0, SOUTH), (4, 5, 3, 1, NORTH)):
                if tile not in tiles:
                    continue
                cell = ghost(near)
                value = middle * cell + along * side(tile, sub, cell, True) + over * ghost(far)
                (low if place == 0 else high)[group, rows, :] = value
                value = over * cell
                value = pick(tile, sub, None, value) if place == 0 else pick(tile, sub, value, None)
                rims[group, rows, lanes(place)] = edges[group, rows, lanes(place)] + value
                value = value * next_[group, rows, lanes(mine)]
                sums[place] = sums[place] + grow * value
                sums[2 + place] = sums[2 + place] + fade * value
        return tuple(sums)

    sums = loop(0, GROUPS, 6, first, (zero,) * 4)
    sums = [total(value) * LN2 for value in sums]
    tend0 = {r: state[TEND0 : TEND0 + 1, column(r)] for r in range(-1, 5)}
    grad0 = [state[GRAD0 : GRAD0 + 1, column(r)] for r in range(ROWS)]
    tend0[0], grad0[0] = tend0[0] - sums[2], grad0[0] + sums[0]
    tend0[3], grad0[3] = tend0[3] - sums[3], grad0[3] + sums[1]
    tend0[-1] = tend0[-1] + ghosts[0, NF + 2 : NF + 3, lanes(1)]
    tend0[4] = tend0[4] + ghosts[1, NF + 2 : NF + 3, lanes(0)]
    for r in range(ROWS):
        grad[0:1, lanes(r)] = grad0[r]
        grad[1:2, lanes(r)] = state[GRAD1 : GRAD1 + 1, column(r)]
    tend0 = {r: full(value) for r, value in tend0.items()}

    def second(group, carry):
        for tile in range(TILES):
            rows, spot = pl.ds(tile * SUB, SUB), bins(group, tile)
            heavy = steep[spot, :]
            middle, along, over = centre[spot, :], back[spot, :], across[spot, :]
            cell = {}
            for r in range(-1, 5):
                if r == -1:
                    if tile not in SOUTH:
                        continue
                    value = low[group, rows, :] * factor_south[group, rows, :]
                elif r == 4:
                    if tile not in NORTH:
                        continue
                    value = high[group, rows, :] * factor_north[group, rows, :]
                else:
                    if r == 0:
                        value = (rims if tile in SOUTH else edges)[group, rows, lanes(0)]
                    elif r == 3:
                        value = (rims if tile in NORTH else edges)[group, rows, lanes(1)]
                    else:
                        value = inside[group, rows, lanes(r - 1)]
                    value = value * factor[group, rows, lanes(r)]
                cell[r] = value + heavy * tend0[r]
            for r in range(ROWS):
                value = middle * cell[r] + along * side(tile, sub, cell[r], True)
                value = value + over * pick(tile, sub, cell.get(r + 1), cell.get(r - 1))
                cells[group, rows, lanes(r)] = sea[r] * value
        return carry

    each = GROUPS // CHUNKS
    copies = []
    for c in range(CHUNKS):
        loop(c * each, (c + 1) * each, 3, second, 0)
        here = pl.ds(c * each, each)
        copies.append(pltpu.make_async_copy(cells.at[here], out.at[here], sems.at[c]))
        copies[c].start()
    for copy in copies:
        copy.wait()


def last(next_, factor, factor_south, factor_north, edges, inside, state, back_a, back_b, coefficients):
    inputs = [(value, True) for value in (next_, factor, factor_south, factor_north, edges, inside, state)]
    inputs += [(back_a, False), (back_b, False)]
    inputs += [(value, True) for value in coefficients]
    return call(
        last_kernel,
        "last",
        inputs,
        [(CELLS, False), ((2, ROWS * W), False)],
        [
            pltpu.VMEM(EDGES, F32),
            pltpu.VMEM(EDGE, F32),
            pltpu.VMEM(EDGE, F32),
            pltpu.VMEM((2, NF + 4, 2 * W), F32),
            pltpu.VMEM((GROUPS, SUB, ROWS * W), F32),
            pltpu.VMEM(CELLS, F32),
            pltpu.SemaphoreType.DMA((CHUNKS,)),
        ],
        out_away=(0,),
    )


def swaps(count):
    near = [(i, i ^ 1) for i in range(count)]
    far = []
    for i in range(1, count - 1, 2):
        far += [(i, i + 1), (i + 1, i)]
    return near, far


def body(
    initial_spectrum,
    wind_forcing,
    sea_mask,
    courant,
    input_rate,
    damping,
    steep_weight,
    obs_owner,
    obs_point,
    obs_value,
    obs_weight,
):
    count = lax.axis_size("geo")
    held = obs_point.shape[0]
    near, far = swaps(count)
    field = initial_spectrum.reshape(CELLS)
    sea = sea_mask.reshape(1, ROWS * W)
    from_far = lax.ppermute(far_rows(field, sea, wind_forcing), "geo", far)
    flow, rate, damp, steep, centre, ahead, back, across, own = local(
        field,
        sea,
        courant,
        input_rate.reshape(1, NB),
        damping.reshape(1, NB),
        steep_weight.reshape(1, NB),
        jnp.asarray(direction_tables()),
    )
    rows = near_rows(field, sea, wind_forcing, own)
    from_near = lax.ppermute(rows, "geo", near)
    next_, factor, moved, state, slots = middle(
        flow, own, wind_forcing, sea, (rate, damp, steep, centre, ahead, across),
        (obs_owner.reshape(1, held), obs_point.reshape(1, held), obs_value.T, obs_weight.reshape(1, held)), rows, count,
    )
    arrived = lax.all_to_all(slots, "geo", split_axis=0, concat_axis=0, tiled=True)
    next_, factor, source, next_south, next_north, edges, state, send_b, lam = late(
        next_, factor, moved, from_far, from_near, arrived, own, state,
        (rate, damp, steep, centre, ahead, back, across), count, held,
    )
    back_b = lax.ppermute(send_b, "geo", far)
    inside, factor_south, factor_north, state, send_a = inner(
        next_, next_south, next_north, source, state, lam, rate, damp, centre, back, across
    )
    back_a = lax.ppermute(send_a, "geo", near)
    out, grad = last(
        next_, factor, factor_south, factor_north, edges, inside, state, back_a, back_b,
        (rate, damp, steep, centre, back, across),
    )
    return grad, out.reshape(NB, ROWS * W)


def solution(mesh):
    return jax.shard_map(
        body,
        mesh=mesh,
        in_specs=(
            P(None, ("groups", "geo")),
            P(None, ("groups", "geo")),
            P(("groups", "geo")),
            P(),
            P(),
            P(),
            P(),
            P(("groups", "geo"), None),
            P(("groups", "geo")),
            P(("groups", "geo"), None),
            P(("groups", "geo")),
        ),
        out_specs=(P(None, ("groups", "geo")), P(None, ("groups", "geo"))),
        check_vma=False,
    )
```

```python
import math

import jax
import jax.numpy as jnp
import numpy as np
from jax import lax
from jax.experimental import pallas as pl
from jax.experimental.pallas import tpu as pltpu
from jax.sharding import PartitionSpec as P

ND = 36
NF = 36
NB = 1296
W = 128
ROWS = 4
SUB = 8
GROUP = 72
TILES = GROUP // SUB
GROUPS = NB // GROUP
CHUNKS = 6
F32 = jnp.float32
BF16 = jnp.bfloat16
LIMIT = 7 * 1024 * 1024
LOG2E = math.log2(math.e)
LN2 = math.log(2.0)
LAND = 1.0e5

CELLS = (GROUPS, GROUP, ROWS * W)
EDGE = (GROUPS, GROUP, W)
EDGES = (GROUPS, GROUP, 2 * W)
BINS = (NB, W)
HALF = NB // 2
HALO = (HALF + SUB, 2 * W)
LOAD = 40
STATE = (16, 8 * W)
STEEP0, WIND0, WIND1, SEA, STEEP1, TEND1, GRAD1, TEND0, GRAD0, PASS0 = range(10)

NORTH = (0, 1, 2, 4, 5, 6)
SOUTH = (2, 3, 4, 6, 7, 8)
FROM_WEST = (0, 4, 8)
FROM_EAST = (2, 6)


def direction_tables():
    angle = np.float32(2.0 * math.pi) * np.arange(ND, dtype=np.float32) / np.float32(ND)
    cosine = np.tile(np.cos(angle), 2)[:, None]
    sine = np.tile(np.sin(angle), 2)[:, None]
    lane = np.arange(W)[None, :]
    east = cosine >= 0
    west_ok = (lane > 0).astype(np.float32)
    east_ok = (lane < W - 1).astype(np.float32)
    one = np.ones((1, W), np.float32)
    forward = np.abs(cosine) * np.where(east, west_ok, east_ok)
    backward = np.abs(cosine) * np.where(east, east_ok, west_ok)
    return np.stack(
        [(np.abs(cosine) + np.abs(sine)) * one, np.abs(sine) * one, forward, backward]
    ).astype(np.float32)


def sublane():
    return lax.broadcasted_iota(jnp.int32, (SUB, W), 0)


def north_mask(tile, sub):
    return {2: sub < 2, 4: sub >= 4, 6: sub < 6}.get(tile)


def west_mask(tile, sub):
    return {1: sub < 1, 3: sub >= 3, 5: sub < 5, 7: sub >= 7}.get(tile)


def side(tile, sub, value, reverse):
    west = tile not in (FROM_WEST if reverse else FROM_EAST)
    east = tile not in (FROM_EAST if reverse else FROM_WEST)
    from_west = pltpu.roll(value, 1, 1) if west else None
    from_east = pltpu.roll(value, W - 1, 1) if east else None
    if from_east is None:
        return from_west
    if from_west is None:
        return from_east
    mask = west_mask(tile, sub)
    return jnp.where(mask, from_east, from_west) if reverse else jnp.where(mask, from_west, from_east)


def pick(tile, sub, north, south):
    mask = north_mask(tile, sub)
    if mask is None:
        return north if tile in NORTH else south
    if north is None and south is None:
        return None
    return jnp.where(mask, 0.0 if north is None else north, 0.0 if south is None else south)


def plus(value, other):
    return value if other is None else value + other


def times(factor, value):
    return None if value is None else factor * value


def speed(tile, sub, courant, group):
    first, second = courant[2 * group], courant[2 * group + 1]
    if tile == 4:
        return jnp.where(sub < 4, first, second)
    return jnp.full((SUB, W), first if tile < 4 else second, F32)


def lanes(row):
    return pl.ds(row * W, W)


def column(row):
    return pl.ds((row + 2) * W, W)


def bins(group, tile):
    return pl.ds(pl.multiple_of(group * GROUP + tile * SUB, SUB), SUB)


def total(value):
    return jnp.sum(value, axis=0, keepdims=True)


def full(value):
    return jnp.broadcast_to(value, (SUB, W))


def loop(low, high, by, body, init):
    def passes(index, carry):
        for k in range(by):
            carry = body(low + index * by + k, carry)
        return carry

    return lax.fori_loop(0, (high - low) // by, passes, init)


def whole(memory=pltpu.VMEM):
    return pl.BlockSpec(memory_space=memory)


def call(kernel, name, inputs, outputs, scratch=(), smem=(), away=(), out_away=(), aliases=None, cost=0):
    specs, operands = [], []
    for place, (value, resident) in enumerate(inputs):
        specs.append(whole(pltpu.SMEM if place in smem else pl.ANY if place in away else pltpu.VMEM))
        operands.append(pltpu.with_memory_space_constraint(value, pltpu.VMEM) if resident else value)
    shapes = [pltpu.VMEM(shape, F32) if resident else jax.ShapeDtypeStruct(shape, F32) for shape, resident in outputs]
    return pl.pallas_call(
        kernel,
        in_specs=specs,
        out_specs=[whole(pl.ANY if place in out_away else pltpu.VMEM) for place in range(len(outputs))],
        out_shape=shapes,
        scratch_shapes=list(scratch),
        input_output_aliases=aliases or {},
        compiler_params=pltpu.CompilerParams(vmem_limit_bytes=LIMIT),
        cost_estimate=pl.CostEstimate(flops=cost, bytes_accessed=cost, transcendentals=0) if cost else None,
        name=name,
    )(*operands)


def pack_rows(cell, put, sub, north):
    both = (sub < 2) | ((sub >= 4) & (sub < 6))
    for row in range(2):
        rest = []
        for half in range(2):
            for place, tile in enumerate((0, 1, 5) if north else (3, 7, 8)):
                put(half * 4 + place, row, cell(half, tile, row))
            second, fourth, sixth = [cell(half, tile, row) for tile in (2, 4, 6)]
            if north:
                put(half * 4 + 3, row, jnp.where(sub < 2, second, jnp.where(sub < 4, sixth, fourth)))
                rest.append(sixth)
            else:
                put(half * 4 + 3, row, jnp.where(sub < 4, fourth, second))
                rest.append(jnp.where(sub < 4, second, sixth))
        other = pltpu.roll(rest[1], 2, 0)
        put(8, row, jnp.where(both, rest[0], other) if north else jnp.where(both, other, rest[0]))


def pack_all(cells, base, sea, out, low, high, north):
    sub = sublane()

    def step(pair, carry):
        def cell(half, tile, row):
            return cells[2 * pair + half, pl.ds(tile * SUB, SUB), pl.ds(base + row * W, W)] * sea[row]

        def put(tile, row, value):
            out[pl.ds(pl.multiple_of(pair * GROUP + tile * SUB, SUB), SUB), lanes(row)] = value

        pack_rows(cell, put, sub, north)
        return carry

    loop(low, high, high - low, step, 0)


def pack_small(out, wind, sea, base):
    here = pl.ds(base * W, 2 * W)
    out[pl.ds(HALF, SUB), :] = jnp.zeros((SUB, 2 * W), F32)
    out[HALF : HALF + 2, :] = wind[:, here]
    out[HALF + 2 : HALF + 3, :] = sea[:, here].astype(F32)


def far_kernel(field, sea_in, wind_in, out, cells, sea, wind, sems):
    even = lax.rem(lax.axis_index("geo"), 2) == 0
    each = GROUPS // 3
    small = [
        pltpu.make_async_copy(sea_in, sea, sems.at[6]),
        pltpu.make_async_copy(wind_in, wind, sems.at[7]),
    ]

    def bring(first, lane):
        copies = []
        for c in range(3):
            for run in range(2):
                here, rows = pl.ds(c * each, each), pl.ds((first + 4 * run) * SUB, 3 * SUB)
                copies.append(
                    pltpu.make_async_copy(
                        field.at[here, rows, pl.ds(lane, 2 * W)], cells.at[here, rows], sems.at[2 * c + run]
                    )
                )
        return copies

    @pl.when(even)
    def _():
        for copy in bring(2, 0):
            copy.start()

    @pl.when(jnp.logical_not(even))
    def _():
        for copy in bring(0, 2 * W):
            copy.start()

    copies = bring(0, 0)
    for copy in small:
        copy.start()
    for copy in small:
        copy.wait()
    for c in range(3):
        copies[2 * c].wait()
        copies[2 * c + 1].wait()

        @pl.when(even)
        def _():
            mask = [full(sea[:, lanes(r)].astype(F32)) for r in (0, 1)]
            pack_all(cells, 0, mask, out, c * each // 2, (c + 1) * each // 2, False)

        @pl.when(jnp.logical_not(even))
        def _():
            mask = [full(sea[:, lanes(r)].astype(F32)) for r in (2, 3)]
            pack_all(cells, 0, mask, out, c * each // 2, (c + 1) * each // 2, True)

    @pl.when(even)
    def _():
        pack_small(out, wind, sea, 0)

    @pl.when(jnp.logical_not(even))
    def _():
        pack_small(out, wind, sea, 2)


def far_rows(field, sea, wind):
    return call(
        far_kernel,
        "far",
        [(pltpu.with_memory_space_constraint(value, pltpu.HBM), False) for value in (field, sea, wind)],
        [(HALO, False)],
        [
            pltpu.VMEM((GROUPS, GROUP, 2 * W), F32),
            pltpu.VMEM((1, ROWS * W), jnp.int32),
            pltpu.VMEM((2, ROWS * W), F32),
            pltpu.SemaphoreType.DMA((8,)),
        ],
        away=(0, 1, 2),
    )[0]


def near_kernel(cells, sea_in, wind, after, out):
    even = lax.rem(lax.axis_index("geo"), 2) == 0

    def rows(base, north):
        mask = [full(sea_in[:, lanes(base + r)].astype(F32)) for r in range(2)]
        pack_all(cells, base * W, mask, out, 0, GROUPS // 2, north)
        pack_small(out, wind, sea_in, base)

    @pl.when(even)
    def _():
        rows(2, True)

    @pl.when(jnp.logical_not(even))
    def _():
        rows(0, False)


def near_rows(field, sea, wind, own):
    return call(near_kernel, "near", [(field, True), (sea, False), (wind, False), (own, True)], [(HALO, False)])[0]


def unpack_north(halo, pair, half, row, sub):
    def get(tile):
        return halo[pl.ds(pl.multiple_of(pair * GROUP + tile * SUB, SUB), SUB), lanes(row)]

    mixed, last = get(half * 4 + 3), get(8)
    if half:
        last = pltpu.roll(last, 6, 0)
    return {
        0: get(half * 4),
        1: get(half * 4 + 1),
        2: mixed,
        4: mixed,
        5: get(half * 4 + 2),
        6: jnp.where((sub >= 2) & (sub < 4), mixed, last),
    }


def unpack_south(halo, pair, half, row, sub):
    def get(tile):
        return halo[pl.ds(pl.multiple_of(pair * GROUP + tile * SUB, SUB), SUB), lanes(row)]

    mixed, last = get(half * 4 + 3), get(8)
    if half:
        last = pltpu.roll(last, 6, 0)
    return {
        2: jnp.where(sub < 4, last, mixed),
        3: get(half * 4),
        4: mixed,
        6: last,
        7: get(half * 4 + 1),
        8: get(half * 4 + 2),
    }


def pieces(value):
    high = value.astype(BF16)
    value = value - high.astype(F32)
    middle = value.astype(BF16)
    return high, middle, (value - middle.astype(F32)).astype(BF16)


def spread(inputs, outputs, flat):
    flat[...] = jnp.zeros_like(flat)
    for place, (row, scale) in enumerate(inputs):
        for k, piece in enumerate(pieces(row[...] * scale)):
            flat[3 * place + k : 3 * place + k + 1, 0:NB] = piece.astype(F32)
    count = len(outputs)
    shape = (flat.shape[0], count * W)
    row, lane = lax.broadcasted_iota(jnp.int32, shape, 0), lax.broadcasted_iota(jnp.int32, shape, 1)
    mask = jnp.zeros(shape, F32)
    for place in range(count):
        mine = (row >= 3 * place) & (row < 3 * place + 3) & (lane >= place * W) & (lane < place * W + W)
        mask = jnp.where(mine, 1.0, mask)
    wide = lax.dot_general(
        flat[...].astype(BF16), mask.astype(BF16), (((0,), (0,)), ((), ())), preferred_element_type=F32
    )
    for place, out in enumerate(outputs):
        out[...] = wide[0:NB, place * W : (place + 1) * W]


def layout(rows, ranks):
    lines = -(-max(2, 2 * rows // ranks) // 3)
    return lines, -(-(lines + 2) // SUB) * SUB


def sort(owner, point, value, weight, ranks):
    rows = owner.shape[1]
    lines, block = layout(rows, ranks)
    hits = owner[...] == lax.broadcasted_iota(jnp.int32, (ranks, rows), 0)
    before = lax.broadcasted_iota(jnp.int32, (rows, rows), 0) < lax.broadcasted_iota(jnp.int32, (rows, rows), 1)
    counts = jnp.dot(hits.astype(F32).astype(BF16), before.astype(F32).astype(BF16), preferred_element_type=F32)
    order = jnp.sum(jnp.where(hits, counts, 0.0), axis=0, keepdims=True).astype(jnp.int32)
    line = (order * 171) >> 9
    third = order - 3 * line
    target = owner[...] * block + line
    spots = lax.broadcasted_iota(jnp.int32, (ranks * block, rows), 0)
    places = [((target == spots) & (third == k)).astype(F32).astype(BF16) for k in range(3)]
    load = jnp.concatenate(
        [
            value[...] * weight[...],
            weight[...],
            point[...].astype(F32),
            jnp.zeros((LOAD - NF - 2, rows), F32),
        ],
        axis=0,
    )
    loads = [
        jnp.concatenate(
            [jnp.zeros((LOAD * k, rows), F32)] * (k > 0) + [load, jnp.zeros((W - LOAD * (k + 1), rows), F32)], axis=0
        )
        for k in range(3)
    ]
    places = jnp.concatenate(places, axis=1)
    result = 0.0
    for piece in zip(*[pieces(part) for part in loads]):
        result = result + lax.dot_general(
            places, jnp.concatenate(piece, axis=1), (((1,), (1,)), ((), ())), preferred_element_type=F32
        )
    return result


def local_kernel(
    cells, sea_in, courant, rate_in, damp_in, steep_in, table,
    flow, rate, damp, steep, centre, ahead, back, across, own, flat,
):
    sub = sublane()
    spread(((rate_in, LOG2E), (damp_in, LOG2E), (steep_in, 1.0)), (rate, damp, steep), flat)
    sea = [full(sea_in[:, lanes(r)].astype(F32)) for r in range(ROWS)]
    zero = jnp.zeros((SUB, W), F32)

    def step(group, sums):
        sums = list(sums)
        for tile in range(TILES):
            rows, spot = pl.ds(tile * SUB, SUB), bins(group, tile)
            pace = speed(tile, sub, courant, group)
            middle = 1.0 - pace * table[0, rows, :]
            over = pace * table[1, rows, :]
            along = pace * table[2, rows, :]
            centre[spot, :] = middle
            across[spot, :] = over
            ahead[spot, :] = along
            back[spot, :] = pace * table[3, rows, :]
            heavy = steep[spot, :]
            cell = {r: cells[group, rows, lanes(r)] * sea[r] for r in range(ROWS)}
            for r in range(ROWS):
                moved = middle * cell[r] + along * side(tile, sub, cell[r], False)
                moved = plus(moved, times(over, pick(tile, sub, cell.get(r - 1), cell.get(r + 1))))
                flow[group, rows, lanes(r)] = moved
                sums[r] = sums[r] + heavy * moved
            gone = heavy * over
            if tile in NORTH:
                sums[ROWS] = sums[ROWS] + pick(tile, sub, gone * cell[ROWS - 1], None)
            if tile in SOUTH:
                sums[ROWS + 1] = sums[ROWS + 1] + pick(tile, sub, None, gone * cell[0])
        return tuple(sums)

    sums = loop(0, GROUPS, GROUPS, step, (zero,) * (ROWS + 2))
    sums = [total(value) for value in sums]
    own[...] = jnp.zeros_like(own)
    for r in range(ROWS):
        own[0:1, lanes(r)] = sums[r] * sea[r][0:1, :]
    own[1:2, lanes(ROWS - 1)] = sums[ROWS]
    own[1:2, lanes(0)] = sums[ROWS + 1]


def local(field, sea, courant, rate, damp, steep, table):
    return call(
        local_kernel,
        "local",
        [(field, True)] + [(arg, False) for arg in (sea, courant, rate, damp, steep, table)],
        [(CELLS, True)] + [(BINS, True)] * 7 + [((SUB, ROWS * W), True)],
        [pltpu.VMEM((16, 11 * W), F32)],
        smem=(2,),
    )


def settle(arrived, wanted, gain, ranks, rows):
    lines, block = layout(rows, ranks)
    size = ranks * block
    shape = (size, W)
    lane = lax.broadcasted_iota(jnp.int32, shape, 1)
    held = lax.rem(lax.broadcasted_iota(jnp.int32, shape, 0), block) < lines
    load = jnp.where(held, arrived[...], 0.0)
    spots = lax.broadcasted_iota(jnp.int32, (size, ROWS * W), 1)
    sums = 0.0
    for k in range(3):
        mine = pltpu.roll(load, W - LOAD * k, 1) if k else load
        point = mine[:, NF + 1 : NF + 2].astype(jnp.int32)
        hits = (point == spots).astype(F32).astype(BF16)
        high, middle, low = [piece.astype(F32) for piece in pieces(jnp.where(lane < LOAD, mine, 0.0))]
        mine = high + pltpu.roll(middle, LOAD, 1) + pltpu.roll(low, 2 * LOAD, 1)
        sums = sums + lax.dot_general(
            mine.astype(BF16), hits, (((0,), (0,)), ((), ())), preferred_element_type=F32
        )
    sums = sums[0:LOAD] + sums[LOAD : 2 * LOAD] + sums[2 * LOAD : 3 * LOAD]
    for f in range(NF):
        rows_of = slice(4 * (f % 2), 4 * (f % 2) + 4)
        wanted[f // 2, rows_of, :] = jnp.broadcast_to(sums[f : f + 1, :] * (1.0 / ND), (4, ROWS * W))
    gain[...] = jnp.broadcast_to(sums[NF : NF + 1, :] * (1.0 / (ND * ND)), gain.shape)


def middle_kernel(
    flow, own, wind, sea_in, rate, damp, steep, centre, ahead, across, owner, point, value, weight, after,
    next_, factor, moved, state, slots, *, ranks,
):
    sub = sublane()
    slots[...] = sort(owner, point, value, weight, ranks)
    _, block = layout(owner.shape[1], ranks)
    me = lax.axis_index("geo")

    def hand(row, dest):
        last = pl.ds(pl.multiple_of(dest * block + block - SUB, SUB), SUB)
        values = jnp.where(sub == SUB - 2, own[0:1, lanes(row)], slots[last, :])
        slots[last, :] = jnp.where(sub == SUB - 1, own[1:2, lanes(row)], values)

    @pl.when(me < ranks - 1)
    def _():
        hand(ROWS - 1, me + 1)

    @pl.when(me > 0)
    def _():
        hand(0, me - 1)

    state[...] = jnp.zeros_like(state)
    here = pl.ds(2 * W, ROWS * W)
    state[WIND0 : WIND0 + 1, here] = wind[0:1, :]
    state[WIND1 : WIND1 + 1, here] = wind[1:2, :]
    state[SEA : SEA + 1, here] = sea_in[...].astype(F32)
    state[STEEP0 : STEEP0 + 1, here] = jnp.where(state[SEA : SEA + 1, here] > 0.5, own[0:1, :], LAND)
    steep0 = {r: full(state[STEEP0 : STEEP0 + 1, column(r)]) for r in (1, 2)}
    wind0 = {r: full(state[WIND0 : WIND0 + 1, column(r)]) for r in (1, 2)}

    def step(group, sums):
        sums = list(sums)
        for tile in range(TILES):
            rows, spot = pl.ds(tile * SUB, SUB), bins(group, tile)
            grow, fade, heavy = rate[spot, :], damp[spot, :], steep[spot, :]
            middle, along, over = centre[spot, :], ahead[spot, :], across[spot, :]
            cell, new = {}, {}
            for r in (1, 2):
                gained = jnp.exp2(grow * wind0[r] - fade * steep0[r])
                factor[group, rows, lanes(r)] = gained
                cell[r] = flow[group, rows, lanes(r)] * gained
                next_[group, rows, lanes(r)] = cell[r]
                new[r] = middle * cell[r] + along * side(tile, sub, cell[r], False)
            new[1] = plus(new[1], pick(tile, sub, None, over * cell[2]))
            new[2] = plus(new[2], pick(tile, sub, over * cell[1], None))
            if tile in SOUTH:
                new[0] = pick(tile, sub, None, over * cell[1])
            if tile in NORTH:
                new[3] = pick(tile, sub, over * cell[2], None)
            for r, value in new.items():
                moved[group, rows, lanes(r)] = value
                sums[r] = sums[r] + heavy * value
        return tuple(sums)

    sums = loop(0, GROUPS, GROUPS, step, (jnp.zeros((SUB, W), F32),) * ROWS)
    for r in range(ROWS):
        state[STEEP1 : STEEP1 + 1, column(r)] = total(sums[r])


def middle(flow, own, wind, sea, coefficients, observed, after, ranks):
    _, block = layout(observed[0].shape[1], ranks)

    def kernel(*refs):
        middle_kernel(*refs, ranks=ranks)

    inputs = [(flow, True), (own, True), (wind, False), (sea, False)]
    inputs += [(value, True) for value in coefficients] + [(value, False) for value in observed + (after,)]
    return call(
        kernel,
        "middle",
        inputs,
        [(CELLS, True)] * 3 + [(STATE, True), ((ranks * block, W), False)],
        away=(len(inputs) - 1,),
        aliases={0: 0},
    )


def split_lam(lam, group, tile, where):
    if tile < 4:
        return lam[group, 0:1, where]
    if tile > 4:
        return lam[group, 4:5, where]
    return lam[group, :, where]


def late_kernel(
    next_in, factor_in, moved_in, from_far, from_near, arrived, own, state_in,
    rate, damp, steep, centre, ahead, back, across,
    next_, factor, moved, next_south, next_north, edges, state, send_b, lam, growth, partial, wanted, gain,
    *, ranks, held_rows,
):
    sub = sublane()
    zero = jnp.zeros((SUB, W), F32)
    even = lax.rem(lax.axis_index("geo"), 2) == 0
    state[...] = state_in[...]
    settle(arrived, wanted, gain, ranks, held_rows)

    def held(place, r):
        return full(state[place : place + 1, column(r)])

    def first(pair, sums, halo_south, halo_north, steep0, wind0):
        sums = list(sums)
        for half in range(2):
            group = 2 * pair + half
            ghosts = {
                -2: unpack_north(halo_south, pair, half, 0, sub),
                -1: unpack_north(halo_south, pair, half, 1, sub),
                4: unpack_south(halo_north, pair, half, 0, sub),
                5: unpack_south(halo_north, pair, half, 1, sub),
            }
            for tile in range(TILES):
                rows, spot = pl.ds(tile * SUB, SUB), bins(group, tile)
                grow, fade, heavy = rate[spot, :], damp[spot, :], steep[spot, :]
                middle, along, over = centre[spot, :], ahead[spot, :], across[spot, :]
                for near, far, mine, second, north in ((-1, -2, 0, 1, True), (4, 5, 3, 2, False)):
                    inward = tile in (NORTH if north else SOUTH)
                    held_back = tile in (SOUTH if north else NORTH)

                    def only(value):
                        return pick(tile, sub, value, None) if north else pick(tile, sub, None, value)

                    here = next_in[group, rows, lanes(mine)]
                    if inward:
                        cell = ghosts[near][tile]
                        gained = jnp.exp2(grow * wind0[near] - fade * steep0[near])
                        value = middle * cell + along * side(tile, sub, cell, False) + over * ghosts[far][tile]
                        value = value * gained
                        (next_south if north else next_north)[group, rows, :] = value
                        here = here + only(over * cell)
                    gained = jnp.exp2(grow * wind0[mine] - fade * steep0[mine])
                    factor[group, rows, lanes(mine)] = gained
                    here = here * gained
                    next_[group, rows, lanes(mine)] = here
                    change = middle * here + along * side(tile, sub, here, False)
                    if inward:
                        change = change + only(over * value)
                    sums[mine] = sums[mine] + heavy * change
                    if held_back:
                        change = change + moved_in[group, rows, lanes(mine)]
                    moved[group, rows, lanes(mine)] = change
                    if inward:
                        change = only(over * here)
                        sums[second] = sums[second] + heavy * change
                        moved[group, rows, lanes(second)] = moved_in[group, rows, lanes(second)] + change
        return tuple(sums)

    def halo_terms(halo_south, halo_north, south, north):
        for halo, rows in ((halo_south, (-2, -1)), (halo_north, (4, 5))):
            here = pl.ds((rows[0] + 2) * W, 2 * W)
            for place, name in enumerate((WIND0, WIND1, SEA)):
                state[name : name + 1, here] = halo[HALF + place : HALF + place + 1, :]
        steeps = {
            -1: south[0] + own[1:2, lanes(0)],
            0: own[0:1, lanes(0)] + south[1],
            3: own[0:1, lanes(3)] + north[1],
            4: north[0] + own[1:2, lanes(3)],
        }
        for r, value in steeps.items():
            known = state[SEA : SEA + 1, column(r)] > 0.5
            state[STEEP0 : STEEP0 + 1, column(r)] = jnp.where(known, value, LAND)
        steep0 = {r: held(STEEP0, r) for r in steeps}
        wind0 = {r: held(WIND0, r) for r in steeps}

        def step(pair, sums):
            return first(pair, sums, halo_south, halo_north, steep0, wind0)

        sums = loop(0, GROUPS // 2, 9, step, (zero,) * ROWS)
        for r in range(ROWS):
            partial[r] = sums[r]

    _, block = layout(held_rows, ranks)
    me = lax.axis_index("geo")

    def sent(source, there):
        source = jnp.clip(source, 0, ranks - 1)
        last = pl.ds(pl.multiple_of(source * block + block - SUB, SUB), SUB)
        values = jnp.where(there, arrived[last, :], 0.0)
        return values[SUB - 2 : SUB - 1, :], values[SUB - 1 : SUB, :]

    @pl.when(even)
    def _():
        halo_terms(from_far, from_near, sent(me - 1, me > 0), sent(me + 1, me < ranks - 1))

    @pl.when(jnp.logical_not(even))
    def _():
        halo_terms(from_near, from_far, sent(me - 1, me > 0), sent(me + 1, me < ranks - 1))

    for r in range(ROWS):
        value = state[STEEP1 : STEEP1 + 1, column(r)] + total(partial[r])
        state[STEEP1 : STEEP1 + 1, column(r)] = jnp.where(state[SEA : SEA + 1, column(r)] > 0.5, value, LAND)
    steep1 = [held(STEEP1, r) for r in range(ROWS)]
    wind1 = [held(WIND1, r) for r in range(ROWS)]
    gains = [gain[:, lanes(r)] for r in range(ROWS)]

    def second(group, sums):
        sums = list(sums)
        means = [[None, None] for _ in range(ROWS)]
        ups = [[None, None] for _ in range(ROWS)]
        downs = [[None, None] for _ in range(ROWS)]
        for tile in range(TILES):
            rows, spot = pl.ds(tile * SUB, SUB), bins(group, tile)
            grow, fade = rate[spot, :], damp[spot, :]
            for r in range(ROWS):
                value = jnp.exp2(grow * wind1[r] - fade * steep1[r])
                growth[group, rows, lanes(r)] = value
                value = value * moved[group, rows, lanes(r)]
                for parts, term in ((means, value), (ups, grow * value), (downs, fade * value)):
                    if tile == 4:
                        parts[r][0] = plus(jnp.where(sub < 4, term, 0.0), parts[r][0])
                        parts[r][1] = jnp.where(sub < 4, 0.0, term)
                    else:
                        f = 0 if tile < 4 else 1
                        parts[r][f] = plus(term, parts[r][f])
        for r in range(ROWS):
            one, two = means[r]
            one = one + pltpu.roll(one, 4, 0)
            two = two + pltpu.roll(two, 4, 0)
            both = jnp.where(sub < 4, one, two)
            both = both + jnp.where((sub & 2) == 0, pltpu.roll(both, 6, 0), pltpu.roll(both, 2, 0))
            both = both + jnp.where((sub & 1) == 0, pltpu.roll(both, 7, 0), pltpu.roll(both, 1, 0))
            value = gains[r] * both - wanted[group, :, lanes(r)]
            lam[group, :, lanes(r)] = value
            up, down = value[0:1, :], value[4:5, :]
            sums[r] = sums[r] + (up * ups[r][0] + down * ups[r][1])
            sums[ROWS + r] = sums[ROWS + r] + (up * downs[r][0] + down * downs[r][1])
        return tuple(sums)

    sums = loop(0, GROUPS, 6, second, (zero,) * (2 * ROWS))
    for r in range(ROWS):
        state[GRAD1 : GRAD1 + 1, column(r)] = total(sums[r]) * LN2
        state[TEND1 : TEND1 + 1, column(r)] = total(sums[ROWS + r]) * (-LN2)
    tend1 = [held(TEND1, r) for r in range(ROWS)]

    def third(group, sums):
        sums = list(sums)
        for tile in range(TILES):
            rows, spot = pl.ds(tile * SUB, SUB), bins(group, tile)
            grow, fade, heavy = rate[spot, :], damp[spot, :], steep[spot, :]
            middle, along, over = centre[spot, :], back[spot, :], across[spot, :]
            cell = {}
            for r in range(ROWS):
                cell[r] = split_lam(lam, group, tile, lanes(r)) * growth[group, rows, lanes(r)] + heavy * tend1[r]
                moved[group, rows, lanes(r)] = cell[r]
            for place, r in enumerate((0, ROWS - 1)):
                value = middle * cell[r] + along * side(tile, sub, cell[r], True)
                value = plus(value, times(over, pick(tile, sub, cell.get(r + 1), cell.get(r - 1))))
                edges[group, rows, lanes(place)] = value
                value = value * next_[group, rows, lanes(r)]
                sums[place] = sums[place] + grow * value
                sums[2 + place] = sums[2 + place] + fade * value
        return tuple(sums)

    sums = loop(0, GROUPS, 6, third, (zero,) * 4)
    for place, r in enumerate((0, ROWS - 1)):
        state[GRAD0 : GRAD0 + 1, column(r)] = total(sums[place]) * LN2
        state[TEND0 : TEND0 + 1, column(r)] = total(sums[2 + place]) * (-LN2)

    @pl.when(even)
    def _():
        fill(send_b, lam, state, 0)

    @pl.when(jnp.logical_not(even))
    def _():
        fill(send_b, lam, state, 2)


def fill(ref, lam, state, base):
    for f in range(NF):
        ref[f : f + 1, :] = lam[f // 2, 4 * (f % 2) : 4 * (f % 2) + 1, pl.ds(base * W, 2 * W)]
    here = pl.ds((base + 2) * W, 2 * W)
    for place, name in enumerate((STEEP1, TEND1, TEND0, TEND0)):
        ref[NF + place : NF + place + 1, :] = state[name : name + 1, here]


def late(next_, factor, moved, from_far, from_near, arrived, own, state, coefficients, ranks, rows):
    def kernel(*refs):
        late_kernel(*refs, ranks=ranks, held_rows=rows)

    inputs = (next_, factor, moved, from_far, from_near, arrived, own, state) + coefficients
    return call(
        kernel,
        "late",
        [(value, True) for value in inputs],
        [(CELLS, True)] * 3 + [(EDGE, True)] * 2 + [(EDGES, True), (STATE, True), ((NF + 4, 2 * W), False)]
        + [((GROUPS, SUB, ROWS * W), True)],
        [
            pltpu.VMEM(CELLS, F32),
            pltpu.VMEM((ROWS, SUB, W), F32),
            pltpu.VMEM((GROUPS, SUB, ROWS * W), F32),
            pltpu.VMEM((SUB, ROWS * W), F32),
        ],
        aliases={0: 0, 1: 1, 2: 2},
    )


def inner_kernel(
    next_, next_south, next_north, source, state_in, lam, rate, damp, centre, back, across,
    inside, factor_south, factor_north, state, send_a,
):
    sub = sublane()
    zero = jnp.zeros((SUB, W), F32)
    state[...] = state_in[...]
    even = lax.rem(lax.axis_index("geo"), 2) == 0

    @pl.when(even)
    def _():
        fill(send_a, lam, state, 2)

    @pl.when(jnp.logical_not(even))
    def _():
        fill(send_a, lam, state, 0)

    wind0 = {r: full(state[WIND0 : WIND0 + 1, column(r)]) for r in (-1, 4)}
    steep0 = {r: full(state[STEEP0 : STEEP0 + 1, column(r)]) for r in (-1, 4)}

    def step(group, sums):
        sums = list(sums)
        for tile in range(TILES):
            rows, spot = pl.ds(tile * SUB, SUB), bins(group, tile)
            grow, fade = rate[spot, :], damp[spot, :]
            if tile in SOUTH:
                factor_south[group, rows, :] = jnp.exp2(grow * wind0[-1] - fade * steep0[-1])
            if tile in NORTH:
                factor_north[group, rows, :] = jnp.exp2(grow * wind0[4] - fade * steep0[4])
            middle, along, over = centre[spot, :], back[spot, :], across[spot, :]
            cell = {r: source[group, rows, lanes(r)] for r in range(ROWS)}
            for place, r in enumerate((1, 2)):
                value = middle * cell[r] + along * side(tile, sub, cell[r], True)
                value = value + over * pick(tile, sub, cell[r + 1], cell[r - 1])
                inside[group, rows, lanes(place)] = value
                value = value * next_[group, rows, lanes(r)]
                sums[place] = sums[place] + grow * value
                sums[2 + place] = sums[2 + place] + fade * value
            gone = fade * over
            if tile in NORTH:
                value = pick(tile, sub, cell[0] * next_south[group, rows, :], None)
                sums[4] = sums[4] + gone * value
            if tile in SOUTH:
                value = pick(tile, sub, None, cell[3] * next_north[group, rows, :])
                sums[5] = sums[5] + gone * value
        return tuple(sums)

    sums = loop(0, GROUPS, 6, step, (zero,) * 6)
    for place, r in enumerate((1, 2)):
        state[GRAD0 : GRAD0 + 1, column(r)] = total(sums[place]) * LN2
        state[TEND0 : TEND0 + 1, column(r)] = total(sums[2 + place]) * (-LN2)
    state[TEND0 : TEND0 + 1, column(-1)] = total(sums[4]) * (-LN2)
    state[TEND0 : TEND0 + 1, column(4)] = total(sums[5]) * (-LN2)


def inner(*args):
    return call(
        inner_kernel,
        "inner",
        [(arg, True) for arg in args],
        [(EDGES, True), (EDGE, True), (EDGE, True), (STATE, True), ((NF + 4, 2 * W), False)],
        cost=1 << 22,
    )


def last_kernel(
    next_, factor, factor_south, factor_north, edges, inside, state, back_a, back_b, rate, damp, steep, centre, back, across,
    out, grad, rims, low, high, ghosts, lam, cells, winds, sems,
):
    sub = sublane()
    zero = jnp.zeros((SUB, W), F32)
    even = lax.rem(lax.axis_index("geo"), 2) == 0
    ghosts[0] = jnp.where(even, back_b[...], back_a[...])
    ghosts[1] = jnp.where(even, back_a[...], back_b[...])
    for group in range(GROUPS):
        for where in range(2):
            for row in range(2):
                one = ghosts[where, 2 * group : 2 * group + 1, lanes(row)]
                two = ghosts[where, 2 * group + 1 : 2 * group + 2, lanes(row)]
                lam[group, :, lanes(2 * where + row)] = jnp.where(sub < 4, one, two)
    sea = {r: full(state[SEA : SEA + 1, column(r)]) for r in range(-2, 6)}
    wind1, steep1, tend1 = {}, {}, {}
    for r in (-2, -1, 4, 5):
        where, here = (0, lanes(r + 2)) if r < 0 else (1, lanes(r - 4))
        wind1[r] = full(state[WIND1 : WIND1 + 1, column(r)])
        value = ghosts[where, NF : NF + 1, here]
        steep1[r] = full(jnp.where(sea[r][0:1, :] > 0.5, value, LAND))
        tend1[r] = full(ghosts[where, NF + 1 : NF + 2, here])

    def first(group, sums):
        sums = list(sums)
        for tile in range(TILES):
            rows, spot = pl.ds(tile * SUB, SUB), bins(group, tile)
            grow, fade, heavy = rate[spot, :], damp[spot, :], steep[spot, :]
            middle, along, over = centre[spot, :], back[spot, :], across[spot, :]

            def ghost(r):
                value = split_lam(lam, group, tile, lanes(r + 2 if r < 0 else r - 2))
                return value * jnp.exp2(grow * wind1[r] - fade * steep1[r]) + heavy * tend1[r]

            for near, far, mine, place, tiles in ((-1, -2, 0, 0, SOUTH), (4, 5, 3, 1, NORTH)):
                if tile not in tiles:
                    continue
                cell = ghost(near)
                value = middle * cell + along * side(tile, sub, cell, True) + over * ghost(far)
                (low if place == 0 else high)[group, rows, :] = value
                value = over * cell
                value = pick(tile, sub, None, value) if place == 0 else pick(tile, sub, value, None)
                rims[group, rows, lanes(place)] = edges[group, rows, lanes(place)] + value
                value = value * next_[group, rows, lanes(mine)]
                sums[place] = sums[place] + grow * value
                sums[2 + place] = sums[2 + place] + fade * value
        return tuple(sums)

    sums = loop(0, GROUPS, 6, first, (zero,) * 4)
    sums = [total(value) * LN2 for value in sums]
    tend0 = {r: state[TEND0 : TEND0 + 1, column(r)] for r in range(-1, 5)}
    grad0 = [state[GRAD0 : GRAD0 + 1, column(r)] for r in range(ROWS)]
    tend0[0], grad0[0] = tend0[0] - sums[2], grad0[0] + sums[0]
    tend0[3], grad0[3] = tend0[3] - sums[3], grad0[3] + sums[1]
    tend0[-1] = tend0[-1] + ghosts[0, NF + 2 : NF + 3, lanes(1)]
    tend0[4] = tend0[4] + ghosts[1, NF + 2 : NF + 3, lanes(0)]
    for r in range(ROWS):
        winds[0:1, lanes(r)] = grad0[r]
        winds[1:2, lanes(r)] = state[GRAD1 : GRAD1 + 1, column(r)]
    sent = pltpu.make_async_copy(winds, grad, sems.at[CHUNKS])
    sent.start()
    tend0 = {r: full(value) for r, value in tend0.items()}

    def second(group, carry):
        for tile in range(TILES):
            rows, spot = pl.ds(tile * SUB, SUB), bins(group, tile)
            heavy = steep[spot, :]
            middle, along, over = centre[spot, :], back[spot, :], across[spot, :]
            cell = {}
            for r in range(-1, 5):
                if r == -1:
                    if tile not in SOUTH:
                        continue
                    value = low[group, rows, :] * factor_south[group, rows, :]
                elif r == 4:
                    if tile not in NORTH:
                        continue
                    value = high[group, rows, :] * factor_north[group, rows, :]
                else:
                    if r == 0:
                        value = (rims if tile in SOUTH else edges)[group, rows, lanes(0)]
                    elif r == 3:
                        value = (rims if tile in NORTH else edges)[group, rows, lanes(1)]
                    else:
                        value = inside[group, rows, lanes(r - 1)]
                    value = value * factor[group, rows, lanes(r)]
                cell[r] = value + heavy * tend0[r]
            for r in range(ROWS):
                value = middle * cell[r] + along * side(tile, sub, cell[r], True)
                value = value + over * pick(tile, sub, cell.get(r + 1), cell.get(r - 1))
                cells[group, rows, lanes(r)] = sea[r] * value
        return carry

    each = GROUPS // CHUNKS
    copies = []
    for c in range(CHUNKS):
        loop(c * each, (c + 1) * each, 3, second, 0)
        here = pl.ds(c * each, each)
        copies.append(pltpu.make_async_copy(cells.at[here], out.at[here], sems.at[c]))
        copies[c].start()
    sent.wait()
    for copy in copies:
        copy.wait()


def last(next_, factor, factor_south, factor_north, edges, inside, state, back_a, back_b, coefficients):
    inputs = [(value, True) for value in (next_, factor, factor_south, factor_north, edges, inside, state)]
    inputs += [(back_a, True), (back_b, True)]
    inputs += [(value, True) for value in coefficients]
    return call(
        last_kernel,
        "last",
        inputs,
        [(CELLS, False), ((2, ROWS * W), False)],
        [
            pltpu.VMEM(EDGES, F32),
            pltpu.VMEM(EDGE, F32),
            pltpu.VMEM(EDGE, F32),
            pltpu.VMEM((2, NF + 4, 2 * W), F32),
            pltpu.VMEM((GROUPS, SUB, ROWS * W), F32),
            pltpu.VMEM(CELLS, F32),
            pltpu.VMEM((2, ROWS * W), F32),
            pltpu.SemaphoreType.DMA((CHUNKS + 1,)),
        ],
        out_away=(0, 1),
    )


def swaps(count):
    near = [(i, i ^ 1) for i in range(count)]
    far = []
    for i in range(1, count - 1, 2):
        far += [(i, i + 1), (i + 1, i)]
    return near, far


def body(
    initial_spectrum,
    wind_forcing,
    sea_mask,
    courant,
    input_rate,
    damping,
    steep_weight,
    obs_owner,
    obs_point,
    obs_value,
    obs_weight,
):
    count = lax.axis_size("geo")
    held = obs_point.shape[0]
    near, far = swaps(count)
    field = initial_spectrum.reshape(CELLS)
    sea = sea_mask.reshape(1, ROWS * W)
    from_far = lax.ppermute(far_rows(field, sea, wind_forcing), "geo", far)
    flow, rate, damp, steep, centre, ahead, back, across, own = local(
        field,
        sea,
        courant,
        input_rate.reshape(1, NB),
        damping.reshape(1, NB),
        steep_weight.reshape(1, NB),
        jnp.asarray(direction_tables()),
    )
    rows = near_rows(field, sea, wind_forcing, own)
    from_near = lax.ppermute(rows, "geo", near)
    next_, factor, moved, state, slots = middle(
        flow, own, wind_forcing, sea, (rate, damp, steep, centre, ahead, across),
        (obs_owner.reshape(1, held), obs_point.reshape(1, held), obs_value.T, obs_weight.reshape(1, held)), rows, count,
    )
    arrived = lax.all_to_all(slots, "geo", split_axis=0, concat_axis=0, tiled=True)
    next_, factor, source, next_south, next_north, edges, state, send_b, lam = late(
        next_, factor, moved, from_far, from_near, arrived, own, state,
        (rate, damp, steep, centre, ahead, back, across), count, held,
    )
    back_b = lax.ppermute(send_b, "geo", far)
    inside, factor_south, factor_north, state, send_a = inner(
        next_, next_south, next_north, source, state, lam, rate, damp, centre, back, across
    )
    back_a = lax.ppermute(send_a, "geo", near)
    out, grad = last(
        next_, factor, factor_south, factor_north, edges, inside, state, back_a, back_b,
        (rate, damp, steep, centre, back, across),
    )
    return grad, out.reshape(NB, ROWS * W)


def solution(mesh):
    return jax.shard_map(
        body,
        mesh=mesh,
        in_specs=(
            P(None, ("groups", "geo")),
            P(None, ("groups", "geo")),
            P(("groups", "geo")),
            P(),
            P(),
            P(),
            P(),
            P(("groups", "geo"), None),
            P(("groups", "geo")),
            P(("groups", "geo"), None),
            P(("groups", "geo")),
        ),
        out_specs=(P(None, ("groups", "geo")), P(None, ("groups", "geo"))),
        check_vma=False,
    )
```

```python
import math

import jax
import jax.numpy as jnp
import numpy as np
from jax import lax
from jax.experimental import pallas as pl
from jax.experimental.pallas import tpu as pltpu
from jax.sharding import PartitionSpec as P

ND = 36
NF = 36
NB = 1296
W = 128
ROWS = 4
SUB = 8
GROUP = 72
TILES = GROUP // SUB
GROUPS = NB // GROUP
CHUNKS = 6
F32 = jnp.float32
BF16 = jnp.bfloat16
LIMIT = 7 * 1024 * 1024
LOG2E = math.log2(math.e)
LN2 = math.log(2.0)
LAND = 1.0e5

CELLS = (GROUPS, GROUP, ROWS * W)
EDGE = (GROUPS, GROUP, W)
EDGES = (GROUPS, GROUP, 2 * W)
BINS = (NB, W)
HALF = NB // 2
HALO = (HALF + SUB, 2 * W)
LOAD = 40
LINES_A = NF + 4
LINES_B = NF + 12
STATE = (16, 8 * W)
STEEP0, WIND0, WIND1, SEA, STEEP1, TEND1, GRAD1, TEND0, GRAD0, PASS0 = range(10)

NORTH = (0, 1, 2, 4, 5, 6)
SOUTH = (2, 3, 4, 6, 7, 8)
FROM_WEST = (0, 4, 8)
FROM_EAST = (2, 6)


def direction_tables():
    angle = np.float32(2.0 * math.pi) * np.arange(ND, dtype=np.float32) / np.float32(ND)
    cosine = np.tile(np.cos(angle), 2)[:, None]
    sine = np.tile(np.sin(angle), 2)[:, None]
    lane = np.arange(W)[None, :]
    east = cosine >= 0
    west_ok = (lane > 0).astype(np.float32)
    east_ok = (lane < W - 1).astype(np.float32)
    one = np.ones((1, W), np.float32)
    forward = np.abs(cosine) * np.where(east, west_ok, east_ok)
    backward = np.abs(cosine) * np.where(east, east_ok, west_ok)
    return np.stack(
        [(np.abs(cosine) + np.abs(sine)) * one, np.abs(sine) * one, forward, backward]
    ).astype(np.float32)


def sublane():
    return lax.broadcasted_iota(jnp.int32, (SUB, W), 0)


def north_mask(tile, sub):
    return {2: sub < 2, 4: sub >= 4, 6: sub < 6}.get(tile)


def west_mask(tile, sub):
    return {1: sub < 1, 3: sub >= 3, 5: sub < 5, 7: sub >= 7}.get(tile)


def side(tile, sub, value, reverse):
    west = tile not in (FROM_WEST if reverse else FROM_EAST)
    east = tile not in (FROM_EAST if reverse else FROM_WEST)
    from_west = pltpu.roll(value, 1, 1) if west else None
    from_east = pltpu.roll(value, W - 1, 1) if east else None
    if from_east is None:
        return from_west
    if from_west is None:
        return from_east
    mask = west_mask(tile, sub)
    return jnp.where(mask, from_east, from_west) if reverse else jnp.where(mask, from_west, from_east)


def pick(tile, sub, north, south):
    mask = north_mask(tile, sub)
    if mask is None:
        return north if tile in NORTH else south
    if north is None and south is None:
        return None
    return jnp.where(mask, 0.0 if north is None else north, 0.0 if south is None else south)


def plus(value, other):
    return value if other is None else value + other


def times(factor, value):
    return None if value is None else factor * value


def speed(tile, sub, courant, group):
    first, second = courant[2 * group], courant[2 * group + 1]
    if tile == 4:
        return jnp.where(sub < 4, first, second)
    return jnp.full((SUB, W), first if tile < 4 else second, F32)


def lanes(row):
    return pl.ds(row * W, W)


def column(row):
    return pl.ds((row + 2) * W, W)


def bins(group, tile):
    return pl.ds(pl.multiple_of(group * GROUP + tile * SUB, SUB), SUB)


def total(value):
    return jnp.sum(value, axis=0, keepdims=True)


def full(value):
    return jnp.broadcast_to(value, (SUB, W))


def loop(low, high, by, body, init):
    def passes(index, carry):
        for k in range(by):
            carry = body(low + index * by + k, carry)
        return carry

    return lax.fori_loop(0, (high - low) // by, passes, init)


def whole(memory=pltpu.VMEM):
    return pl.BlockSpec(memory_space=memory)


def call(kernel, name, inputs, outputs, scratch=(), smem=(), away=(), out_away=(), aliases=None, cost=0):
    specs, operands = [], []
    for place, (value, resident) in enumerate(inputs):
        specs.append(whole(pltpu.SMEM if place in smem else pl.ANY if place in away else pltpu.VMEM))
        operands.append(pltpu.with_memory_space_constraint(value, pltpu.VMEM) if resident else value)
    shapes = [pltpu.VMEM(shape, F32) if resident else jax.ShapeDtypeStruct(shape, F32) for shape, resident in outputs]
    return pl.pallas_call(
        kernel,
        in_specs=specs,
        out_specs=[whole(pl.ANY if place in out_away else pltpu.VMEM) for place in range(len(outputs))],
        out_shape=shapes,
        scratch_shapes=list(scratch),
        input_output_aliases=aliases or {},
        compiler_params=pltpu.CompilerParams(vmem_limit_bytes=LIMIT),
        cost_estimate=pl.CostEstimate(flops=cost, bytes_accessed=cost, transcendentals=0) if cost else None,
        name=name,
    )(*operands)


def pack_rows(cell, put, sub, north):
    both = (sub < 2) | ((sub >= 4) & (sub < 6))
    for row in range(2):
        rest = []
        for half in range(2):
            for place, tile in enumerate((0, 1, 5) if north else (3, 7, 8)):
                put(half * 4 + place, row, cell(half, tile, row))
            second, fourth, sixth = [cell(half, tile, row) for tile in (2, 4, 6)]
            if north:
                put(half * 4 + 3, row, jnp.where(sub < 2, second, jnp.where(sub < 4, sixth, fourth)))
                rest.append(sixth)
            else:
                put(half * 4 + 3, row, jnp.where(sub < 4, fourth, second))
                rest.append(jnp.where(sub < 4, second, sixth))
        other = pltpu.roll(rest[1], 2, 0)
        put(8, row, jnp.where(both, rest[0], other) if north else jnp.where(both, other, rest[0]))


def pack_all(cells, base, sea, out, low, high, north):
    sub = sublane()

    def step(pair, carry):
        def cell(half, tile, row):
            return cells[2 * pair + half, pl.ds(tile * SUB, SUB), pl.ds(base + row * W, W)] * sea[row]

        def put(tile, row, value):
            out[pl.ds(pl.multiple_of(pair * GROUP + tile * SUB, SUB), SUB), lanes(row)] = value

        pack_rows(cell, put, sub, north)
        return carry

    loop(low, high, high - low, step, 0)


def pack_small(out, wind, sea, base):
    here = pl.ds(base * W, 2 * W)
    out[pl.ds(HALF, SUB), :] = jnp.zeros((SUB, 2 * W), F32)
    out[HALF : HALF + 2, :] = wind[:, here]
    out[HALF + 2 : HALF + 3, :] = sea[:, here].astype(F32)


def far_kernel(field, sea_in, wind_in, out, cells, sea, wind, sems):
    even = lax.rem(lax.axis_index("geo"), 2) == 0
    each = GROUPS
    small = [
        pltpu.make_async_copy(sea_in, sea, sems.at[6]),
        pltpu.make_async_copy(wind_in, wind, sems.at[7]),
    ]

    def bring(first, lane):
        copies = []
        for c in range(1):
            for run in range(2):
                here, rows = pl.ds(c * each, each), pl.ds((first + 4 * run) * SUB, 3 * SUB)
                copies.append(
                    pltpu.make_async_copy(
                        field.at[here, rows, pl.ds(lane, 2 * W)], cells.at[here, rows], sems.at[2 * c + run]
                    )
                )
        return copies

    @pl.when(even)
    def _():
        for copy in bring(2, 0):
            copy.start()

    @pl.when(jnp.logical_not(even))
    def _():
        for copy in bring(0, 2 * W):
            copy.start()

    copies = bring(0, 0)
    for copy in small:
        copy.start()
    for copy in small:
        copy.wait()
    for c in range(1):
        copies[2 * c].wait()
        copies[2 * c + 1].wait()

        @pl.when(even)
        def _():
            mask = [full(sea[:, lanes(r)].astype(F32)) for r in (0, 1)]
            pack_all(cells, 0, mask, out, c * each // 2, (c + 1) * each // 2, False)

        @pl.when(jnp.logical_not(even))
        def _():
            mask = [full(sea[:, lanes(r)].astype(F32)) for r in (2, 3)]
            pack_all(cells, 0, mask, out, c * each // 2, (c + 1) * each // 2, True)

    @pl.when(even)
    def _():
        pack_small(out, wind, sea, 0)

    @pl.when(jnp.logical_not(even))
    def _():
        pack_small(out, wind, sea, 2)


def far_rows(field, sea, wind):
    return call(
        far_kernel,
        "far",
        [(pltpu.with_memory_space_constraint(value, pltpu.HBM), False) for value in (field, sea, wind)],
        [(HALO, False)],
        [
            pltpu.VMEM((GROUPS, GROUP, 2 * W), F32),
            pltpu.VMEM((1, ROWS * W), jnp.int32),
            pltpu.VMEM((2, ROWS * W), F32),
            pltpu.SemaphoreType.DMA((8,)),
        ],
        away=(0, 1, 2),
    )[0]


def near_kernel(cells, sea_in, wind, after, out):
    even = lax.rem(lax.axis_index("geo"), 2) == 0

    def rows(base, north):
        mask = [full(sea_in[:, lanes(base + r)].astype(F32)) for r in range(2)]
        pack_all(cells, base * W, mask, out, 0, GROUPS // 2, north)
        pack_small(out, wind, sea_in, base)

    @pl.when(even)
    def _():
        rows(2, True)

    @pl.when(jnp.logical_not(even))
    def _():
        rows(0, False)


def near_rows(field, sea, wind, own):
    return call(near_kernel, "near", [(field, True), (sea, False), (wind, False), (own, True)], [(HALO, False)])[0]


def unpack_north(halo, pair, half, row, sub):
    def get(tile):
        return halo[pl.ds(pl.multiple_of(pair * GROUP + tile * SUB, SUB), SUB), lanes(row)]

    mixed, last = get(half * 4 + 3), get(8)
    if half:
        last = pltpu.roll(last, 6, 0)
    return {
        0: get(half * 4),
        1: get(half * 4 + 1),
        2: mixed,
        4: mixed,
        5: get(half * 4 + 2),
        6: jnp.where((sub >= 2) & (sub < 4), mixed, last),
    }


def unpack_south(halo, pair, half, row, sub):
    def get(tile):
        return halo[pl.ds(pl.multiple_of(pair * GROUP + tile * SUB, SUB), SUB), lanes(row)]

    mixed, last = get(half * 4 + 3), get(8)
    if half:
        last = pltpu.roll(last, 6, 0)
    return {
        2: jnp.where(sub < 4, last, mixed),
        3: get(half * 4),
        4: mixed,
        6: last,
        7: get(half * 4 + 1),
        8: get(half * 4 + 2),
    }


def pieces(value):
    high = value.astype(BF16)
    value = value - high.astype(F32)
    middle = value.astype(BF16)
    return high, middle, (value - middle.astype(F32)).astype(BF16)


def spread(inputs, outputs, flat):
    flat[...] = jnp.zeros_like(flat)
    for place, (row, scale) in enumerate(inputs):
        for k, piece in enumerate(pieces(row[...] * scale)):
            flat[3 * place + k : 3 * place + k + 1, 0:NB] = piece.astype(F32)
    count = len(outputs)
    shape = (flat.shape[0], count * W)
    row, lane = lax.broadcasted_iota(jnp.int32, shape, 0), lax.broadcasted_iota(jnp.int32, shape, 1)
    mask = jnp.zeros(shape, F32)
    for place in range(count):
        mine = (row >= 3 * place) & (row < 3 * place + 3) & (lane >= place * W) & (lane < place * W + W)
        mask = jnp.where(mine, 1.0, mask)
    wide = lax.dot_general(
        flat[...].astype(BF16), mask.astype(BF16), (((0,), (0,)), ((), ())), preferred_element_type=F32
    )
    for place, out in enumerate(outputs):
        out[...] = wide[0:NB, place * W : (place + 1) * W]


def layout(rows, ranks):
    lines = -(-max(2, 2 * rows // ranks) // 3)
    return lines, -(-(lines + 2) // SUB) * SUB


def sort(owner, point, value, weight, ranks):
    rows = owner.shape[1]
    lines, block = layout(rows, ranks)
    hits = owner[...] == lax.broadcasted_iota(jnp.int32, (ranks, rows), 0)
    before = lax.broadcasted_iota(jnp.int32, (rows, rows), 0) < lax.broadcasted_iota(jnp.int32, (rows, rows), 1)
    counts = jnp.dot(hits.astype(F32).astype(BF16), before.astype(F32).astype(BF16), preferred_element_type=F32)
    order = jnp.sum(jnp.where(hits, counts, 0.0), axis=0, keepdims=True).astype(jnp.int32)
    line = (order * 171) >> 9
    third = order - 3 * line
    target = owner[...] * block + line
    spots = lax.broadcasted_iota(jnp.int32, (ranks * block, rows), 0)
    places = [((target == spots) & (third == k)).astype(F32).astype(BF16) for k in range(3)]
    load = jnp.concatenate(
        [
            value[...] * weight[...],
            weight[...],
            point[...].astype(F32),
            jnp.zeros((LOAD - NF - 2, rows), F32),
        ],
        axis=0,
    )
    loads = [
        jnp.concatenate(
            [jnp.zeros((LOAD * k, rows), F32)] * (k > 0) + [load, jnp.zeros((W - LOAD * (k + 1), rows), F32)], axis=0
        )
        for k in range(3)
    ]
    places = jnp.concatenate(places, axis=1)
    result = 0.0
    for piece in zip(*[pieces(part) for part in loads]):
        result = result + lax.dot_general(
            places, jnp.concatenate(piece, axis=1), (((1,), (1,)), ((), ())), preferred_element_type=F32
        )
    return result


def local_kernel(
    cells, sea_in, courant, rate_in, damp_in, steep_in, table,
    flow, rate, damp, steep, centre, ahead, back, across, own, flat,
):
    sub = sublane()
    spread(((rate_in, LOG2E), (damp_in, LOG2E), (steep_in, 1.0)), (rate, damp, steep), flat)
    sea = [full(sea_in[:, lanes(r)].astype(F32)) for r in range(ROWS)]
    zero = jnp.zeros((SUB, W), F32)

    def step(group, sums):
        sums = list(sums)
        for tile in range(TILES):
            rows, spot = pl.ds(tile * SUB, SUB), bins(group, tile)
            pace = speed(tile, sub, courant, group)
            middle = 1.0 - pace * table[0, rows, :]
            over = pace * table[1, rows, :]
            along = pace * table[2, rows, :]
            centre[spot, :] = middle
            across[spot, :] = over
            ahead[spot, :] = along
            back[spot, :] = pace * table[3, rows, :]
            heavy = steep[spot, :]
            cell = {r: cells[group, rows, lanes(r)] * sea[r] for r in range(ROWS)}
            for r in range(ROWS):
                moved = middle * cell[r] + along * side(tile, sub, cell[r], False)
                moved = plus(moved, times(over, pick(tile, sub, cell.get(r - 1), cell.get(r + 1))))
                flow[group, rows, lanes(r)] = moved
                sums[r] = sums[r] + heavy * moved
            gone = heavy * over
            if tile in NORTH:
                sums[ROWS] = sums[ROWS] + pick(tile, sub, gone * cell[ROWS - 1], None)
            if tile in SOUTH:
                sums[ROWS + 1] = sums[ROWS + 1] + pick(tile, sub, None, gone * cell[0])
        return tuple(sums)

    sums = loop(0, GROUPS, GROUPS, step, (zero,) * (ROWS + 2))
    sums = [total(value) for value in sums]
    own[...] = jnp.zeros_like(own)
    for r in range(ROWS):
        own[0:1, lanes(r)] = sums[r] * sea[r][0:1, :]
    own[1:2, lanes(ROWS - 1)] = sums[ROWS]
    own[1:2, lanes(0)] = sums[ROWS + 1]


def local(field, sea, courant, rate, damp, steep, table):
    return call(
        local_kernel,
        "local",
        [(field, True)] + [(arg, False) for arg in (sea, courant, rate, damp, steep, table)],
        [(CELLS, True)] + [(BINS, True)] * 7 + [((SUB, ROWS * W), True)],
        [pltpu.VMEM((16, 11 * W), F32)],
        smem=(2,),
    )


def settle(arrived, wanted, gain, ranks, rows):
    lines, block = layout(rows, ranks)
    size = ranks * block
    shape = (size, W)
    lane = lax.broadcasted_iota(jnp.int32, shape, 1)
    held = lax.rem(lax.broadcasted_iota(jnp.int32, shape, 0), block) < lines
    load = jnp.where(held, arrived[...], 0.0)
    spots = lax.broadcasted_iota(jnp.int32, (size, ROWS * W), 1)
    sums = 0.0
    for k in range(3):
        mine = pltpu.roll(load, W - LOAD * k, 1) if k else load
        point = mine[:, NF + 1 : NF + 2].astype(jnp.int32)
        hits = (point == spots).astype(F32).astype(BF16)
        high, middle, low = [piece.astype(F32) for piece in pieces(jnp.where(lane < LOAD, mine, 0.0))]
        mine = high + pltpu.roll(middle, LOAD, 1) + pltpu.roll(low, 2 * LOAD, 1)
        sums = sums + lax.dot_general(
            mine.astype(BF16), hits, (((0,), (0,)), ((), ())), preferred_element_type=F32
        )
    sums = sums[0:LOAD] + sums[LOAD : 2 * LOAD] + sums[2 * LOAD : 3 * LOAD]
    for f in range(NF):
        rows_of = slice(4 * (f % 2), 4 * (f % 2) + 4)
        wanted[f // 2, rows_of, :] = jnp.broadcast_to(sums[f : f + 1, :] * (1.0 / ND), (4, ROWS * W))
    gain[...] = jnp.broadcast_to(sums[NF : NF + 1, :] * (1.0 / (ND * ND)), gain.shape)


def middle_kernel(
    flow, own, wind, sea_in, rate, damp, steep, centre, ahead, across, owner, point, value, weight, after,
    next_, factor, moved, state, slots, *, ranks,
):
    sub = sublane()
    slots[...] = sort(owner, point, value, weight, ranks)
    _, block = layout(owner.shape[1], ranks)
    me = lax.axis_index("geo")

    def hand(row, dest):
        last = pl.ds(pl.multiple_of(dest * block + block - SUB, SUB), SUB)
        values = jnp.where(sub == SUB - 2, own[0:1, lanes(row)], slots[last, :])
        slots[last, :] = jnp.where(sub == SUB - 1, own[1:2, lanes(row)], values)

    @pl.when(me < ranks - 1)
    def _():
        hand(ROWS - 1, me + 1)

    @pl.when(me > 0)
    def _():
        hand(0, me - 1)

    state[...] = jnp.zeros_like(state)
    here = pl.ds(2 * W, ROWS * W)
    state[WIND0 : WIND0 + 1, here] = wind[0:1, :]
    state[WIND1 : WIND1 + 1, here] = wind[1:2, :]
    state[SEA : SEA + 1, here] = sea_in[...].astype(F32)
    state[STEEP0 : STEEP0 + 1, here] = jnp.where(state[SEA : SEA + 1, here] > 0.5, own[0:1, :], LAND)
    steep0 = {r: full(state[STEEP0 : STEEP0 + 1, column(r)]) for r in (1, 2)}
    wind0 = {r: full(state[WIND0 : WIND0 + 1, column(r)]) for r in (1, 2)}

    def step(group, sums):
        sums = list(sums)
        for tile in range(TILES):
            rows, spot = pl.ds(tile * SUB, SUB), bins(group, tile)
            grow, fade, heavy = rate[spot, :], damp[spot, :], steep[spot, :]
            middle, along, over = centre[spot, :], ahead[spot, :], across[spot, :]
            cell, new = {}, {}
            for r in (1, 2):
                gained = jnp.exp2(grow * wind0[r] - fade * steep0[r])
                factor[group, rows, lanes(r)] = gained
                cell[r] = flow[group, rows, lanes(r)] * gained
                next_[group, rows, lanes(r)] = cell[r]
                new[r] = middle * cell[r] + along * side(tile, sub, cell[r], False)
            new[1] = plus(new[1], pick(tile, sub, None, over * cell[2]))
            new[2] = plus(new[2], pick(tile, sub, over * cell[1], None))
            if tile in SOUTH:
                new[0] = pick(tile, sub, None, over * cell[1])
            if tile in NORTH:
                new[3] = pick(tile, sub, over * cell[2], None)
            for r, value in new.items():
                moved[group, rows, lanes(r)] = value
                sums[r] = sums[r] + heavy * value
        return tuple(sums)

    sums = loop(0, GROUPS, GROUPS, step, (jnp.zeros((SUB, W), F32),) * ROWS)
    for r in range(ROWS):
        state[STEEP1 : STEEP1 + 1, column(r)] = total(sums[r])


def middle(flow, own, wind, sea, coefficients, observed, after, ranks):
    _, block = layout(observed[0].shape[1], ranks)

    def kernel(*refs):
        middle_kernel(*refs, ranks=ranks)

    inputs = [(flow, True), (own, True), (wind, False), (sea, False)]
    inputs += [(value, True) for value in coefficients] + [(value, False) for value in observed + (after,)]
    return call(
        kernel,
        "middle",
        inputs,
        [(CELLS, True)] * 3 + [(STATE, True), ((ranks * block, W), False)],
        away=(len(inputs) - 1,),
        aliases={0: 0},
    )


def split_lam(lam, group, tile, where):
    if tile < 4:
        return lam[group, 0:1, where]
    if tile > 4:
        return lam[group, 4:5, where]
    return lam[group, :, where]


def late_kernel(
    next_in, factor_in, moved_in, from_far, from_near, arrived, own, state_in,
    rate, damp, steep, centre, ahead, back, across,
    next_, factor, moved, next_south, next_north, edges, state, send_b, lam, growth, partial, wanted, gain,
    *, ranks, held_rows,
):
    sub = sublane()
    zero = jnp.zeros((SUB, W), F32)
    even = lax.rem(lax.axis_index("geo"), 2) == 0
    state[...] = state_in[...]
    settle(arrived, wanted, gain, ranks, held_rows)

    def held(place, r):
        return full(state[place : place + 1, column(r)])

    def first(pair, sums, halo_south, halo_north, steep0, wind0):
        sums = list(sums)
        for half in range(2):
            group = 2 * pair + half
            ghosts = {
                -2: unpack_north(halo_south, pair, half, 0, sub),
                -1: unpack_north(halo_south, pair, half, 1, sub),
                4: unpack_south(halo_north, pair, half, 0, sub),
                5: unpack_south(halo_north, pair, half, 1, sub),
            }
            for tile in range(TILES):
                rows, spot = pl.ds(tile * SUB, SUB), bins(group, tile)
                grow, fade, heavy = rate[spot, :], damp[spot, :], steep[spot, :]
                middle, along, over = centre[spot, :], ahead[spot, :], across[spot, :]
                for near, far, mine, second, north in ((-1, -2, 0, 1, True), (4, 5, 3, 2, False)):
                    inward = tile in (NORTH if north else SOUTH)
                    held_back = tile in (SOUTH if north else NORTH)

                    def only(value):
                        return pick(tile, sub, value, None) if north else pick(tile, sub, None, value)

                    here = next_in[group, rows, lanes(mine)]
                    if inward:
                        cell = ghosts[near][tile]
                        gained = jnp.exp2(grow * wind0[near] - fade * steep0[near])
                        value = middle * cell + along * side(tile, sub, cell, False) + over * ghosts[far][tile]
                        value = value * gained
                        (next_south if north else next_north)[group, rows, :] = value
                        here = here + only(over * cell)
                    gained = jnp.exp2(grow * wind0[mine] - fade * steep0[mine])
                    factor[group, rows, lanes(mine)] = gained
                    here = here * gained
                    next_[group, rows, lanes(mine)] = here
                    change = middle * here + along * side(tile, sub, here, False)
                    if inward:
                        change = change + only(over * value)
                    sums[mine] = sums[mine] + heavy * change
                    if held_back:
                        change = change + moved_in[group, rows, lanes(mine)]
                    moved[group, rows, lanes(mine)] = change
                    if inward:
                        change = only(over * here)
                        sums[second] = sums[second] + heavy * change
                        moved[group, rows, lanes(second)] = moved_in[group, rows, lanes(second)] + change
        return tuple(sums)

    def halo_terms(halo_south, halo_north, south, north):
        for halo, rows in ((halo_south, (-2, -1)), (halo_north, (4, 5))):
            here = pl.ds((rows[0] + 2) * W, 2 * W)
            for place, name in enumerate((WIND0, WIND1, SEA)):
                state[name : name + 1, here] = halo[HALF + place : HALF + place + 1, :]
        steeps = {
            -1: south[0] + own[1:2, lanes(0)],
            0: own[0:1, lanes(0)] + south[1],
            3: own[0:1, lanes(3)] + north[1],
            4: north[0] + own[1:2, lanes(3)],
        }
        for r, value in steeps.items():
            known = state[SEA : SEA + 1, column(r)] > 0.5
            state[STEEP0 : STEEP0 + 1, column(r)] = jnp.where(known, value, LAND)
        steep0 = {r: held(STEEP0, r) for r in steeps}
        wind0 = {r: held(WIND0, r) for r in steeps}

        def step(pair, sums):
            return first(pair, sums, halo_south, halo_north, steep0, wind0)

        sums = loop(0, GROUPS // 2, 9, step, (zero,) * ROWS)
        for r in range(ROWS):
            partial[r] = sums[r]

    _, block = layout(held_rows, ranks)
    me = lax.axis_index("geo")

    def sent(source, there):
        source = jnp.clip(source, 0, ranks - 1)
        last = pl.ds(pl.multiple_of(source * block + block - SUB, SUB), SUB)
        values = jnp.where(there, arrived[last, :], 0.0)
        return values[SUB - 2 : SUB - 1, :], values[SUB - 1 : SUB, :]

    @pl.when(even)
    def _():
        halo_terms(from_far, from_near, sent(me - 1, me > 0), sent(me + 1, me < ranks - 1))

    @pl.when(jnp.logical_not(even))
    def _():
        halo_terms(from_near, from_far, sent(me - 1, me > 0), sent(me + 1, me < ranks - 1))

    for r in range(ROWS):
        value = state[STEEP1 : STEEP1 + 1, column(r)] + total(partial[r])
        state[STEEP1 : STEEP1 + 1, column(r)] = jnp.where(state[SEA : SEA + 1, column(r)] > 0.5, value, LAND)
    steep1 = [held(STEEP1, r) for r in range(ROWS)]
    wind1 = [held(WIND1, r) for r in range(ROWS)]
    gains = [gain[:, lanes(r)] for r in range(ROWS)]

    def second(group, sums):
        sums = list(sums)
        means = [[None, None] for _ in range(ROWS)]
        ups = [[None, None] for _ in range(ROWS)]
        downs = [[None, None] for _ in range(ROWS)]
        for tile in range(TILES):
            rows, spot = pl.ds(tile * SUB, SUB), bins(group, tile)
            grow, fade = rate[spot, :], damp[spot, :]
            for r in range(ROWS):
                value = jnp.exp2(grow * wind1[r] - fade * steep1[r])
                growth[group, rows, lanes(r)] = value
                value = value * moved[group, rows, lanes(r)]
                for parts, term in ((means, value), (ups, grow * value), (downs, fade * value)):
                    if tile == 4:
                        parts[r][0] = plus(jnp.where(sub < 4, term, 0.0), parts[r][0])
                        parts[r][1] = jnp.where(sub < 4, 0.0, term)
                    else:
                        f = 0 if tile < 4 else 1
                        parts[r][f] = plus(term, parts[r][f])
        for r in range(ROWS):
            one, two = means[r]
            one = one + pltpu.roll(one, 4, 0)
            two = two + pltpu.roll(two, 4, 0)
            both = jnp.where(sub < 4, one, two)
            both = both + jnp.where((sub & 2) == 0, pltpu.roll(both, 6, 0), pltpu.roll(both, 2, 0))
            both = both + jnp.where((sub & 1) == 0, pltpu.roll(both, 7, 0), pltpu.roll(both, 1, 0))
            value = gains[r] * both - wanted[group, :, lanes(r)]
            lam[group, :, lanes(r)] = value
            up, down = value[0:1, :], value[4:5, :]
            sums[r] = sums[r] + (up * ups[r][0] + down * ups[r][1])
            sums[ROWS + r] = sums[ROWS + r] + (up * downs[r][0] + down * downs[r][1])
        return tuple(sums)

    sums = loop(0, GROUPS, 6, second, (zero,) * (2 * ROWS))
    for r in range(ROWS):
        state[GRAD1 : GRAD1 + 1, column(r)] = total(sums[r]) * LN2
        state[TEND1 : TEND1 + 1, column(r)] = total(sums[ROWS + r]) * (-LN2)
    tend1 = [held(TEND1, r) for r in range(ROWS)]

    def third(group, sums):
        sums = list(sums)
        for tile in range(TILES):
            rows, spot = pl.ds(tile * SUB, SUB), bins(group, tile)
            grow, fade, heavy = rate[spot, :], damp[spot, :], steep[spot, :]
            middle, along, over = centre[spot, :], back[spot, :], across[spot, :]
            cell = {}
            for r in range(ROWS):
                cell[r] = split_lam(lam, group, tile, lanes(r)) * growth[group, rows, lanes(r)] + heavy * tend1[r]
                moved[group, rows, lanes(r)] = cell[r]
            for place, r in enumerate((0, ROWS - 1)):
                value = middle * cell[r] + along * side(tile, sub, cell[r], True)
                value = plus(value, times(over, pick(tile, sub, cell.get(r + 1), cell.get(r - 1))))
                edges[group, rows, lanes(place)] = value
                value = value * next_[group, rows, lanes(r)]
                sums[place] = sums[place] + grow * value
                sums[2 + place] = sums[2 + place] + fade * value
        return tuple(sums)

    sums = loop(0, GROUPS, 6, third, (zero,) * 4)
    for place, r in enumerate((0, ROWS - 1)):
        state[GRAD0 : GRAD0 + 1, column(r)] = total(sums[place]) * LN2
        state[TEND0 : TEND0 + 1, column(r)] = total(sums[2 + place]) * (-LN2)

    @pl.when(even)
    def _():
        fill(send_b, lam, state, 0)

    @pl.when(jnp.logical_not(even))
    def _():
        fill(send_b, lam, state, 2)


def fill(ref, lam, state, base):
    for f in range(NF):
        ref[f : f + 1, :] = lam[f // 2, 4 * (f % 2) : 4 * (f % 2) + 1, pl.ds(base * W, 2 * W)]
    here = pl.ds((base + 2) * W, 2 * W)
    for place, name in enumerate((STEEP1, TEND1, TEND0, TEND0)):
        ref[NF + place : NF + place + 1, :] = state[name : name + 1, here]
    if ref.shape[0] > NF + 4:
        ref[NF + 4 :, :] = jnp.zeros((ref.shape[0] - NF - 4, 2 * W), F32)


def late(next_, factor, moved, from_far, from_near, arrived, own, state, coefficients, ranks, rows):
    def kernel(*refs):
        late_kernel(*refs, ranks=ranks, held_rows=rows)

    inputs = (next_, factor, moved, from_far, from_near, arrived, own, state) + coefficients
    return call(
        kernel,
        "late",
        [(value, True) for value in inputs],
        [(CELLS, True)] * 3 + [(EDGE, True)] * 2 + [(EDGES, True), (STATE, True), ((LINES_B, 2 * W), False)]
        + [((GROUPS, SUB, ROWS * W), True)],
        [
            pltpu.VMEM(CELLS, F32),
            pltpu.VMEM((ROWS, SUB, W), F32),
            pltpu.VMEM((GROUPS, SUB, ROWS * W), F32),
            pltpu.VMEM((SUB, ROWS * W), F32),
        ],
        aliases={0: 0, 1: 1, 2: 2},
    )


def hand_kernel(lam, state, send):
    even = lax.rem(lax.axis_index("geo"), 2) == 0

    @pl.when(even)
    def _():
        fill(send, lam, state, 2)

    @pl.when(jnp.logical_not(even))
    def _():
        fill(send, lam, state, 0)


def hand(lam, state):
    return call(hand_kernel, "hand", [(lam, True), (state, True)], [((LINES_A, 2 * W), False)])[0]


def inner_kernel(
    next_, next_south, next_north, source, state_in, rate, damp, centre, back, across,
    inside, factor_south, factor_north, state,
):
    sub = sublane()
    zero = jnp.zeros((SUB, W), F32)
    state[...] = state_in[...]
    wind0 = {r: full(state[WIND0 : WIND0 + 1, column(r)]) for r in (-1, 4)}
    steep0 = {r: full(state[STEEP0 : STEEP0 + 1, column(r)]) for r in (-1, 4)}

    def step(group, sums):
        sums = list(sums)
        for tile in range(TILES):
            rows, spot = pl.ds(tile * SUB, SUB), bins(group, tile)
            grow, fade = rate[spot, :], damp[spot, :]
            if tile in SOUTH:
                factor_south[group, rows, :] = jnp.exp2(grow * wind0[-1] - fade * steep0[-1])
            if tile in NORTH:
                factor_north[group, rows, :] = jnp.exp2(grow * wind0[4] - fade * steep0[4])
            middle, along, over = centre[spot, :], back[spot, :], across[spot, :]
            cell = {r: source[group, rows, lanes(r)] for r in range(ROWS)}
            for place, r in enumerate((1, 2)):
                value = middle * cell[r] + along * side(tile, sub, cell[r], True)
                value = value + over * pick(tile, sub, cell[r + 1], cell[r - 1])
                inside[group, rows, lanes(place)] = value
                value = value * next_[group, rows, lanes(r)]
                sums[place] = sums[place] + grow * value
                sums[2 + place] = sums[2 + place] + fade * value
            gone = fade * over
            if tile in NORTH:
                value = pick(tile, sub, cell[0] * next_south[group, rows, :], None)
                sums[4] = sums[4] + gone * value
            if tile in SOUTH:
                value = pick(tile, sub, None, cell[3] * next_north[group, rows, :])
                sums[5] = sums[5] + gone * value
        return tuple(sums)

    sums = loop(0, GROUPS, 6, step, (zero,) * 6)
    for place, r in enumerate((1, 2)):
        state[GRAD0 : GRAD0 + 1, column(r)] = total(sums[place]) * LN2
        state[TEND0 : TEND0 + 1, column(r)] = total(sums[2 + place]) * (-LN2)
    state[TEND0 : TEND0 + 1, column(-1)] = total(sums[4]) * (-LN2)
    state[TEND0 : TEND0 + 1, column(4)] = total(sums[5]) * (-LN2)


def inner(*args):
    return call(
        inner_kernel,
        "inner",
        [(arg, True) for arg in args],
        [(EDGES, True), (EDGE, True), (EDGE, True), (STATE, True)],
        cost=1 << 22,
    )


def last_kernel(
    next_, factor, factor_south, factor_north, edges, inside, state, back_a, back_b, rate, damp, steep, centre, back, across,
    out, grad, rims, low, high, ghosts, lam, cells, winds, sems,
):
    sub = sublane()
    zero = jnp.zeros((SUB, W), F32)
    even = lax.rem(lax.axis_index("geo"), 2) == 0
    first_b, first_a = back_b[0 : NF + 4, :], back_a[0 : NF + 4, :]
    ghosts[0] = jnp.where(even, first_b, first_a)
    ghosts[1] = jnp.where(even, first_a, first_b)
    for group in range(GROUPS):
        for where in range(2):
            for row in range(2):
                one = ghosts[where, 2 * group : 2 * group + 1, lanes(row)]
                two = ghosts[where, 2 * group + 1 : 2 * group + 2, lanes(row)]
                lam[group, :, lanes(2 * where + row)] = jnp.where(sub < 4, one, two)
    sea = {r: full(state[SEA : SEA + 1, column(r)]) for r in range(-2, 6)}
    wind1, steep1, tend1 = {}, {}, {}
    for r in (-2, -1, 4, 5):
        where, here = (0, lanes(r + 2)) if r < 0 else (1, lanes(r - 4))
        wind1[r] = full(state[WIND1 : WIND1 + 1, column(r)])
        value = ghosts[where, NF : NF + 1, here]
        steep1[r] = full(jnp.where(sea[r][0:1, :] > 0.5, value, LAND))
        tend1[r] = full(ghosts[where, NF + 1 : NF + 2, here])

    def first(group, sums):
        sums = list(sums)
        for tile in range(TILES):
            rows, spot = pl.ds(tile * SUB, SUB), bins(group, tile)
            grow, fade, heavy = rate[spot, :], damp[spot, :], steep[spot, :]
            middle, along, over = centre[spot, :], back[spot, :], across[spot, :]

            def ghost(r):
                value = split_lam(lam, group, tile, lanes(r + 2 if r < 0 else r - 2))
                return value * jnp.exp2(grow * wind1[r] - fade * steep1[r]) + heavy * tend1[r]

            for near, far, mine, place, tiles in ((-1, -2, 0, 0, SOUTH), (4, 5, 3, 1, NORTH)):
                if tile not in tiles:
                    continue
                cell = ghost(near)
                value = middle * cell + along * side(tile, sub, cell, True) + over * ghost(far)
                (low if place == 0 else high)[group, rows, :] = value
                value = over * cell
                value = pick(tile, sub, None, value) if place == 0 else pick(tile, sub, value, None)
                rims[group, rows, lanes(place)] = edges[group, rows, lanes(place)] + value
                value = value * next_[group, rows, lanes(mine)]
                sums[place] = sums[place] + grow * value
                sums[2 + place] = sums[2 + place] + fade * value
        return tuple(sums)

    sums = loop(0, GROUPS, 6, first, (zero,) * 4)
    sums = [total(value) * LN2 for value in sums]
    tend0 = {r: state[TEND0 : TEND0 + 1, column(r)] for r in range(-1, 5)}
    grad0 = [state[GRAD0 : GRAD0 + 1, column(r)] for r in range(ROWS)]
    tend0[0], grad0[0] = tend0[0] - sums[2], grad0[0] + sums[0]
    tend0[3], grad0[3] = tend0[3] - sums[3], grad0[3] + sums[1]
    tend0[-1] = tend0[-1] + ghosts[0, NF + 2 : NF + 3, lanes(1)]
    tend0[4] = tend0[4] + ghosts[1, NF + 2 : NF + 3, lanes(0)]
    for r in range(ROWS):
        winds[0:1, lanes(r)] = grad0[r]
        winds[1:2, lanes(r)] = state[GRAD1 : GRAD1 + 1, column(r)]
    sent = pltpu.make_async_copy(winds, grad, sems.at[CHUNKS])
    sent.start()
    tend0 = {r: full(value) for r, value in tend0.items()}

    def second(group, carry):
        for tile in range(TILES):
            rows, spot = pl.ds(tile * SUB, SUB), bins(group, tile)
            heavy = steep[spot, :]
            middle, along, over = centre[spot, :], back[spot, :], across[spot, :]
            cell = {}
            for r in range(-1, 5):
                if r == -1:
                    if tile not in SOUTH:
                        continue
                    value = low[group, rows, :] * factor_south[group, rows, :]
                elif r == 4:
                    if tile not in NORTH:
                        continue
                    value = high[group, rows, :] * factor_north[group, rows, :]
                else:
                    if r == 0:
                        value = (rims if tile in SOUTH else edges)[group, rows, lanes(0)]
                    elif r == 3:
                        value = (rims if tile in NORTH else edges)[group, rows, lanes(1)]
                    else:
                        value = inside[group, rows, lanes(r - 1)]
                    value = value * factor[group, rows, lanes(r)]
                cell[r] = value + heavy * tend0[r]
            for r in range(ROWS):
                value = middle * cell[r] + along * side(tile, sub, cell[r], True)
                value = value + over * pick(tile, sub, cell.get(r + 1), cell.get(r - 1))
                cells[group, rows, lanes(r)] = sea[r] * value
        return carry

    each = GROUPS // CHUNKS
    copies = []
    for c in range(CHUNKS):
        loop(c * each, (c + 1) * each, 3, second, 0)
        here = pl.ds(c * each, each)
        copies.append(pltpu.make_async_copy(cells.at[here], out.at[here], sems.at[c]))
        copies[c].start()
    sent.wait()
    for copy in copies:
        copy.wait()


def last(next_, factor, factor_south, factor_north, edges, inside, state, back_a, back_b, coefficients):
    inputs = [(value, True) for value in (next_, factor, factor_south, factor_north, edges, inside, state)]
    inputs += [(back_a, True), (back_b, True)]
    inputs += [(value, True) for value in coefficients]
    return call(
        last_kernel,
        "last",
        inputs,
        [(CELLS, False), ((2, ROWS * W), False)],
        [
            pltpu.VMEM(EDGES, F32),
            pltpu.VMEM(EDGE, F32),
            pltpu.VMEM(EDGE, F32),
            pltpu.VMEM((2, NF + 4, 2 * W), F32),
            pltpu.VMEM((GROUPS, SUB, ROWS * W), F32),
            pltpu.VMEM(CELLS, F32),
            pltpu.VMEM((2, ROWS * W), F32),
            pltpu.SemaphoreType.DMA((CHUNKS + 1,)),
        ],
        out_away=(0, 1),
    )


def swaps(count):
    near = [(i, i ^ 1) for i in range(count)]
    far = []
    for i in range(1, count - 1, 2):
        far += [(i, i + 1), (i + 1, i)]
    return near, far


def body(
    initial_spectrum,
    wind_forcing,
    sea_mask,
    courant,
    input_rate,
    damping,
    steep_weight,
    obs_owner,
    obs_point,
    obs_value,
    obs_weight,
):
    count = lax.axis_size("geo")
    held = obs_point.shape[0]
    near, far = swaps(count)
    field = initial_spectrum.reshape(CELLS)
    sea = sea_mask.reshape(1, ROWS * W)
    from_far = lax.ppermute(far_rows(field, sea, wind_forcing), "geo", far)
    flow, rate, damp, steep, centre, ahead, back, across, own = local(
        field,
        sea,
        courant,
        input_rate.reshape(1, NB),
        damping.reshape(1, NB),
        steep_weight.reshape(1, NB),
        jnp.asarray(direction_tables()),
    )
    rows = near_rows(field, sea, wind_forcing, own)
    from_near = lax.ppermute(rows, "geo", near)
    next_, factor, moved, state, slots = middle(
        flow, own, wind_forcing, sea, (rate, damp, steep, centre, ahead, across),
        (obs_owner.reshape(1, held), obs_point.reshape(1, held), obs_value.T, obs_weight.reshape(1, held)), rows, count,
    )
    arrived = lax.all_to_all(slots, "geo", split_axis=0, concat_axis=0, tiled=True)
    next_, factor, source, next_south, next_north, edges, state, send_b, lam = late(
        next_, factor, moved, from_far, from_near, arrived, own, state,
        (rate, damp, steep, centre, ahead, back, across), count, held,
    )
    back_b = lax.ppermute(send_b, "geo", far)
    back_a = lax.ppermute(hand(lam, state), "geo", near)
    inside, factor_south, factor_north, state = inner(
        next_, next_south, next_north, source, state, rate, damp, centre, back, across
    )
    out, grad = last(
        next_, factor, factor_south, factor_north, edges, inside, state, back_a, back_b,
        (rate, damp, steep, centre, back, across),
    )
    return grad, out.reshape(NB, ROWS * W)


def solution(mesh):
    return jax.shard_map(
        body,
        mesh=mesh,
        in_specs=(
            P(None, ("groups", "geo")),
            P(None, ("groups", "geo")),
            P(("groups", "geo")),
            P(),
            P(),
            P(),
            P(),
            P(("groups", "geo"), None),
            P(("groups", "geo")),
            P(("groups", "geo"), None),
            P(("groups", "geo")),
        ),
        out_specs=(P(None, ("groups", "geo")), P(None, ("groups", "geo"))),
        check_vma=False,
    )
```

```python
import math

import jax
import jax.numpy as jnp
import numpy as np
from jax import lax
from jax.experimental import pallas as pl
from jax.experimental.pallas import tpu as pltpu
from jax.sharding import PartitionSpec as P

ND = 36
NF = 36
NB = 1296
W = 128
ROWS = 4
SUB = 8
GROUP = 72
TILES = GROUP // SUB
GROUPS = NB // GROUP
CHUNKS = 6
F32 = jnp.float32
BF16 = jnp.bfloat16
LIMIT = 7 * 1024 * 1024
LOG2E = math.log2(math.e)
LN2 = math.log(2.0)
LAND = 1.0e5

CELLS = (GROUPS, GROUP, ROWS * W)
EDGE = (GROUPS, GROUP, W)
EDGES = (GROUPS, GROUP, 2 * W)
BINS = (NB, W)
HALF = NB // 2
HALO = (HALF + SUB, 2 * W)
LOAD = 40
LINES_A = NF + 4
LINES_B = NF + 12
STATE = (16, 8 * W)
STEEP0, WIND0, WIND1, SEA, STEEP1, TEND1, GRAD1, TEND0, GRAD0, PASS0 = range(10)

NORTH = (0, 1, 2, 4, 5, 6)
SOUTH = (2, 3, 4, 6, 7, 8)
FROM_WEST = (0, 4, 8)
FROM_EAST = (2, 6)


def direction_tables():
    angle = np.float32(2.0 * math.pi) * np.arange(ND, dtype=np.float32) / np.float32(ND)
    cosine = np.tile(np.cos(angle), 2)[:, None]
    sine = np.tile(np.sin(angle), 2)[:, None]
    lane = np.arange(W)[None, :]
    east = cosine >= 0
    west_ok = (lane > 0).astype(np.float32)
    east_ok = (lane < W - 1).astype(np.float32)
    one = np.ones((1, W), np.float32)
    forward = np.abs(cosine) * np.where(east, west_ok, east_ok)
    backward = np.abs(cosine) * np.where(east, east_ok, west_ok)
    return np.stack(
        [(np.abs(cosine) + np.abs(sine)) * one, np.abs(sine) * one, forward, backward]
    ).astype(np.float32)


def sublane():
    return lax.broadcasted_iota(jnp.int32, (SUB, W), 0)


def north_mask(tile, sub):
    return {2: sub < 2, 4: sub >= 4, 6: sub < 6}.get(tile)


def west_mask(tile, sub):
    return {1: sub < 1, 3: sub >= 3, 5: sub < 5, 7: sub >= 7}.get(tile)


def side(tile, sub, value, reverse):
    west = tile not in (FROM_WEST if reverse else FROM_EAST)
    east = tile not in (FROM_EAST if reverse else FROM_WEST)
    from_west = pltpu.roll(value, 1, 1) if west else None
    from_east = pltpu.roll(value, W - 1, 1) if east else None
    if from_east is None:
        return from_west
    if from_west is None:
        return from_east
    mask = west_mask(tile, sub)
    return jnp.where(mask, from_east, from_west) if reverse else jnp.where(mask, from_west, from_east)


def pick(tile, sub, north, south):
    mask = north_mask(tile, sub)
    if mask is None:
        return north if tile in NORTH else south
    if north is None and south is None:
        return None
    return jnp.where(mask, 0.0 if north is None else north, 0.0 if south is None else south)


def plus(value, other):
    return value if other is None else value + other


def times(factor, value):
    return None if value is None else factor * value


def speed(tile, sub, courant, group):
    first, second = courant[2 * group], courant[2 * group + 1]
    if tile == 4:
        return jnp.where(sub < 4, first, second)
    return jnp.full((SUB, W), first if tile < 4 else second, F32)


def lanes(row):
    return pl.ds(row * W, W)


def column(row):
    return pl.ds((row + 2) * W, W)


def bins(group, tile):
    return pl.ds(pl.multiple_of(group * GROUP + tile * SUB, SUB), SUB)


def total(value):
    return jnp.sum(value, axis=0, keepdims=True)


def full(value):
    return jnp.broadcast_to(value, (SUB, W))


def loop(low, high, by, body, init):
    def passes(index, carry):
        for k in range(by):
            carry = body(low + index * by + k, carry)
        return carry

    return lax.fori_loop(0, (high - low) // by, passes, init)


def whole(memory=pltpu.VMEM):
    return pl.BlockSpec(memory_space=memory)


def call(kernel, name, inputs, outputs, scratch=(), smem=(), away=(), out_away=(), aliases=None, cost=0):
    specs, operands = [], []
    for place, (value, resident) in enumerate(inputs):
        specs.append(whole(pltpu.SMEM if place in smem else pl.ANY if place in away else pltpu.VMEM))
        operands.append(pltpu.with_memory_space_constraint(value, pltpu.VMEM) if resident else value)
    shapes = [pltpu.VMEM(shape, F32) if resident else jax.ShapeDtypeStruct(shape, F32) for shape, resident in outputs]
    return pl.pallas_call(
        kernel,
        in_specs=specs,
        out_specs=[whole(pl.ANY if place in out_away else pltpu.VMEM) for place in range(len(outputs))],
        out_shape=shapes,
        scratch_shapes=list(scratch),
        input_output_aliases=aliases or {},
        compiler_params=pltpu.CompilerParams(vmem_limit_bytes=LIMIT),
        cost_estimate=pl.CostEstimate(flops=cost, bytes_accessed=cost, transcendentals=0) if cost else None,
        name=name,
    )(*operands)


def pack_rows(cell, put, sub, north):
    both = (sub < 2) | ((sub >= 4) & (sub < 6))
    for row in range(2):
        rest = []
        for half in range(2):
            for place, tile in enumerate((0, 1, 5) if north else (3, 7, 8)):
                put(half * 4 + place, row, cell(half, tile, row))
            second, fourth, sixth = [cell(half, tile, row) for tile in (2, 4, 6)]
            if north:
                put(half * 4 + 3, row, jnp.where(sub < 2, second, jnp.where(sub < 4, sixth, fourth)))
                rest.append(sixth)
            else:
                put(half * 4 + 3, row, jnp.where(sub < 4, fourth, second))
                rest.append(jnp.where(sub < 4, second, sixth))
        other = pltpu.roll(rest[1], 2, 0)
        put(8, row, jnp.where(both, rest[0], other) if north else jnp.where(both, other, rest[0]))


def pack_all(cells, base, sea, out, low, high, north):
    sub = sublane()

    def step(pair, carry):
        def cell(half, tile, row):
            return cells[2 * pair + half, pl.ds(tile * SUB, SUB), pl.ds(base + row * W, W)] * sea[row]

        def put(tile, row, value):
            out[pl.ds(pl.multiple_of(pair * GROUP + tile * SUB, SUB), SUB), lanes(row)] = value

        pack_rows(cell, put, sub, north)
        return carry

    loop(low, high, high - low, step, 0)


def pack_small(out, wind, sea, base):
    here = pl.ds(base * W, 2 * W)
    out[pl.ds(HALF, SUB), :] = jnp.zeros((SUB, 2 * W), F32)
    out[HALF : HALF + 2, :] = wind[:, here]
    out[HALF + 2 : HALF + 3, :] = sea[:, here].astype(F32)


def far_kernel(field, sea_in, wind_in, out, cells, sea, wind, sems):
    even = lax.rem(lax.axis_index("geo"), 2) == 0
    each = GROUPS
    small = [
        pltpu.make_async_copy(sea_in, sea, sems.at[6]),
        pltpu.make_async_copy(wind_in, wind, sems.at[7]),
    ]

    def bring(first, lane):
        copies = []
        for c in range(1):
            for run in range(2):
                here, rows = pl.ds(c * each, each), pl.ds((first + 4 * run) * SUB, 3 * SUB)
                copies.append(
                    pltpu.make_async_copy(
                        field.at[here, rows, pl.ds(lane, 2 * W)], cells.at[here, rows], sems.at[2 * c + run]
                    )
                )
        return copies

    @pl.when(even)
    def _():
        for copy in bring(2, 0):
            copy.start()

    @pl.when(jnp.logical_not(even))
    def _():
        for copy in bring(0, 2 * W):
            copy.start()

    copies = bring(0, 0)
    for copy in small:
        copy.start()
    for copy in small:
        copy.wait()
    for c in range(1):
        copies[2 * c].wait()
        copies[2 * c + 1].wait()

        @pl.when(even)
        def _():
            mask = [full(sea[:, lanes(r)].astype(F32)) for r in (0, 1)]
            pack_all(cells, 0, mask, out, c * each // 2, (c + 1) * each // 2, False)

        @pl.when(jnp.logical_not(even))
        def _():
            mask = [full(sea[:, lanes(r)].astype(F32)) for r in (2, 3)]
            pack_all(cells, 0, mask, out, c * each // 2, (c + 1) * each // 2, True)

    @pl.when(even)
    def _():
        pack_small(out, wind, sea, 0)

    @pl.when(jnp.logical_not(even))
    def _():
        pack_small(out, wind, sea, 2)


def far_rows(field, sea, wind):
    return call(
        far_kernel,
        "far",
        [(pltpu.with_memory_space_constraint(value, pltpu.HBM), False) for value in (field, sea, wind)],
        [(HALO, False)],
        [
            pltpu.VMEM((GROUPS, GROUP, 2 * W), F32),
            pltpu.VMEM((1, ROWS * W), jnp.int32),
            pltpu.VMEM((2, ROWS * W), F32),
            pltpu.SemaphoreType.DMA((8,)),
        ],
        away=(0, 1, 2),
    )[0]


def near_kernel(cells, sea_in, wind, after, out):
    even = lax.rem(lax.axis_index("geo"), 2) == 0

    def rows(base, north):
        mask = [full(sea_in[:, lanes(base + r)].astype(F32)) for r in range(2)]
        pack_all(cells, base * W, mask, out, 0, GROUPS // 2, north)
        pack_small(out, wind, sea_in, base)

    @pl.when(even)
    def _():
        rows(2, True)

    @pl.when(jnp.logical_not(even))
    def _():
        rows(0, False)


def near_rows(field, sea, wind, own):
    return call(near_kernel, "near", [(field, True), (sea, False), (wind, False), (own, True)], [(HALO, False)])[0]


def unpack_north(halo, pair, half, row, sub):
    def get(tile):
        return halo[pl.ds(pl.multiple_of(pair * GROUP + tile * SUB, SUB), SUB), lanes(row)]

    mixed, last = get(half * 4 + 3), get(8)
    if half:
        last = pltpu.roll(last, 6, 0)
    return {
        0: get(half * 4),
        1: get(half * 4 + 1),
        2: mixed,
        4: mixed,
        5: get(half * 4 + 2),
        6: jnp.where((sub >= 2) & (sub < 4), mixed, last),
    }


def unpack_south(halo, pair, half, row, sub):
    def get(tile):
        return halo[pl.ds(pl.multiple_of(pair * GROUP + tile * SUB, SUB), SUB), lanes(row)]

    mixed, last = get(half * 4 + 3), get(8)
    if half:
        last = pltpu.roll(last, 6, 0)
    return {
        2: jnp.where(sub < 4, last, mixed),
        3: get(half * 4),
        4: mixed,
        6: last,
        7: get(half * 4 + 1),
        8: get(half * 4 + 2),
    }


def pieces(value):
    high = value.astype(BF16)
    value = value - high.astype(F32)
    middle = value.astype(BF16)
    return high, middle, (value - middle.astype(F32)).astype(BF16)


def spread(inputs, outputs, flat):
    flat[...] = jnp.zeros_like(flat)
    for place, (row, scale) in enumerate(inputs):
        for k, piece in enumerate(pieces(row[...] * scale)):
            flat[3 * place + k : 3 * place + k + 1, 0:NB] = piece.astype(F32)
    count = len(outputs)
    shape = (flat.shape[0], count * W)
    row, lane = lax.broadcasted_iota(jnp.int32, shape, 0), lax.broadcasted_iota(jnp.int32, shape, 1)
    mask = jnp.zeros(shape, F32)
    for place in range(count):
        mine = (row >= 3 * place) & (row < 3 * place + 3) & (lane >= place * W) & (lane < place * W + W)
        mask = jnp.where(mine, 1.0, mask)
    wide = lax.dot_general(
        flat[...].astype(BF16), mask.astype(BF16), (((0,), (0,)), ((), ())), preferred_element_type=F32
    )
    for place, out in enumerate(outputs):
        out[...] = wide[0:NB, place * W : (place + 1) * W]


def layout(rows, ranks):
    lines = -(-max(2, 2 * rows // ranks) // 3)
    return lines, -(-(lines + 2) // SUB) * SUB


def sort(owner, point, value, weight, ranks):
    rows = owner.shape[1]
    lines, block = layout(rows, ranks)
    hits = owner[...] == lax.broadcasted_iota(jnp.int32, (ranks, rows), 0)
    before = lax.broadcasted_iota(jnp.int32, (rows, rows), 0) < lax.broadcasted_iota(jnp.int32, (rows, rows), 1)
    counts = jnp.dot(hits.astype(F32).astype(BF16), before.astype(F32).astype(BF16), preferred_element_type=F32)
    order = jnp.sum(jnp.where(hits, counts, 0.0), axis=0, keepdims=True).astype(jnp.int32)
    line = (order * 171) >> 9
    third = order - 3 * line
    target = owner[...] * block + line
    spots = lax.broadcasted_iota(jnp.int32, (ranks * block, rows), 0)
    places = [((target == spots) & (third == k)).astype(F32).astype(BF16) for k in range(3)]
    load = jnp.concatenate(
        [
            value[...] * weight[...],
            weight[...],
            point[...].astype(F32),
            jnp.zeros((LOAD - NF - 2, rows), F32),
        ],
        axis=0,
    )
    loads = [
        jnp.concatenate(
            [jnp.zeros((LOAD * k, rows), F32)] * (k > 0) + [load, jnp.zeros((W - LOAD * (k + 1), rows), F32)], axis=0
        )
        for k in range(3)
    ]
    places = jnp.concatenate(places, axis=1)
    result = 0.0
    for piece in zip(*[pieces(part) for part in loads]):
        result = result + lax.dot_general(
            places, jnp.concatenate(piece, axis=1), (((1,), (1,)), ((), ())), preferred_element_type=F32
        )
    return result


def local_kernel(
    cells, sea_in, courant, rate_in, damp_in, steep_in, table,
    flow, rate, damp, steep, centre, ahead, back, across, own, flat,
):
    sub = sublane()
    spread(((rate_in, LOG2E), (damp_in, LOG2E), (steep_in, 1.0)), (rate, damp, steep), flat)
    sea = [full(sea_in[:, lanes(r)].astype(F32)) for r in range(ROWS)]
    zero = jnp.zeros((SUB, W), F32)

    def step(group, sums):
        sums = list(sums)
        for tile in range(TILES):
            rows, spot = pl.ds(tile * SUB, SUB), bins(group, tile)
            pace = speed(tile, sub, courant, group)
            middle = 1.0 - pace * table[0, rows, :]
            over = pace * table[1, rows, :]
            along = pace * table[2, rows, :]
            centre[spot, :] = middle
            across[spot, :] = over
            ahead[spot, :] = along
            back[spot, :] = pace * table[3, rows, :]
            heavy = steep[spot, :]
            cell = {r: cells[group, rows, lanes(r)] * sea[r] for r in range(ROWS)}
            for r in range(ROWS):
                moved = middle * cell[r] + along * side(tile, sub, cell[r], False)
                moved = plus(moved, times(over, pick(tile, sub, cell.get(r - 1), cell.get(r + 1))))
                flow[group, rows, lanes(r)] = moved
                sums[r] = sums[r] + heavy * moved
            gone = heavy * over
            if tile in NORTH:
                sums[ROWS] = sums[ROWS] + pick(tile, sub, gone * cell[ROWS - 1], None)
            if tile in SOUTH:
                sums[ROWS + 1] = sums[ROWS + 1] + pick(tile, sub, None, gone * cell[0])
        return tuple(sums)

    sums = loop(0, GROUPS, GROUPS, step, (zero,) * (ROWS + 2))
    sums = [total(value) for value in sums]
    own[...] = jnp.zeros_like(own)
    for r in range(ROWS):
        own[0:1, lanes(r)] = sums[r] * sea[r][0:1, :]
    own[1:2, lanes(ROWS - 1)] = sums[ROWS]
    own[1:2, lanes(0)] = sums[ROWS + 1]


def local(field, sea, courant, rate, damp, steep, table):
    return call(
        local_kernel,
        "local",
        [(field, True)] + [(arg, False) for arg in (sea, courant, rate, damp, steep, table)],
        [(CELLS, True)] + [(BINS, True)] * 7 + [((SUB, ROWS * W), True)],
        [pltpu.VMEM((16, 11 * W), F32)],
        smem=(2,),
    )


def settle(arrived, wanted, gain, ranks, rows):
    lines, block = layout(rows, ranks)
    size = ranks * block
    shape = (size, W)
    lane = lax.broadcasted_iota(jnp.int32, shape, 1)
    held = lax.rem(lax.broadcasted_iota(jnp.int32, shape, 0), block) < lines
    load = jnp.where(held, arrived[...], 0.0)
    spots = lax.broadcasted_iota(jnp.int32, (size, ROWS * W), 1)
    sums = 0.0
    for k in range(3):
        mine = pltpu.roll(load, W - LOAD * k, 1) if k else load
        point = mine[:, NF + 1 : NF + 2].astype(jnp.int32)
        hits = (point == spots).astype(F32).astype(BF16)
        high, middle, low = [piece.astype(F32) for piece in pieces(jnp.where(lane < LOAD, mine, 0.0))]
        mine = high + pltpu.roll(middle, LOAD, 1) + pltpu.roll(low, 2 * LOAD, 1)
        sums = sums + lax.dot_general(
            mine.astype(BF16), hits, (((0,), (0,)), ((), ())), preferred_element_type=F32
        )
    sums = sums[0:LOAD] + sums[LOAD : 2 * LOAD] + sums[2 * LOAD : 3 * LOAD]
    for f in range(NF):
        rows_of = slice(4 * (f % 2), 4 * (f % 2) + 4)
        wanted[f // 2, rows_of, :] = jnp.broadcast_to(sums[f : f + 1, :] * (1.0 / ND), (4, ROWS * W))
    gain[...] = jnp.broadcast_to(sums[NF : NF + 1, :] * (1.0 / (ND * ND)), gain.shape)


def middle_kernel(
    flow, own, wind, sea_in, rate, damp, steep, centre, ahead, across, owner, point, value, weight, after,
    next_, factor, moved, state, slots, *, ranks,
):
    sub = sublane()
    slots[...] = sort(owner, point, value, weight, ranks)
    _, block = layout(owner.shape[1], ranks)
    me = lax.axis_index("geo")

    def hand(row, dest):
        last = pl.ds(pl.multiple_of(dest * block + block - SUB, SUB), SUB)
        values = jnp.where(sub == SUB - 2, own[0:1, lanes(row)], slots[last, :])
        slots[last, :] = jnp.where(sub == SUB - 1, own[1:2, lanes(row)], values)

    @pl.when(me < ranks - 1)
    def _():
        hand(ROWS - 1, me + 1)

    @pl.when(me > 0)
    def _():
        hand(0, me - 1)

    state[...] = jnp.zeros_like(state)
    here = pl.ds(2 * W, ROWS * W)
    state[WIND0 : WIND0 + 1, here] = wind[0:1, :]
    state[WIND1 : WIND1 + 1, here] = wind[1:2, :]
    state[SEA : SEA + 1, here] = sea_in[...].astype(F32)
    state[STEEP0 : STEEP0 + 1, here] = jnp.where(state[SEA : SEA + 1, here] > 0.5, own[0:1, :], LAND)
    steep0 = {r: full(state[STEEP0 : STEEP0 + 1, column(r)]) for r in (1, 2)}
    wind0 = {r: full(state[WIND0 : WIND0 + 1, column(r)]) for r in (1, 2)}

    def step(group, sums):
        sums = list(sums)
        for tile in range(TILES):
            rows, spot = pl.ds(tile * SUB, SUB), bins(group, tile)
            grow, fade, heavy = rate[spot, :], damp[spot, :], steep[spot, :]
            middle, along, over = centre[spot, :], ahead[spot, :], across[spot, :]
            cell, new = {}, {}
            for r in (1, 2):
                gained = jnp.exp2(grow * wind0[r] - fade * steep0[r])
                factor[group, rows, lanes(r)] = gained
                cell[r] = flow[group, rows, lanes(r)] * gained
                next_[group, rows, lanes(r)] = cell[r]
                new[r] = middle * cell[r] + along * side(tile, sub, cell[r], False)
            new[1] = plus(new[1], pick(tile, sub, None, over * cell[2]))
            new[2] = plus(new[2], pick(tile, sub, over * cell[1], None))
            if tile in SOUTH:
                new[0] = pick(tile, sub, None, over * cell[1])
            if tile in NORTH:
                new[3] = pick(tile, sub, over * cell[2], None)
            for r, value in new.items():
                moved[group, rows, lanes(r)] = value
                sums[r] = sums[r] + heavy * value
        return tuple(sums)

    sums = loop(0, GROUPS, GROUPS, step, (jnp.zeros((SUB, W), F32),) * ROWS)
    for r in range(ROWS):
        state[STEEP1 : STEEP1 + 1, column(r)] = total(sums[r])


def middle(flow, own, wind, sea, coefficients, observed, after, ranks):
    _, block = layout(observed[0].shape[1], ranks)

    def kernel(*refs):
        middle_kernel(*refs, ranks=ranks)

    inputs = [(flow, True), (own, True), (wind, False), (sea, False)]
    inputs += [(value, True) for value in coefficients] + [(value, False) for value in observed + (after,)]
    return call(
        kernel,
        "middle",
        inputs,
        [(CELLS, True)] * 3 + [(STATE, True), ((ranks * block, W), False)],
        away=(len(inputs) - 1,),
        aliases={0: 0},
    )


def split_lam(lam, group, tile, where):
    if tile < 4:
        return lam[group, 0:1, where]
    if tile > 4:
        return lam[group, 4:5, where]
    return lam[group, :, where]


def late_kernel(
    next_in, factor_in, moved_in, from_far, from_near, arrived, own, state_in,
    rate, damp, steep, centre, ahead, back, across,
    next_, factor, moved, next_south, next_north, edges, state, send_b, lam, growth, partial, wanted, gain,
    *, ranks, held_rows,
):
    sub = sublane()
    zero = jnp.zeros((SUB, W), F32)
    even = lax.rem(lax.axis_index("geo"), 2) == 0
    state[...] = state_in[...]
    settle(arrived, wanted, gain, ranks, held_rows)

    def held(place, r):
        return full(state[place : place + 1, column(r)])

    def first(pair, sums, halo_south, halo_north, steep0, wind0):
        sums = list(sums)
        for half in range(2):
            group = 2 * pair + half
            ghosts = {
                -2: unpack_north(halo_south, pair, half, 0, sub),
                -1: unpack_north(halo_south, pair, half, 1, sub),
                4: unpack_south(halo_north, pair, half, 0, sub),
                5: unpack_south(halo_north, pair, half, 1, sub),
            }
            for tile in range(TILES):
                rows, spot = pl.ds(tile * SUB, SUB), bins(group, tile)
                grow, fade, heavy = rate[spot, :], damp[spot, :], steep[spot, :]
                middle, along, over = centre[spot, :], ahead[spot, :], across[spot, :]
                for near, far, mine, second, north in ((-1, -2, 0, 1, True), (4, 5, 3, 2, False)):
                    inward = tile in (NORTH if north else SOUTH)
                    held_back = tile in (SOUTH if north else NORTH)

                    def only(value):
                        return pick(tile, sub, value, None) if north else pick(tile, sub, None, value)

                    here = next_in[group, rows, lanes(mine)]
                    if inward:
                        cell = ghosts[near][tile]
                        gained = jnp.exp2(grow * wind0[near] - fade * steep0[near])
                        value = middle * cell + along * side(tile, sub, cell, False) + over * ghosts[far][tile]
                        value = value * gained
                        (next_south if north else next_north)[group, rows, :] = value
                        here = here + only(over * cell)
                    gained = jnp.exp2(grow * wind0[mine] - fade * steep0[mine])
                    factor[group, rows, lanes(mine)] = gained
                    here = here * gained
                    next_[group, rows, lanes(mine)] = here
                    change = middle * here + along * side(tile, sub, here, False)
                    if inward:
                        change = change + only(over * value)
                    sums[mine] = sums[mine] + heavy * change
                    if held_back:
                        change = change + moved_in[group, rows, lanes(mine)]
                    moved[group, rows, lanes(mine)] = change
                    if inward:
                        change = only(over * here)
                        sums[second] = sums[second] + heavy * change
                        moved[group, rows, lanes(second)] = moved_in[group, rows, lanes(second)] + change
        return tuple(sums)

    def halo_terms(halo_south, halo_north, south, north):
        for halo, rows in ((halo_south, (-2, -1)), (halo_north, (4, 5))):
            here = pl.ds((rows[0] + 2) * W, 2 * W)
            for place, name in enumerate((WIND0, WIND1, SEA)):
                state[name : name + 1, here] = halo[HALF + place : HALF + place + 1, :]
        steeps = {
            -1: south[0] + own[1:2, lanes(0)],
            0: own[0:1, lanes(0)] + south[1],
            3: own[0:1, lanes(3)] + north[1],
            4: north[0] + own[1:2, lanes(3)],
        }
        for r, value in steeps.items():
            known = state[SEA : SEA + 1, column(r)] > 0.5
            state[STEEP0 : STEEP0 + 1, column(r)] = jnp.where(known, value, LAND)
        steep0 = {r: held(STEEP0, r) for r in steeps}
        wind0 = {r: held(WIND0, r) for r in steeps}

        def step(pair, sums):
            return first(pair, sums, halo_south, halo_north, steep0, wind0)

        sums = loop(0, GROUPS // 2, 9, step, (zero,) * ROWS)
        for r in range(ROWS):
            partial[r] = sums[r]

    _, block = layout(held_rows, ranks)
    me = lax.axis_index("geo")

    def sent(source, there):
        source = jnp.clip(source, 0, ranks - 1)
        last = pl.ds(pl.multiple_of(source * block + block - SUB, SUB), SUB)
        values = jnp.where(there, arrived[last, :], 0.0)
        return values[SUB - 2 : SUB - 1, :], values[SUB - 1 : SUB, :]

    @pl.when(even)
    def _():
        halo_terms(from_far, from_near, sent(me - 1, me > 0), sent(me + 1, me < ranks - 1))

    @pl.when(jnp.logical_not(even))
    def _():
        halo_terms(from_near, from_far, sent(me - 1, me > 0), sent(me + 1, me < ranks - 1))

    for r in range(ROWS):
        value = state[STEEP1 : STEEP1 + 1, column(r)] + total(partial[r])
        state[STEEP1 : STEEP1 + 1, column(r)] = jnp.where(state[SEA : SEA + 1, column(r)] > 0.5, value, LAND)
    steep1 = [held(STEEP1, r) for r in range(ROWS)]
    wind1 = [held(WIND1, r) for r in range(ROWS)]
    gains = [gain[:, lanes(r)] for r in range(ROWS)]

    def second(group, sums):
        sums = list(sums)
        means = [[None, None] for _ in range(ROWS)]
        ups = [[None, None] for _ in range(ROWS)]
        downs = [[None, None] for _ in range(ROWS)]
        for tile in range(TILES):
            rows, spot = pl.ds(tile * SUB, SUB), bins(group, tile)
            grow, fade = rate[spot, :], damp[spot, :]
            for r in range(ROWS):
                value = jnp.exp2(grow * wind1[r] - fade * steep1[r])
                growth[group, rows, lanes(r)] = value
                value = value * moved[group, rows, lanes(r)]
                for parts, term in ((means, value), (ups, grow * value), (downs, fade * value)):
                    if tile == 4:
                        parts[r][0] = plus(jnp.where(sub < 4, term, 0.0), parts[r][0])
                        parts[r][1] = jnp.where(sub < 4, 0.0, term)
                    else:
                        f = 0 if tile < 4 else 1
                        parts[r][f] = plus(term, parts[r][f])
        for r in range(ROWS):
            one, two = means[r]
            one = one + pltpu.roll(one, 4, 0)
            two = two + pltpu.roll(two, 4, 0)
            both = jnp.where(sub < 4, one, two)
            both = both + jnp.where((sub & 2) == 0, pltpu.roll(both, 6, 0), pltpu.roll(both, 2, 0))
            both = both + jnp.where((sub & 1) == 0, pltpu.roll(both, 7, 0), pltpu.roll(both, 1, 0))
            value = gains[r] * both - wanted[group, :, lanes(r)]
            lam[group, :, lanes(r)] = value
            up, down = value[0:1, :], value[4:5, :]
            sums[r] = sums[r] + (up * ups[r][0] + down * ups[r][1])
            sums[ROWS + r] = sums[ROWS + r] + (up * downs[r][0] + down * downs[r][1])
        return tuple(sums)

    sums = loop(0, GROUPS, 6, second, (zero,) * (2 * ROWS))
    for r in range(ROWS):
        state[GRAD1 : GRAD1 + 1, column(r)] = total(sums[r]) * LN2
        state[TEND1 : TEND1 + 1, column(r)] = total(sums[ROWS + r]) * (-LN2)
    tend1 = [held(TEND1, r) for r in range(ROWS)]

    def third(group, sums):
        sums = list(sums)
        for tile in range(TILES):
            rows, spot = pl.ds(tile * SUB, SUB), bins(group, tile)
            grow, fade, heavy = rate[spot, :], damp[spot, :], steep[spot, :]
            middle, along, over = centre[spot, :], back[spot, :], across[spot, :]
            cell = {}
            for r in range(ROWS):
                cell[r] = split_lam(lam, group, tile, lanes(r)) * growth[group, rows, lanes(r)] + heavy * tend1[r]
                moved[group, rows, lanes(r)] = cell[r]
            for place, r in enumerate((0, ROWS - 1)):
                value = middle * cell[r] + along * side(tile, sub, cell[r], True)
                value = plus(value, times(over, pick(tile, sub, cell.get(r + 1), cell.get(r - 1))))
                edges[group, rows, lanes(place)] = value
                value = value * next_[group, rows, lanes(r)]
                sums[place] = sums[place] + grow * value
                sums[2 + place] = sums[2 + place] + fade * value
        return tuple(sums)

    sums = loop(0, GROUPS, 6, third, (zero,) * 4)
    for place, r in enumerate((0, ROWS - 1)):
        state[GRAD0 : GRAD0 + 1, column(r)] = total(sums[place]) * LN2
        state[TEND0 : TEND0 + 1, column(r)] = total(sums[2 + place]) * (-LN2)

    @pl.when(even)
    def _():
        fill(send_b, lam, state, 0)

    @pl.when(jnp.logical_not(even))
    def _():
        fill(send_b, lam, state, 2)


def fill(ref, lam, state, base):
    for f in range(NF):
        ref[f : f + 1, :] = lam[f // 2, 4 * (f % 2) : 4 * (f % 2) + 1, pl.ds(base * W, 2 * W)]
    here = pl.ds((base + 2) * W, 2 * W)
    for place, name in enumerate((STEEP1, TEND1, TEND0, TEND0)):
        ref[NF + place : NF + place + 1, :] = state[name : name + 1, here]
    if ref.shape[0] > NF + 4:
        ref[NF + 4 :, :] = jnp.zeros((ref.shape[0] - NF - 4, 2 * W), F32)


def late(next_, factor, moved, from_far, from_near, arrived, own, state, coefficients, ranks, rows):
    def kernel(*refs):
        late_kernel(*refs, ranks=ranks, held_rows=rows)

    inputs = (next_, factor, moved, from_far, from_near, arrived, own, state) + coefficients
    return call(
        kernel,
        "late",
        [(value, True) for value in inputs],
        [(CELLS, True)] * 3 + [(EDGE, True)] * 2 + [(EDGES, True), (STATE, True), ((LINES_B, 2 * W), False)]
        + [((GROUPS, SUB, ROWS * W), True)],
        [
            pltpu.VMEM(CELLS, F32),
            pltpu.VMEM((ROWS, SUB, W), F32),
            pltpu.VMEM((GROUPS, SUB, ROWS * W), F32),
            pltpu.VMEM((SUB, ROWS * W), F32),
        ],
        aliases={0: 0, 1: 1, 2: 2},
    )


def hand_kernel(lam, state, send):
    even = lax.rem(lax.axis_index("geo"), 2) == 0

    @pl.when(even)
    def _():
        fill(send, lam, state, 2)

    @pl.when(jnp.logical_not(even))
    def _():
        fill(send, lam, state, 0)


def hand(lam, state):
    return call(hand_kernel, "hand", [(lam, True), (state, True)], [((LINES_A, 2 * W), False)])[0]


def rim_kernel(
    next_south, next_north, source, state, rate, damp, across, factor_south, factor_north, beyond,
):
    sub = sublane()
    zero = jnp.zeros((SUB, W), F32)
    wind0 = {r: full(state[WIND0 : WIND0 + 1, column(r)]) for r in (-1, 4)}
    steep0 = {r: full(state[STEEP0 : STEEP0 + 1, column(r)]) for r in (-1, 4)}

    def step(group, sums):
        sums = list(sums)
        for tile in range(TILES):
            rows, spot = pl.ds(tile * SUB, SUB), bins(group, tile)
            grow, fade = rate[spot, :], damp[spot, :]
            if tile in SOUTH:
                factor_south[group, rows, :] = jnp.exp2(grow * wind0[-1] - fade * steep0[-1])
            if tile in NORTH:
                factor_north[group, rows, :] = jnp.exp2(grow * wind0[4] - fade * steep0[4])
            gone = fade * across[spot, :]
            if tile in NORTH:
                value = pick(tile, sub, source[group, rows, lanes(0)] * next_south[group, rows, :], None)
                sums[0] = sums[0] + gone * value
            if tile in SOUTH:
                value = pick(tile, sub, None, source[group, rows, lanes(3)] * next_north[group, rows, :])
                sums[1] = sums[1] + gone * value
        return tuple(sums)

    sums = loop(0, GROUPS, 6, step, (zero,) * 2)
    beyond[...] = jnp.zeros_like(beyond)
    for place in range(2):
        beyond[0:1, lanes(place)] = total(sums[place]) * (-LN2)


def rim(*args):
    return call(
        rim_kernel,
        "rim",
        [(arg, True) for arg in args],
        [(EDGE, True), (EDGE, True), ((SUB, 2 * W), True)],
        cost=1 << 24,
    )


def inner_kernel(
    next_, factor, source, state_in, rate, damp, steep, centre, back, across, grown, part, state, inside,
):
    sub = sublane()
    zero = jnp.zeros((SUB, W), F32)
    state[...] = state_in[...]

    def step(group, sums):
        sums = list(sums)
        for tile in range(TILES):
            rows, spot = pl.ds(tile * SUB, SUB), bins(group, tile)
            grow, fade = rate[spot, :], damp[spot, :]
            middle, along, over = centre[spot, :], back[spot, :], across[spot, :]
            cell = {r: source[group, rows, lanes(r)] for r in range(ROWS)}
            for place, r in enumerate((1, 2)):
                value = middle * cell[r] + along * side(tile, sub, cell[r], True)
                value = value + over * pick(tile, sub, cell[r + 1], cell[r - 1])
                inside[group, rows, lanes(place)] = value
                value = value * next_[group, rows, lanes(r)]
                sums[place] = sums[place] + grow * value
                sums[2 + place] = sums[2 + place] + fade * value
        return tuple(sums)

    sums = loop(0, GROUPS, 6, step, (zero,) * 4)
    for place, r in enumerate((1, 2)):
        state[GRAD0 : GRAD0 + 1, column(r)] = total(sums[place]) * LN2
        state[TEND0 : TEND0 + 1, column(r)] = total(sums[2 + place]) * (-LN2)
    tend0 = {r: full(state[TEND0 : TEND0 + 1, column(r)]) for r in (1, 2)}
    sea = {r: full(state[SEA : SEA + 1, column(r)]) for r in (1, 2)}

    def grow_back(group, carry):
        for tile in range(TILES):
            rows, spot = pl.ds(tile * SUB, SUB), bins(group, tile)
            heavy = steep[spot, :]
            middle, along, over = centre[spot, :], back[spot, :], across[spot, :]
            cell = {}
            for place, r in enumerate((1, 2)):
                cell[r] = inside[group, rows, lanes(place)] * factor[group, rows, lanes(r)] + heavy * tend0[r]
                grown[group, rows, lanes(place)] = cell[r]
            met = {1: pick(tile, sub, over * cell[2], None), 2: pick(tile, sub, None, over * cell[1])}
            for place, r in enumerate((1, 2)):
                value = middle * cell[r] + along * side(tile, sub, cell[r], True)
                part[group, rows, lanes(place)] = sea[r] * plus(value, met[r])
        return carry

    loop(0, GROUPS, 6, grow_back, 0)


def inner(*args):
    return call(
        inner_kernel,
        "inner",
        [(arg, True) for arg in args],
        [(EDGES, True), (EDGES, True), (STATE, True)],
        [pltpu.VMEM(EDGES, F32)],
        cost=1 << 22,
    )


def last_kernel(
    next_, factor, factor_south, factor_north, edges, grown, part, beyond, state, back_a, back_b,
    rate, damp, steep, centre, back, across,
    out, grad, rims, low, high, ghosts, lam, cells, winds, sems,
):
    sub = sublane()
    zero = jnp.zeros((SUB, W), F32)
    even = lax.rem(lax.axis_index("geo"), 2) == 0
    first_b, first_a = back_b[0 : NF + 4, :], back_a[0 : NF + 4, :]
    ghosts[0] = jnp.where(even, first_b, first_a)
    ghosts[1] = jnp.where(even, first_a, first_b)
    for group in range(GROUPS):
        for where in range(2):
            for row in range(2):
                one = ghosts[where, 2 * group : 2 * group + 1, lanes(row)]
                two = ghosts[where, 2 * group + 1 : 2 * group + 2, lanes(row)]
                lam[group, :, lanes(2 * where + row)] = jnp.where(sub < 4, one, two)
    sea = {r: full(state[SEA : SEA + 1, column(r)]) for r in range(-2, 6)}
    wind1, steep1, tend1 = {}, {}, {}
    for r in (-2, -1, 4, 5):
        where, here = (0, lanes(r + 2)) if r < 0 else (1, lanes(r - 4))
        wind1[r] = full(state[WIND1 : WIND1 + 1, column(r)])
        value = ghosts[where, NF : NF + 1, here]
        steep1[r] = full(jnp.where(sea[r][0:1, :] > 0.5, value, LAND))
        tend1[r] = full(ghosts[where, NF + 1 : NF + 2, here])

    def first(group, sums):
        sums = list(sums)
        for tile in range(TILES):
            rows, spot = pl.ds(tile * SUB, SUB), bins(group, tile)
            grow, fade, heavy = rate[spot, :], damp[spot, :], steep[spot, :]
            middle, along, over = centre[spot, :], back[spot, :], across[spot, :]

            def ghost(r):
                value = split_lam(lam, group, tile, lanes(r + 2 if r < 0 else r - 2))
                return value * jnp.exp2(grow * wind1[r] - fade * steep1[r]) + heavy * tend1[r]

            for near, far, mine, place, tiles in ((-1, -2, 0, 0, SOUTH), (4, 5, 3, 1, NORTH)):
                if tile not in tiles:
                    continue
                cell = ghost(near)
                value = middle * cell + along * side(tile, sub, cell, True) + over * ghost(far)
                (low if place == 0 else high)[group, rows, :] = value
                value = over * cell
                value = pick(tile, sub, None, value) if place == 0 else pick(tile, sub, value, None)
                rims[group, rows, lanes(place)] = edges[group, rows, lanes(place)] + value
                value = value * next_[group, rows, lanes(mine)]
                sums[place] = sums[place] + grow * value
                sums[2 + place] = sums[2 + place] + fade * value
        return tuple(sums)

    sums = loop(0, GROUPS, 6, first, (zero,) * 4)
    sums = [total(value) * LN2 for value in sums]
    tend0 = {r: state[TEND0 : TEND0 + 1, column(r)] for r in (0, 3)}
    grad0 = [state[GRAD0 : GRAD0 + 1, column(r)] for r in range(ROWS)]
    tend0[0], grad0[0] = tend0[0] - sums[2], grad0[0] + sums[0]
    tend0[3], grad0[3] = tend0[3] - sums[3], grad0[3] + sums[1]
    tend0[-1] = beyond[0:1, lanes(0)] + ghosts[0, NF + 2 : NF + 3, lanes(1)]
    tend0[4] = beyond[0:1, lanes(1)] + ghosts[1, NF + 2 : NF + 3, lanes(0)]
    for r in range(ROWS):
        winds[0:1, lanes(r)] = grad0[r]
        winds[1:2, lanes(r)] = state[GRAD1 : GRAD1 + 1, column(r)]
    sent = pltpu.make_async_copy(winds, grad, sems.at[CHUNKS])
    sent.start()
    tend0 = {r: full(value) for r, value in tend0.items()}

    def second(group, carry):
        for tile in range(TILES):
            rows, spot = pl.ds(tile * SUB, SUB), bins(group, tile)
            heavy = steep[spot, :]
            middle, along, over = centre[spot, :], back[spot, :], across[spot, :]
            cell = {1: grown[group, rows, lanes(0)], 2: grown[group, rows, lanes(1)]}
            for r, mine, ghost, gained in ((-1, SOUTH, low, factor_south), (4, NORTH, high, factor_north)):
                if tile in mine:
                    cell[r] = ghost[group, rows, :] * gained[group, rows, :] + heavy * tend0[r]
            for r, place, mine in ((0, 0, SOUTH), (3, 1, NORTH)):
                value = (rims if tile in mine else edges)[group, rows, lanes(place)]
                cell[r] = value * factor[group, rows, lanes(r)] + heavy * tend0[r]
            for r in (0, 3):
                value = middle * cell[r] + along * side(tile, sub, cell[r], True)
                value = value + over * pick(tile, sub, cell.get(r + 1), cell.get(r - 1))
                cells[group, rows, lanes(r)] = sea[r] * value
            met = {
                1: pick(tile, sub, None, sea[1] * (over * cell[0])),
                2: pick(tile, sub, sea[2] * (over * cell[3]), None),
            }
            for r in (1, 2):
                cells[group, rows, lanes(r)] = plus(part[group, rows, lanes(r - 1)], met[r])
        return carry

    each = GROUPS // CHUNKS
    copies = []
    for c in range(CHUNKS):
        loop(c * each, (c + 1) * each, 3, second, 0)
        here = pl.ds(c * each, each)
        copies.append(pltpu.make_async_copy(cells.at[here], out.at[here], sems.at[c]))
        copies[c].start()
    sent.wait()
    for copy in copies:
        copy.wait()


def last(next_, factor, factor_south, factor_north, edges, grown, part, beyond, state, back_a, back_b, coefficients):
    inputs = (next_, factor, factor_south, factor_north, edges, grown, part, beyond, state)
    inputs = [(value, True) for value in inputs]
    inputs += [(back_a, True), (back_b, True)]
    inputs += [(value, True) for value in coefficients]
    return call(
        last_kernel,
        "last",
        inputs,
        [(CELLS, False), ((2, ROWS * W), False)],
        [
            pltpu.VMEM(EDGES, F32),
            pltpu.VMEM(EDGE, F32),
            pltpu.VMEM(EDGE, F32),
            pltpu.VMEM((2, NF + 4, 2 * W), F32),
            pltpu.VMEM((GROUPS, SUB, ROWS * W), F32),
            pltpu.VMEM(CELLS, F32),
            pltpu.VMEM((2, ROWS * W), F32),
            pltpu.SemaphoreType.DMA((CHUNKS + 1,)),
        ],
        out_away=(0, 1),
    )


def swaps(count):
    near = [(i, i ^ 1) for i in range(count)]
    far = []
    for i in range(1, count - 1, 2):
        far += [(i, i + 1), (i + 1, i)]
    return near, far


def body(
    initial_spectrum,
    wind_forcing,
    sea_mask,
    courant,
    input_rate,
    damping,
    steep_weight,
    obs_owner,
    obs_point,
    obs_value,
    obs_weight,
):
    count = lax.axis_size("geo")
    held = obs_point.shape[0]
    near, far = swaps(count)
    field = initial_spectrum.reshape(CELLS)
    sea = sea_mask.reshape(1, ROWS * W)
    from_far = lax.ppermute(far_rows(field, sea, wind_forcing), "geo", far)
    flow, rate, damp, steep, centre, ahead, back, across, own = local(
        field,
        sea,
        courant,
        input_rate.reshape(1, NB),
        damping.reshape(1, NB),
        steep_weight.reshape(1, NB),
        jnp.asarray(direction_tables()),
    )
    rows = near_rows(field, sea, wind_forcing, own)
    from_near = lax.ppermute(rows, "geo", near)
    next_, factor, moved, state, slots = middle(
        flow, own, wind_forcing, sea, (rate, damp, steep, centre, ahead, across),
        (obs_owner.reshape(1, held), obs_point.reshape(1, held), obs_value.T, obs_weight.reshape(1, held)), rows, count,
    )
    arrived = lax.all_to_all(slots, "geo", split_axis=0, concat_axis=0, tiled=True)
    next_, factor, source, next_south, next_north, edges, state, send_b, lam = late(
        next_, factor, moved, from_far, from_near, arrived, own, state,
        (rate, damp, steep, centre, ahead, back, across), count, held,
    )
    back_b = lax.ppermute(send_b, "geo", far)
    back_a = lax.ppermute(hand(lam, state), "geo", near)
    factor_south, factor_north, beyond = rim(next_south, next_north, source, state, rate, damp, across)
    grown, part, state = inner(next_, factor, source, state, rate, damp, steep, centre, back, across)
    out, grad = last(
        next_, factor, factor_south, factor_north, edges, grown, part, beyond, state, back_a, back_b,
        (rate, damp, steep, centre, back, across),
    )
    return grad, out.reshape(NB, ROWS * W)


def solution(mesh):
    return jax.shard_map(
        body,
        mesh=mesh,
        in_specs=(
            P(None, ("groups", "geo")),
            P(None, ("groups", "geo")),
            P(("groups", "geo")),
            P(),
            P(),
            P(),
            P(),
            P(("groups", "geo"), None),
            P(("groups", "geo")),
            P(("groups", "geo"), None),
            P(("groups", "geo")),
        ),
        out_specs=(P(None, ("groups", "geo")), P(None, ("groups", "geo"))),
        check_vma=False,
    )
```
